32 devices in a mesh: feat: 8 (over z, x), dp: 4 (over y, core).
Axes of the slice: x: 2, y: 2, z: 4, core: 2. Of those that a mesh axis runs over, the one named last changes fastest.
Arguments:
- node_feats: bfloat16 [1024, 131072], P('feat'), may hold values from -6 to 6
- first_layer: bfloat16 [2, 1024, 256], P(None, 'feat'), may hold values from -0.125 to 0.125
- second_layer: bfloat16 [2, 256, 172], replicated, may hold values from -0.375 to 0.375
- seed_ids: int32 [32, 64], P('dp'), may hold values from 0 to 131071
- hop1_ids: int32 [32, 640], P('dp'), may hold values from 0 to 131071
- hop1_count: int32 [32, 64], P('dp'), may hold values from 1 to 10, 352 in all within a row
- hop2_ids: int32 [32, 7040], P('dp'), may hold values from 0 to 131071
- hop2_count: int32 [32, 704], P('dp'), may hold values from 1 to 10, 3872 in all within a row
- batch_sizes: int32 [32], replicated, may hold values from 1 to 64, 1536 in all
- label_ids: int32 [32, 64], P('dp'), may hold values from 0 to 171
Outputs:
- grad_first: float32 [2, 1024, 256], P(None, 'feat')
- grad_second: float32 [2, 256, 172], replicated
The draws below stay inside these ranges and needn't reach their ends.
Inputs may be any that keep to these rules, and one draw needn't show every extreme that they name: The first hop1_count entries of a seed's list are used; the counts of one mini-batch sum to 352. The first hop2_count entries of a row's list are used; the counts of one mini-batch sum to 3872. Seeds at positions batch_sizes[o] and beyond are padding; the sizes sum to 1536.
All inputs are finite; a program needn't handle non-finite values.
Results may differ from the reference program's by a relative error of at most 0.0035.
The reference program's roundings to bfloat16 on the way (of `averaged`, `inputs`, `hidden`, `near_mean`, `dlogits` and `dpreact`) count: a program that leaves them out, or rounds other values in their place, can miss the bound.
Values may be sent and summed in bfloat16 or wider, within the bound.
No kernel may reach another device: no remote copies, remote signals or barrier semaphores. Data moves between devices by JAX's collectives and lax.ppermute only.
A program may use at most 512 MiB of HBM per device.

```python
import math
import jax
import jax.numpy as jnp
import numpy as np
from jax import lax

FEATURES = 1024
HIDDEN_SIZE = 256
CLASSES = 172
SEEDS = 64
FAN1 = 10
FAN2 = 10
NODES = 131072
ROWS = 704
OWNERS = 32


def plant(drawn, stream_key, least, largest):
    dims = drawn.shape
    spot = [jax.random.randint(jax.random.fold_in(stream_key, axis), (), 0, dims[axis]) for axis in range(len(dims))]
    drawn = drawn.at[tuple(spot)].set(least)
    longest = dims.index(max(dims))
    spot[longest] = (spot[longest] + 1) % dims[longest]
    return drawn.at[tuple(spot)].set(largest)


def steps_of(stream_key, dims, split, least, top_value):
    def one(dim, shards_of):
        heights = jax.random.uniform(jax.random.fold_in(jax.random.fold_in(stream_key, 6), dim), (shards_of,), jnp.float32, least / len(split), top_value / len(split))
        return jnp.repeat(jnp.exp(heights), dims[dim] // shards_of).reshape((-1,) + (1,) * (len(dims) - dim - 1))

    level = one(*split[0])
    for cut in split[1:]:
        level = level * one(*cut)
    return level


def split_up(count, total, limit, skew):
    loads = [(1 << 20) // math.isqrt(grade ** skew) + 1 for grade in range(2, count + 1)]
    rest, holding = total - limit - (count - 1), [1] * (count - 1)
    while rest > 0:
        movable = [i for i in range(count - 1) if holding[i] < limit]
        whole, budget = sum([loads[i] for i in movable]), rest
        for i in movable:
            more = min(limit - holding[i], max(1, budget * loads[i] // whole), rest)
            holding[i] = holding[i] + more
            rest = rest - more
    return np.array([limit] + holding)


def uneven_parts(own_key, number_of, total, most, skew):
    if number_of == 2:
        one = jax.random.randint(own_key, (), max(1, total - most), min(most, total - 1) + 1)
        return jnp.stack([one, total - one])
    sizes = jnp.asarray(split_up(number_of, total, most, skew), jnp.int32)
    pairs = (number_of - 1) // 2
    source_of, receiver = sizes[1:1 + 2 * pairs:2], sizes[2:2 + 2 * pairs:2]
    slack = jnp.minimum(source_of - 1, most - receiver)
    moved = jax.random.randint(jax.random.fold_in(own_key, 1), (pairs,), 0, 1 << 20) % (slack + 1)
    sizes = sizes.at[1:1 + 2 * pairs:2].set(source_of - moved).at[2:2 + 2 * pairs:2].set(receiver + moved)
    return sizes[jax.random.permutation(jax.random.fold_in(own_key, 2), number_of)]


def scatter_about(rng, dims, width, limit, split=(), held_as=jnp.bfloat16):
    array = jax.random.normal(rng, dims, jnp.float32) * width
    if len(split) > 0:
        array = steps_of(rng, dims, split, -0.22, 0.18) * array
    return jnp.clip(array, min=-limit, max=limit).astype(held_as)


def setup_inputs(seed: int = 0) -> dict:
    key_list = jax.random.split(jax.random.key(seed), 11)
    node_feats = scatter_about(key_list[0], (FEATURES, NODES), 1.0, 6.0, ((0, 8),))
    first_layer = scatter_about(key_list[1], (2, FEATURES, HIDDEN_SIZE), (2 * FEATURES) ** -0.5, 0.125, ((1, 8),))
    second_layer = scatter_about(key_list[2], (2, HIDDEN_SIZE, CLASSES), HIDDEN_SIZE ** -0.5, 0.375)
    seed_ids = plant(jax.random.randint(key_list[3], (OWNERS, SEEDS), 0, NODES), jax.random.fold_in(key_list[3], 1), 0, NODES - 1).astype(jnp.int32)
    hop1_ids = plant(jax.random.randint(key_list[4], (OWNERS, SEEDS * FAN1), 0, NODES), jax.random.fold_in(key_list[4], 1), 0, NODES - 1).astype(jnp.int32)
    hop1_count = jax.vmap(lambda own: uneven_parts(own, SEEDS, SEEDS * (FAN1 + 1) // 2, FAN1, 1))(jax.random.split(key_list[5], OWNERS)).reshape((OWNERS, SEEDS)).astype(jnp.int32)
    hop2_ids = plant(jax.random.randint(key_list[6], (OWNERS, ROWS * FAN2), 0, NODES), jax.random.fold_in(key_list[6], 1), 0, NODES - 1).astype(jnp.int32)
    hop2_count = jax.vmap(lambda own: uneven_parts(own, ROWS, ROWS * (FAN2 + 1) // 2, FAN2, 1))(jax.random.split(key_list[7], OWNERS)).reshape((OWNERS, ROWS)).astype(jnp.int32)
    batch_sizes = uneven_parts(key_list[8], OWNERS, OWNERS * SEEDS * 3 // 4, SEEDS, 2).astype(jnp.int32)
    label_ids = plant(jax.random.randint(key_list[9], (OWNERS, SEEDS), 0, CLASSES), jax.random.fold_in(key_list[9], 1), 0, CLASSES - 1).astype(jnp.int32)
    return dict(node_feats=node_feats, first_layer=first_layer, second_layer=second_layer, seed_ids=seed_ids, hop1_ids=hop1_ids, hop1_count=hop1_count, hop2_ids=hop2_ids, hop2_count=hop2_count, batch_sizes=batch_sizes, label_ids=label_ids)


def upper_layers(preact, second_layer, hop1_count, label_ids, batch_size):
    seed_total = hop1_count.shape[0]
    hidden_width = preact.shape[1]
    fanout = (preact.shape[0] - seed_total) // seed_total
    hidden = jnp.maximum(preact, 0.0).astype(jnp.bfloat16)
    seed_hidden = hidden[:seed_total]
    neighbour_hidden = hidden[seed_total:].reshape(seed_total, fanout, hidden_width).astype(jnp.float32)
    keep_one = jnp.arange(fanout)[None, :] < hop1_count[:, None]
    counts = hop1_count.astype(jnp.float32)[:, None]
    near_mean = (jnp.sum(jnp.where(keep_one[:, :, None], neighbour_hidden, 0.0), axis=1) / counts).astype(jnp.bfloat16)
    logits = jnp.dot(seed_hidden, second_layer[0], preferred_element_type=jnp.float32)
    logits = logits + jnp.dot(near_mean, second_layer[1], preferred_element_type=jnp.float32)
    shifted = logits - jnp.max(logits, axis=1, keepdims=True)
    exponent = jnp.exp(shifted)
    probabilities = exponent / jnp.sum(exponent, axis=1, keepdims=True)
    onehot = (label_ids[:, None] == jnp.arange(logits.shape[1])[None, :]).astype(jnp.float32)
    valid_rows = (jnp.arange(seed_total) < batch_size).astype(jnp.float32)
    dlogits = ((probabilities - onehot) * valid_rows[:, None] / batch_size.astype(jnp.float32)).astype(jnp.bfloat16)
    grad_second = jnp.stack([jnp.dot(seed_hidden.T, dlogits, preferred_element_type=jnp.float32),
                             jnp.dot(near_mean.T, dlogits, preferred_element_type=jnp.float32)])
    back_seed = jnp.dot(dlogits, second_layer[0].T, preferred_element_type=jnp.float32)
    back_near = jnp.dot(dlogits, second_layer[1].T, preferred_element_type=jnp.float32)
    spread = jnp.where(keep_one[:, :, None], (back_near / counts)[:, None, :], 0.0)
    back_hidden = jnp.concatenate([back_seed, spread.reshape(-1, hidden_width)], axis=0)
    dpreact = jnp.where(preact > 0, back_hidden, 0.0).astype(jnp.bfloat16)
    return dpreact, grad_second


def owner_terms(node_feats, first_layer, second_layer, seed_row, hop1_row, count1_row, hop2_row, count2_row, label_row, batch_size):
    node_list = jnp.concatenate([seed_row, hop1_row])
    row_total = count2_row.shape[0]
    own_rows = node_feats[:, node_list].T
    neighbours = node_feats[:, hop2_row.reshape(row_total, -1)].astype(jnp.float32)
    keep_two = jnp.arange(neighbours.shape[2])[None, :] < count2_row[:, None]
    summed = jnp.sum(jnp.where(keep_two[None, :, :], neighbours, 0.0), axis=2).T
    averaged = (summed / count2_row[:, None].astype(jnp.float32)).astype(jnp.bfloat16)
    inputs = jnp.concatenate([own_rows, averaged], axis=1)
    weights = first_layer.reshape(2 * FEATURES, HIDDEN_SIZE)
    preact = jnp.dot(inputs, weights, preferred_element_type=jnp.float32)
    dpreact, grad_second = upper_layers(preact, second_layer, count1_row, label_row, batch_size)
    grad_first = jnp.dot(inputs.T, dpreact, preferred_element_type=jnp.float32).reshape(2, FEATURES, HIDDEN_SIZE)
    return grad_first, grad_second


def reference(node_feats, first_layer, second_layer, seed_ids, hop1_ids, hop1_count, hop2_ids, hop2_count, batch_sizes, label_ids):
    def accumulate(totals, owner_data):
        seed_row, hop1_row, count1_row, hop2_row, count2_row, label_row, batch_size = owner_data
        first_term, second_term = owner_terms(node_feats, first_layer, second_layer, seed_row, hop1_row, count1_row,
                                              hop2_row, count2_row, label_row, batch_size)
        return (totals[0] + first_term, totals[1] + second_term), None

    initial = (jnp.zeros((2, FEATURES, HIDDEN_SIZE), jnp.float32), jnp.zeros((2, HIDDEN_SIZE, CLASSES), jnp.float32))
    totals, unused = lax.scan(accumulate, initial,
                              (seed_ids, hop1_ids, hop1_count, hop2_ids, hop2_count, label_ids, batch_sizes))
    return totals[0], totals[1]
```

```python
import functools

import jax
import jax.numpy as jnp
from jax import lax
from jax.experimental import pallas as pl
from jax.experimental.pallas import tpu as pltpu
from jax.sharding import PartitionSpec as P

LANES = 128
TILE = 16
CODE_BITS = 5
CODES = 1 << CODE_BITS
UNROLL = 4
BLOCK = 256


def round_up(value, step):
    return (value + step - 1) // step * step


def plan_rows(hop1_count, hop2_count, sizes, kept):
    groups, seed_total = hop1_count.shape
    row_total = hop2_count.shape[1]
    fanout = (row_total - seed_total) // seed_total
    live = jnp.arange(seed_total)[None, :] < sizes[:, None]
    near = jnp.arange(fanout)[None, None, :] < jnp.where(live, hop1_count, 0)[:, :, None]
    used = jnp.concatenate([live, near.reshape(groups, -1)], axis=1)
    count = jnp.where(used, hop2_count, 0)
    row = jnp.arange(row_total)[None, :]
    mixed = count * row_total + (row_total - 1 - row)
    place = jnp.sum((mixed[:, None, :] > mixed[:, :, None]).astype(jnp.int32), axis=2)
    packed = row * 16 + count
    order = jnp.sum(
        jnp.where(place[:, None, :] == jnp.arange(kept)[None, :, None], packed[:, None, :], 0), axis=2
    )
    enough = jnp.sum(
        (count[:, None, :] >= jnp.arange(16)[None, :, None]).astype(jnp.int32), axis=2
    )
    return order, enough


def slot_codes(ids, live):
    return (ids // TILE) * CODES + jnp.where(live, ids % TILE, TILE)


def gather_kernel(
    loads, fanout, capacity, enough_ref, order_ref, own_ref, near_ref, count_ref, feats_ref, weights_ref,
    inputs_ref, preact_ref, table_ref, mask_ref, own_sum_ref, near_sum_ref,
):
    step = pl.program_id(0)
    width, chunk = feats_ref.shape
    padded = table_ref.shape[1]

    @pl.when(step == 0)
    def _():
        shape = mask_ref.shape
        code = lax.broadcasted_iota(jnp.int32, shape, 0)
        line = lax.broadcasted_iota(jnp.int32, shape, 1)
        mask_ref[...] = jnp.where(code == line, 1.0, 0.0).astype(jnp.bfloat16)
        own_sum_ref[...] = jnp.zeros_like(own_sum_ref)
        near_sum_ref[...] = jnp.zeros_like(near_sum_ref)

    @pl.when(step < loads)
    def _():
        down = lax.broadcasted_iota(jnp.int32, (BLOCK, BLOCK), 0)
        across = lax.broadcasted_iota(jnp.int32, (BLOCK, BLOCK), 1)
        identity = jnp.where(down == across, 1.0, 0.0).astype(jnp.bfloat16)
        for part in range(chunk // BLOCK):
            piece = feats_ref[:, part * BLOCK : (part + 1) * BLOCK]
            if padded > width:
                piece = jnp.concatenate([piece, jnp.zeros((padded - width, BLOCK), piece.dtype)], axis=0)
            turned = lax.dot_general(
                identity, piece, (((1,), (1,)), ((), ())), preferred_element_type=jnp.float32
            )
            start = pl.multiple_of(step * chunk + part * BLOCK, BLOCK)
            table_ref[pl.ds(start, BLOCK), :] = turned.astype(jnp.bfloat16)

    @pl.when(step >= loads)
    def _():
        tiles = table_ref.reshape(table_ref.shape[0] // TILE, TILE, padded)

        def fetch(code):
            return (tiles[code >> CODE_BITS] * mask_ref[code & (CODES - 1)]).astype(jnp.float32)

        def fold(value):
            return value[: TILE // 2] + value[TILE // 2 :]

        def gather_rows(slots, number, carry):
            first = number * UNROLL
            rows = [order_ref[0, 0, first + i] >> 4 for i in range(UNROLL)]
            for i, row in enumerate(rows):
                start = pl.multiple_of((first + i) * 8, 8)
                own_sum_ref[pl.ds(start, 8), :] = fold(fetch(own_ref[0, 0, row]))
                total = fetch(near_ref[0, 0, row * fanout])
                for slot in range(1, slots):
                    total = total + fetch(near_ref[0, 0, row * fanout + slot])
                near_sum_ref[pl.ds(start, 8), :] = fold(total)
            return carry

        begin = 0
        for slots in range(fanout, 0, -1):
            end = lax.div(enough_ref[0, 0, slots] + UNROLL - 1, UNROLL)
            lax.fori_loop(begin, end, functools.partial(gather_rows, slots), 0)
            begin = end

        def collect(ref):
            total = ref[pl.ds(0, capacity, stride=8), :]
            for line in range(1, 8):
                total = total + ref[pl.ds(line, capacity, stride=8), :]
            return total

        counts = jnp.transpose(jnp.broadcast_to(count_ref[0], (padded, count_ref.shape[2])))[:capacity]
        own = collect(own_sum_ref).astype(jnp.bfloat16)[:, :width]
        near = (collect(near_sum_ref) / counts).astype(jnp.bfloat16)[:, :width]
        inputs_ref[0] = jnp.concatenate([own, near], axis=1)
        preact_ref[0] = jnp.dot(own, weights_ref[0], preferred_element_type=jnp.float32) + jnp.dot(
            near, weights_ref[1], preferred_element_type=jnp.float32
        )


def gather_layer(node_feats, first_layer, enough, order, own_codes, near_codes, capacity):
    width, nodes = node_feats.shape
    groups, kept = order.shape
    hidden_width = first_layer.shape[2]
    row_total = own_codes.shape[1]
    fanout = near_codes.shape[1] // row_total
    padded = max(width, LANES)
    chunk = min(nodes, 8192)
    loads = nodes // chunk
    counts = jnp.maximum(order % 16, 1).astype(jnp.float32)

    def per_group(length):
        return pl.BlockSpec(
            (1, 1, length), lambda step: (jnp.maximum(step - loads, 0), 0, 0), memory_space=pltpu.SMEM
        )

    return pl.pallas_call(
        functools.partial(gather_kernel, loads, fanout, capacity),
        grid=(loads + groups,),
        in_specs=[
            per_group(16),
            per_group(kept),
            per_group(row_total),
            per_group(row_total * fanout),
            pl.BlockSpec((1, 1, kept), lambda step: (jnp.maximum(step - loads, 0), 0, 0)),
            pl.BlockSpec((width, chunk), lambda step: (0, jnp.minimum(step, loads - 1))),
            pl.BlockSpec((2, width, hidden_width), lambda step: (0, 0, 0)),
        ],
        out_specs=[
            pl.BlockSpec((1, capacity, 2 * width), lambda step: (jnp.maximum(step - loads, 0), 0, 0)),
            pl.BlockSpec((1, capacity, hidden_width), lambda step: (jnp.maximum(step - loads, 0), 0, 0)),
        ],
        out_shape=[
            jax.ShapeDtypeStruct((groups, capacity, 2 * width), jnp.bfloat16),
            jax.ShapeDtypeStruct((groups, capacity, hidden_width), jnp.float32),
        ],
        scratch_shapes=[
            pltpu.VMEM((nodes, padded), jnp.bfloat16),
            pltpu.VMEM((CODES, TILE, padded), jnp.bfloat16),
            pltpu.VMEM((capacity * 8, padded), jnp.float32),
            pltpu.VMEM((capacity * 8, padded), jnp.float32),
        ],
        compiler_params=pltpu.CompilerParams(vmem_limit_bytes=52 * 2**20),
        name="gather_layer",
    )(
        enough[:, None, :], order[:, None, :], own_codes[:, None, :], near_codes[:, None, :],
        counts[:, None, :], node_feats, first_layer,
    )


def upper_kernel(fanout, size_ref, preact_ref, layer_ref, row_ref, count_ref, label_ref, out_ref):
    seed_total = count_ref.shape[0]
    capacity, hidden_width = preact_ref.shape
    classes = layer_ref.shape[2]
    size = size_ref[0]
    seed = lax.broadcasted_iota(jnp.int32, (seed_total, capacity), 0)
    row = jnp.broadcast_to(row_ref[...], (seed_total, capacity))
    first = seed_total + seed * fanout
    is_seed = jnp.where(row == seed, 1.0, 0.0).astype(jnp.bfloat16)
    is_near = jnp.where((row >= first) & (row < first + fanout), 1.0, 0.0).astype(jnp.bfloat16)
    preact = preact_ref[...]
    hidden = jnp.maximum(preact, 0.0).astype(jnp.bfloat16)
    counts = count_ref[...]
    seed_hidden = jnp.dot(is_seed, hidden, preferred_element_type=jnp.float32).astype(jnp.bfloat16)
    near_mean = (jnp.dot(is_near, hidden, preferred_element_type=jnp.float32) / counts).astype(jnp.bfloat16)
    logits = jnp.dot(seed_hidden, layer_ref[0], preferred_element_type=jnp.float32) + jnp.dot(
        near_mean, layer_ref[1], preferred_element_type=jnp.float32
    )
    exponent = jnp.exp(logits - jnp.max(logits, axis=1, keepdims=True))
    probabilities = exponent / jnp.sum(exponent, axis=1, keepdims=True)
    label = jnp.broadcast_to(label_ref[...], (seed_total, classes))
    onehot = jnp.where(label == lax.broadcasted_iota(jnp.int32, (seed_total, classes), 1), 1.0, 0.0)
    valid = lax.broadcasted_iota(jnp.int32, (seed_total, classes), 0) < size
    dlogits = jnp.where(valid, (probabilities - onehot) / size.astype(jnp.float32), 0.0).astype(jnp.bfloat16)
    last = (((1,), (1,)), ((), ()))
    back_seed = lax.dot_general(dlogits, layer_ref[0], last, preferred_element_type=jnp.float32)
    back_near = lax.dot_general(dlogits, layer_ref[1], last, preferred_element_type=jnp.float32) / counts
    rows = (((0,), (0,)), ((), ()))
    spread = lax.dot_general(is_seed, back_seed.astype(jnp.bfloat16), rows, preferred_element_type=jnp.float32)
    spread = spread + lax.dot_general(
        is_near, back_near.astype(jnp.bfloat16), rows, preferred_element_type=jnp.float32
    )
    out_ref[:capacity] = jnp.where(preact > 0, spread, 0.0).astype(jnp.bfloat16)
    out_ref[capacity : capacity + seed_total] = seed_hidden
    out_ref[capacity + seed_total : capacity + 2 * seed_total] = near_mean
    out_ref[capacity + 2 * seed_total :] = jnp.zeros((seed_total, hidden_width), jnp.bfloat16)
    out_ref[capacity + 2 * seed_total :, :classes] = dlogits


def upper_layers(preact, second_layer, order, hop1_count, label_ids, size, fanout):
    seed_total = hop1_count.shape[0]
    capacity, hidden_width = preact.shape
    row = jnp.where(order % 16 > 0, order // 16, -1)[None, :]
    vmem = pl.BlockSpec(memory_space=pltpu.VMEM)
    return pl.pallas_call(
        functools.partial(upper_kernel, fanout),
        in_specs=[pl.BlockSpec(memory_space=pltpu.SMEM)] + [vmem] * 5,
        out_specs=vmem,
        out_shape=jax.ShapeDtypeStruct((capacity + 3 * seed_total, hidden_width), jnp.bfloat16),
        compiler_params=pltpu.CompilerParams(vmem_limit_bytes=24 * 2**20),
        name="upper_layers",
    )(
        size[None], preact, second_layer, row, hop1_count.astype(jnp.float32)[:, None], label_ids[:, None]
    )


def shards(
    node_feats,
    first_layer,
    second_layer,
    seed_ids,
    hop1_ids,
    hop1_count,
    hop2_ids,
    hop2_count,
    batch_sizes,
    label_ids,
):
    groups, seed_total = seed_ids.shape
    row_total = hop2_count.shape[1]
    fanout = hop1_ids.shape[1] // seed_total
    slots = hop2_ids.shape[1] // row_total
    slice_width = node_feats.shape[0]
    hidden_width = first_layer.shape[2]
    classes = second_layer.shape[2]
    capacity = round_up(seed_total + row_total // 2, 16)
    kept = round_up(capacity, LANES)
    column_rank = lax.axis_index("feat")
    group_start = lax.axis_index("dp") * groups
    sizes = lax.dynamic_slice_in_dim(batch_sizes, group_start, groups)
    order, enough = plan_rows(hop1_count, hop2_count, sizes, kept)
    own_codes = slot_codes(jnp.concatenate([seed_ids, hop1_ids], axis=1), True)
    near_codes = slot_codes(
        hop2_ids.reshape(groups, row_total, slots),
        jnp.arange(slots)[None, None, :] < hop2_count[:, :, None],
    ).reshape(groups, row_total * slots)
    inputs, partial = gather_layer(
        node_feats, first_layer, enough, order, own_codes, near_codes, capacity
    )
    preact = lax.psum_scatter(partial, "feat", scatter_dimension=0, tiled=True)[0]

    def own(array):
        return lax.dynamic_index_in_dim(array, column_rank, 0, keepdims=False)

    sent = upper_layers(
        preact, second_layer, own(order)[:capacity], own(hop1_count), own(label_ids), own(sizes), fanout
    )
    every = lax.all_gather(sent[None], "feat", axis=0, tiled=True)
    grad_first = jnp.einsum(
        "brf,brh->fh", inputs, every[:, :capacity], preferred_element_type=jnp.float32
    )
    units = every[:, capacity : capacity + 2 * seed_total].reshape(groups, 2, seed_total, hidden_width)
    dlogits = every[:, capacity + 2 * seed_total :, :classes]
    grad_second = jnp.einsum("blsh,bsc->lhc", units, dlogits, preferred_element_type=jnp.float32)
    grad_first = lax.psum(grad_first.reshape(2, slice_width, hidden_width), "dp")
    grad_second = lax.psum(grad_second, "dp")
    return (grad_first, grad_second)


def solution(mesh):
    return jax.shard_map(
        shards,
        mesh=mesh,
        in_specs=(
            P("feat", None),
            P(None, "feat", None),
            P(),
            P("dp", None),
            P("dp", None),
            P("dp", None),
            P("dp", None),
            P("dp", None),
            P(),
            P("dp", None),
        ),
        out_specs=(P(None, "feat", None), P()),
        check_vma=False,
    )
```

```python
import functools

import jax
import jax.numpy as jnp
from jax import lax
from jax.experimental import pallas as pl
from jax.experimental.pallas import tpu as pltpu
from jax.sharding import PartitionSpec as P

LANES = 128
TILE = 16
CODE_BITS = 5
CODES = 1 << CODE_BITS
UNROLL = 4
BLOCK = 256


def round_up(value, step):
    return (value + step - 1) // step * step


def plan_rows(hop1_count, hop2_count, sizes, kept):
    groups, seed_total = hop1_count.shape
    row_total = hop2_count.shape[1]
    fanout = (row_total - seed_total) // seed_total
    live = jnp.arange(seed_total)[None, :] < sizes[:, None]
    near = jnp.arange(fanout)[None, None, :] < jnp.where(live, hop1_count, 0)[:, :, None]
    used = jnp.concatenate([live, near.reshape(groups, -1)], axis=1)
    count = jnp.where(used, hop2_count, 0)
    row = jnp.arange(row_total)[None, :]
    mixed = count * row_total + (row_total - 1 - row)
    place = jnp.sum((mixed[:, None, :] > mixed[:, :, None]).astype(jnp.int32), axis=2)
    packed = row * 16 + count
    order = jnp.sum(
        jnp.where(place[:, None, :] == jnp.arange(kept)[None, :, None], packed[:, None, :], 0), axis=2
    )
    enough = jnp.sum(
        (count[:, None, :] >= jnp.arange(16)[None, :, None]).astype(jnp.int32), axis=2
    )
    return order, enough


def slot_codes(ids, live):
    return (ids // TILE) * CODES + jnp.where(live, ids % TILE, TILE)


def gather_kernel(
    loads, fanout, capacity, turn_ref, enough_ref, order_ref, own_ref, near_ref, count_ref, feats_ref, *rest
):
    *inputs_refs, table_ref, mask_ref, own_sum_ref, near_sum_ref = rest
    step = pl.program_id(0)
    width, chunk = feats_ref.shape
    padded = table_ref.shape[1]

    @pl.when(step == 0)
    def _():
        shape = mask_ref.shape
        code = lax.broadcasted_iota(jnp.int32, shape, 0)
        line = lax.broadcasted_iota(jnp.int32, shape, 1)
        mask_ref[...] = jnp.where(code == line, 1.0, 0.0).astype(jnp.bfloat16)
        own_sum_ref[...] = jnp.zeros_like(own_sum_ref)
        near_sum_ref[...] = jnp.zeros_like(near_sum_ref)

    @pl.when(step < loads)
    def _():
        down = lax.broadcasted_iota(jnp.int32, (BLOCK, BLOCK), 0)
        across = lax.broadcasted_iota(jnp.int32, (BLOCK, BLOCK), 1)
        identity = jnp.where(down == across, 1.0, 0.0).astype(jnp.bfloat16)
        for part in range(chunk // BLOCK):
            piece = feats_ref[:, part * BLOCK : (part + 1) * BLOCK]
            if padded > width:
                piece = jnp.concatenate([piece, jnp.zeros((padded - width, BLOCK), piece.dtype)], axis=0)
            turned = lax.dot_general(
                identity, piece, (((1,), (1,)), ((), ())), preferred_element_type=jnp.float32
            )
            start = pl.multiple_of(step * chunk + part * BLOCK, BLOCK)
            table_ref[pl.ds(start, BLOCK), :] = turned.astype(jnp.bfloat16)

    @pl.when(step >= loads)
    def _():
        tiles = table_ref.reshape(table_ref.shape[0] // TILE, TILE, padded)

        def fetch(code):
            return (tiles[code >> CODE_BITS] * mask_ref[code & (CODES - 1)]).astype(jnp.float32)

        def fold(value):
            return value[: TILE // 2] + value[TILE // 2 :]

        def gather_rows(slots, number, carry):
            first = number * UNROLL
            rows = [order_ref[0, 0, first + i] >> 4 for i in range(UNROLL)]
            for i, row in enumerate(rows):
                start = pl.multiple_of((first + i) * 8, 8)
                own_sum_ref[pl.ds(start, 8), :] = fold(fetch(own_ref[0, 0, row]))
                total = fetch(near_ref[0, 0, row * fanout])
                for slot in range(1, slots):
                    total = total + fetch(near_ref[0, 0, row * fanout + slot])
                near_sum_ref[pl.ds(start, 8), :] = fold(total)
            return carry

        begin = 0
        for slots in range(fanout, 0, -1):
            end = lax.div(enough_ref[0, 0, slots] + UNROLL - 1, UNROLL)
            lax.fori_loop(begin, end, functools.partial(gather_rows, slots), 0)
            begin = end

        def collect(ref):
            total = ref[pl.ds(0, capacity, stride=8), :]
            for line in range(1, 8):
                total = total + ref[pl.ds(line, capacity, stride=8), :]
            return total

        counts = jnp.transpose(jnp.broadcast_to(count_ref[0], (padded, count_ref.shape[2])))[:capacity]
        own = collect(own_sum_ref).astype(jnp.bfloat16)[:, :width]
        near = (collect(near_sum_ref) / counts).astype(jnp.bfloat16)[:, :width]
        both = jnp.concatenate([own, near], axis=1)
        for place, inputs_ref in enumerate(inputs_refs):

            @pl.when(step == loads + place)
            def _():
                inputs_ref[...] = both


def gather_layer(node_feats, turn, enough, order, own_codes, near_codes, capacity):
    width, nodes = node_feats.shape
    groups, kept = order.shape
    row_total = own_codes.shape[1]
    fanout = near_codes.shape[1] // row_total
    padded = max(width, LANES)
    chunk = min(nodes, 8192)
    loads = nodes // chunk
    counts = jnp.maximum(order % 16, 1).astype(jnp.float32)

    def group_of(step, turn_ref):
        return (turn_ref[jnp.maximum(step - loads, 0)], 0, 0)

    def per_group(length):
        return pl.BlockSpec((1, 1, length), group_of, memory_space=pltpu.SMEM)

    return pl.pallas_call(
        functools.partial(gather_kernel, loads, fanout, capacity),
        grid_spec=pltpu.PrefetchScalarGridSpec(
            num_scalar_prefetch=1,
            grid=(loads + groups,),
            in_specs=[
                per_group(16),
                per_group(kept),
                per_group(row_total),
                per_group(row_total * fanout),
                pl.BlockSpec((1, 1, kept), group_of),
                pl.BlockSpec((width, chunk), lambda step, turn_ref: (0, jnp.minimum(step, loads - 1))),
            ],
            out_specs=[pl.BlockSpec((capacity, 2 * width), lambda step, turn_ref: (0, 0))] * groups,
            scratch_shapes=[
                pltpu.VMEM((nodes, padded), jnp.bfloat16),
                pltpu.VMEM((CODES, TILE, padded), jnp.bfloat16),
                pltpu.VMEM((capacity * 8, padded), jnp.float32),
                pltpu.VMEM((capacity * 8, padded), jnp.float32),
            ],
        ),
        out_shape=[jax.ShapeDtypeStruct((capacity, 2 * width), jnp.bfloat16)] * groups,
        compiler_params=pltpu.CompilerParams(vmem_limit_bytes=52 * 2**20),
        name="gather_layer",
    )(
        turn, enough[:, None, :], order[:, None, :], own_codes[:, None, :], near_codes[:, None, :],
        counts[:, None, :], node_feats,
    )


def upper_kernel(fanout, own_ref, weights_ref, layer_ref, row_ref, count_ref, label_ref, *rest):
    *inputs_refs, out_ref = rest
    seed_total = count_ref.shape[0]
    capacity = inputs_refs[0].shape[0]
    hidden_width = weights_ref.shape[2]
    classes = layer_ref.shape[2]
    size = own_ref[0]
    seed = lax.broadcasted_iota(jnp.int32, (seed_total, capacity), 0)
    row = jnp.broadcast_to(row_ref[...], (seed_total, capacity))
    first = seed_total + seed * fanout
    is_seed = jnp.where(row == seed, 1.0, 0.0).astype(jnp.bfloat16)
    is_near = jnp.where((row >= first) & (row < first + fanout), 1.0, 0.0).astype(jnp.bfloat16)
    preact = jnp.dot(inputs_refs[0][...], weights_ref[own_ref[1]], preferred_element_type=jnp.float32)
    for place in range(1, len(inputs_refs)):
        preact = preact + jnp.dot(
            inputs_refs[place][...], weights_ref[own_ref[1 + place]], preferred_element_type=jnp.float32
        )
    hidden = jnp.maximum(preact, 0.0).astype(jnp.bfloat16)
    counts = count_ref[...]
    seed_hidden = jnp.dot(is_seed, hidden, preferred_element_type=jnp.float32).astype(jnp.bfloat16)
    near_mean = (jnp.dot(is_near, hidden, preferred_element_type=jnp.float32) / counts).astype(jnp.bfloat16)
    logits = jnp.dot(seed_hidden, layer_ref[0], preferred_element_type=jnp.float32) + jnp.dot(
        near_mean, layer_ref[1], preferred_element_type=jnp.float32
    )
    exponent = jnp.exp(logits - jnp.max(logits, axis=1, keepdims=True))
    probabilities = exponent / jnp.sum(exponent, axis=1, keepdims=True)
    label = jnp.broadcast_to(label_ref[...], (seed_total, classes))
    onehot = jnp.where(label == lax.broadcasted_iota(jnp.int32, (seed_total, classes), 1), 1.0, 0.0)
    valid = lax.broadcasted_iota(jnp.int32, (seed_total, classes), 0) < size
    dlogits = jnp.where(valid, (probabilities - onehot) / size.astype(jnp.float32), 0.0).astype(jnp.bfloat16)
    last = (((1,), (1,)), ((), ()))
    back_seed = lax.dot_general(dlogits, layer_ref[0], last, preferred_element_type=jnp.float32)
    back_near = lax.dot_general(dlogits, layer_ref[1], last, preferred_element_type=jnp.float32) / counts
    rows = (((0,), (0,)), ((), ()))
    spread = lax.dot_general(is_seed, back_seed.astype(jnp.bfloat16), rows, preferred_element_type=jnp.float32)
    spread = spread + lax.dot_general(
        is_near, back_near.astype(jnp.bfloat16), rows, preferred_element_type=jnp.float32
    )
    out_ref[:capacity] = jnp.where(preact > 0, spread, 0.0).astype(jnp.bfloat16)
    out_ref[capacity : capacity + seed_total] = seed_hidden
    out_ref[capacity + seed_total : capacity + 2 * seed_total] = near_mean
    out_ref[capacity + 2 * seed_total :] = jnp.zeros((seed_total, hidden_width), jnp.bfloat16)
    out_ref[capacity + 2 * seed_total :, :classes] = dlogits


def upper_layers(inputs, sources, weights, second_layer, order, hop1_count, label_ids, size, fanout):
    seed_total = hop1_count.shape[0]
    capacity = inputs[0].shape[0]
    hidden_width = weights.shape[2]
    row = jnp.where(order % 16 > 0, order // 16, -1)[None, :]
    vmem = pl.BlockSpec(memory_space=pltpu.VMEM)
    return pl.pallas_call(
        functools.partial(upper_kernel, fanout),
        in_specs=[pl.BlockSpec(memory_space=pltpu.SMEM)] + [vmem] * (5 + len(inputs)),
        out_specs=vmem,
        out_shape=jax.ShapeDtypeStruct((capacity + 3 * seed_total, hidden_width), jnp.bfloat16),
        compiler_params=pltpu.CompilerParams(vmem_limit_bytes=32 * 2**20),
        name="upper_layers",
    )(
        jnp.concatenate([size[None], sources]), weights, second_layer, row,
        hop1_count.astype(jnp.float32)[:, None], label_ids[:, None], *inputs,
    )


def grad_kernel(seed_total, classes, source_ref, *rest):
    count = (len(rest) - 2) // 2
    inputs_refs, sent_refs = rest[:count], rest[count : 2 * count]
    out_ref, units_ref = rest[2 * count :]
    capacity, double = inputs_refs[0].shape
    hidden_width = out_ref.shape[1]
    rows = (((0,), (0,)), ((), ()))
    first = jnp.zeros((double, hidden_width), jnp.float32)
    for place in range(count):
        first = first + lax.dot_general(
            inputs_refs[place][...], sent_refs[place][:capacity], rows, preferred_element_type=jnp.float32
        )
        start = pl.multiple_of(source_ref[place] * seed_total, seed_total)
        for part in range(3):
            units_ref[part, pl.ds(start, seed_total), :] = sent_refs[place][
                capacity + part * seed_total : capacity + (part + 1) * seed_total
            ]
    out_ref[:double] = first
    for layer in range(2):
        second = lax.dot_general(units_ref[2], units_ref[layer], rows, preferred_element_type=jnp.float32)
        start = double + layer * round_up(classes, 8)
        out_ref[start : start + round_up(classes, 8)] = second[: round_up(classes, 8)]


def grad_layer(inputs, sent, sources, seed_total, classes):
    capacity, double = inputs[0].shape
    hidden_width = sent[0].shape[1]
    vmem = pl.BlockSpec(memory_space=pltpu.VMEM)
    return pl.pallas_call(
        functools.partial(grad_kernel, seed_total, classes),
        in_specs=[pl.BlockSpec(memory_space=pltpu.SMEM)] + [vmem] * (2 * len(inputs)),
        out_specs=vmem,
        out_shape=jax.ShapeDtypeStruct((double + 2 * round_up(classes, 8), hidden_width), jnp.float32),
        scratch_shapes=[pltpu.VMEM((3, len(inputs) * seed_total, hidden_width), jnp.bfloat16)],
        compiler_params=pltpu.CompilerParams(vmem_limit_bytes=40 * 2**20),
        name="grad_layer",
    )(sources, *inputs, *sent)


def final_kernel(mine_ref, other_ref, first_ref, second_ref):
    width = first_ref.shape[1]
    classes = second_ref.shape[2]
    total = mine_ref[...].astype(jnp.float32) + other_ref[...].astype(jnp.float32)
    for layer in range(2):
        first_ref[layer] = total[layer * width : (layer + 1) * width]
        start = 2 * width + layer * round_up(classes, 8)
        second_ref[layer] = jnp.transpose(total[start : start + round_up(classes, 8)])[:, :classes]


def final_sum(mine, other, width, classes):
    hidden_width = mine.shape[1]
    return pl.pallas_call(
        final_kernel,
        out_shape=[
            jax.ShapeDtypeStruct((2, width, hidden_width), jnp.float32),
            jax.ShapeDtypeStruct((2, hidden_width, classes), jnp.float32),
        ],
        name="final_sum",
    )(mine, other)


def ring_of(count):
    if count % 2:
        return list(range(count))
    return list(range(0, count, 2)) + list(range(count - 1, 0, -2))


def send_along(array, ring, shift):
    count = len(ring)
    return lax.ppermute(array, "feat", [(ring[i], ring[(i + shift) % count]) for i in range(count)])


def ring_gather(array, ring):
    count = len(ring)
    result = [array] + [None] * (count - 1)
    ahead = behind = array
    for hop in range(1, count // 2 + 1):
        behind = send_along(behind, ring, 1)
        result[count - hop] = behind
        if 2 * hop < count:
            ahead = send_along(ahead, ring, -1)
            result[hop] = ahead
    return result


def group_sum(grads, width, classes):
    count = lax.axis_size("dp")
    mine = grads
    stride = 1
    while 2 * stride < count:
        mine = mine + lax.ppermute(mine, "dp", [(i, i ^ stride) for i in range(count)])
        stride *= 2
    mine = mine.astype(jnp.bfloat16)
    if count > 1:
        other = lax.ppermute(mine, "dp", [(i, i ^ stride) for i in range(count)])
    else:
        other = jnp.zeros_like(mine)
    return final_sum(mine, other, width, classes)


def shards(
    node_feats,
    first_layer,
    second_layer,
    seed_ids,
    hop1_ids,
    hop1_count,
    hop2_ids,
    hop2_count,
    batch_sizes,
    label_ids,
):
    groups, seed_total = seed_ids.shape
    row_total = hop2_count.shape[1]
    fanout = hop1_ids.shape[1] // seed_total
    slots = hop2_ids.shape[1] // row_total
    slice_width = node_feats.shape[0]
    hidden_width = first_layer.shape[2]
    classes = second_layer.shape[2]
    capacity = round_up(seed_total + row_total // 2, 16)
    kept = round_up(capacity, LANES)
    column_rank = lax.axis_index("feat")
    group_start = lax.axis_index("dp") * groups
    sizes = lax.dynamic_slice_in_dim(batch_sizes, group_start, groups)
    order, enough = plan_rows(hop1_count, hop2_count, sizes, kept)
    own_codes = slot_codes(jnp.concatenate([seed_ids, hop1_ids], axis=1), True)
    near_codes = slot_codes(
        hop2_ids.reshape(groups, row_total, slots),
        jnp.arange(slots)[None, None, :] < hop2_count[:, :, None],
    ).reshape(groups, row_total * slots)
    count = lax.axis_size("feat")
    ring = ring_of(count)
    turns = jnp.array([[ring[(ring.index(i) + t) % count] for t in range(count)] for i in range(count)], jnp.int32)
    turn = lax.dynamic_index_in_dim(turns, column_rank, 0, keepdims=False)
    weights = lax.all_gather(first_layer.reshape(2 * slice_width, hidden_width), "feat", axis=0)
    inputs = gather_layer(node_feats, turn, enough, order, own_codes, near_codes, capacity)
    received = [inputs[0]] + [send_along(inputs[t], ring, t) for t in range(1, count)]
    behind = jnp.concatenate([turn[:1], turn[:0:-1]])

    def own(array):
        return lax.dynamic_index_in_dim(array, column_rank, 0, keepdims=False)

    sent = upper_layers(
        received, behind, weights, second_layer, own(order)[:capacity], own(hop1_count), own(label_ids),
        own(sizes), fanout,
    )
    grads = grad_layer(inputs, ring_gather(sent, ring), turn, seed_total, classes)
    return tuple(group_sum(grads, slice_width, classes))


def solution(mesh):
    return jax.shard_map(
        shards,
        mesh=mesh,
        in_specs=(
            P("feat", None),
            P(None, "feat", None),
            P(),
            P("dp", None),
            P("dp", None),
            P("dp", None),
            P("dp", None),
            P("dp", None),
            P(),
            P("dp", None),
        ),
        out_specs=(P(None, "feat", None), P()),
        check_vma=False,
    )
```

```python
import functools

import jax
import jax.numpy as jnp
from jax import lax
from jax.experimental import pallas as pl
from jax.experimental.pallas import tpu as pltpu
from jax.sharding import PartitionSpec as P

LANES = 128
TILE = 16
TILE_BITS = 4
UNROLL = 4
CALLS = 3
BLOCK = 256


def round_up(value, step):
    return (value + step - 1) // step * step


def plan_rows(hop1_count, hop2_count, sizes, kept):
    groups, seed_total = hop1_count.shape
    row_total = hop2_count.shape[1]
    fanout = (row_total - seed_total) // seed_total
    live = jnp.arange(seed_total)[None, :] < sizes[:, None]
    near = jnp.arange(fanout)[None, None, :] < jnp.where(live, hop1_count, 0)[:, :, None]
    used = jnp.concatenate([live, near.reshape(groups, -1)], axis=1)
    count = jnp.where(used, hop2_count, 0)
    row = jnp.arange(row_total)[None, :]
    mixed = count * row_total + (row_total - 1 - row)
    place = jnp.sum((mixed[:, None, :] > mixed[:, :, None]).astype(jnp.int32), axis=2)
    packed = row * 16 + count
    order = jnp.sum(
        jnp.where(place[:, None, :] == jnp.arange(kept)[None, :, None], packed[:, None, :], 0), axis=2
    )
    enough = jnp.sum(
        (count[:, None, :] >= jnp.arange(16)[None, :, None]).astype(jnp.int32), axis=2
    )
    return order, enough


def table_kernel(feats_ref, table_ref):
    step = pl.program_id(0)
    width, chunk = feats_ref.shape
    padded = table_ref.shape[1]
    down = lax.broadcasted_iota(jnp.int32, (BLOCK, BLOCK), 0)
    across = lax.broadcasted_iota(jnp.int32, (BLOCK, BLOCK), 1)
    identity = jnp.where(down == across, 1.0, 0.0).astype(jnp.bfloat16)
    for part in range(chunk // BLOCK):
        piece = feats_ref[:, part * BLOCK : (part + 1) * BLOCK]
        if padded > width:
            piece = jnp.concatenate([piece, jnp.zeros((padded - width, BLOCK), piece.dtype)], axis=0)
        turned = lax.dot_general(
            identity, piece, (((1,), (1,)), ((), ())), preferred_element_type=jnp.float32
        )
        start = pl.multiple_of(step * chunk + part * BLOCK, BLOCK)
        table_ref[pl.ds(start, BLOCK), :] = turned.astype(jnp.bfloat16)


def build_table(node_feats):
    width, nodes = node_feats.shape
    padded = max(width, LANES)
    chunk = min(nodes, 8192)
    return pl.pallas_call(
        table_kernel,
        grid=(nodes // chunk,),
        in_specs=[pl.BlockSpec((width, chunk), lambda step: (0, step))],
        out_specs=pl.BlockSpec(memory_space=pltpu.VMEM),
        out_shape=pltpu.VMEM((nodes, padded), jnp.bfloat16),
        compiler_params=pltpu.CompilerParams(vmem_limit_bytes=8 * 2**20),
        name="build_table",
    )(node_feats)


def gather_kernel(
    fanout, capacity, turn_ref, enough_ref, order_ref, own_ref, near_ref, count_ref, table_ref, *rest
):
    *inputs_refs, _, mask_ref, own_sum_ref, near_sum_ref = rest
    step = pl.program_id(0)
    width = inputs_refs[0].shape[1] // 2
    padded = table_ref.shape[1]

    @pl.when(step == 0)
    def _():
        shape = mask_ref.shape
        code = lax.broadcasted_iota(jnp.int32, shape, 0)
        line = lax.broadcasted_iota(jnp.int32, shape, 1)
        mask_ref[...] = jnp.where(code == line, 1.0, 0.0).astype(jnp.bfloat16)

    tiles = table_ref.reshape(table_ref.shape[0] // TILE, TILE, padded)

    def fetch(node):
        return (tiles[node >> TILE_BITS] * mask_ref[node & (TILE - 1)]).astype(jnp.float32)

    def fold(value):
        return value[: TILE // 2] + value[TILE // 2 :]

    def gather_rows(slots, first, number):
        owns, nears = [], []
        for i in range(number):
            row = order_ref[0, 0, first + i] >> 4
            owns.append(fold(fetch(own_ref[0, 0, row])))
            totals = [fetch(near_ref[0, 0, row * fanout + slot]) for slot in range(slots)]
            while len(totals) > 1:
                totals = [sum(totals[at + 1 : at + 2], totals[at]) for at in range(0, len(totals), 2)]
            nears.append(fold(totals[0]))
        for i in range(number):
            start = pl.multiple_of((first + i) * 8, 8)
            own_sum_ref[pl.ds(start, 8), :] = owns[i]
            near_sum_ref[pl.ds(start, 8), :] = nears[i]

    begin = 0
    for slots in range(fanout, 0, -1):
        end = enough_ref[0, 0, slots]
        whole = end - begin >= UNROLL

        def chunk_of(number, carry, slots=slots, begin=begin, end=end):
            gather_rows(slots, jnp.minimum(begin + number * UNROLL, end - UNROLL), UNROLL)
            return carry

        def one_of(at, carry, slots=slots):
            gather_rows(slots, at, 1)
            return carry

        lax.fori_loop(0, jnp.where(whole, lax.div(end - begin + UNROLL - 1, UNROLL), 0), chunk_of, 0)
        lax.fori_loop(begin, jnp.where(whole, begin, end), one_of, 0)
        begin = end

    def clear(at, carry):
        start = pl.multiple_of(at * 8, 8)
        own_sum_ref[pl.ds(start, 8), :] = jnp.zeros((8, padded), jnp.float32)
        near_sum_ref[pl.ds(start, 8), :] = jnp.zeros((8, padded), jnp.float32)
        return carry

    lax.fori_loop(begin, capacity, clear, 0)

    def collect(ref):
        total = ref[pl.ds(0, capacity, stride=8), :]
        for line in range(1, 8):
            total = total + ref[pl.ds(line, capacity, stride=8), :]
        return total

    counts = jnp.transpose(jnp.broadcast_to(count_ref[0], (padded, count_ref.shape[2])))[:capacity]
    own = collect(own_sum_ref).astype(jnp.bfloat16)[:, :width]
    near = (collect(near_sum_ref) / counts).astype(jnp.bfloat16)[:, :width]
    both = jnp.concatenate([own, near], axis=1)
    for place, inputs_ref in enumerate(inputs_refs):

        @pl.when(step == place)
        def _():
            inputs_ref[...] = both


def gather_layer(table, turn, begin, end, enough, order, counts, own_ids, near_ids, width, capacity):
    nodes, padded = table.shape
    groups = end - begin
    kept = order.shape[2]
    row_total = own_ids.shape[2]
    fanout = near_ids.shape[2] // row_total

    def group_of(step, turn_ref):
        return (turn_ref[begin + step], 0, 0)

    def per_group(length):
        return pl.BlockSpec((1, 1, length), group_of, memory_space=pltpu.SMEM)

    return pl.pallas_call(
        functools.partial(gather_kernel, fanout, capacity),
        grid_spec=pltpu.PrefetchScalarGridSpec(
            num_scalar_prefetch=1,
            grid=(groups,),
            in_specs=[
                per_group(16),
                per_group(kept),
                per_group(row_total),
                per_group(row_total * fanout),
                pl.BlockSpec((1, 1, kept), group_of),
                pl.BlockSpec(memory_space=pltpu.VMEM),
            ],
            out_specs=[pl.BlockSpec((capacity, 2 * width), lambda step, turn_ref: (0, 0))] * groups
            + [pl.BlockSpec(memory_space=pltpu.VMEM)],
            scratch_shapes=[
                pltpu.VMEM((TILE, TILE, padded), jnp.bfloat16),
                pltpu.VMEM((capacity * 8, padded), jnp.float32),
                pltpu.VMEM((capacity * 8, padded), jnp.float32),
            ],
        ),
        out_shape=[jax.ShapeDtypeStruct((capacity, 2 * width), jnp.bfloat16)] * groups
        + [pltpu.VMEM((nodes, padded), jnp.bfloat16)],
        input_output_aliases={6: groups},
        cost_estimate=pl.CostEstimate(
            flops=0, bytes_accessed=groups * capacity * fanout * TILE * padded * 2, transcendentals=0
        ),
        compiler_params=pltpu.CompilerParams(vmem_limit_bytes=14 * 2**20),
        name="gather_layer",
    )(
        turn, enough, order, own_ids, near_ids, counts,
        pltpu.with_memory_space_constraint(table, pltpu.VMEM),
    )


def upper_kernel(fanout, size_ref, turn_ref, weights_ref, layer_ref, row_ref, seed_ref, *rest):
    *inputs_refs, out_ref = rest
    seed_total = seed_ref.shape[1]
    capacity = inputs_refs[0].shape[0]
    hidden_width = weights_ref.shape[2]
    classes = layer_ref.shape[1]
    size = size_ref[0]
    seed = lax.broadcasted_iota(jnp.int32, (seed_total, capacity), 0)
    row = jnp.broadcast_to(row_ref[...], (seed_total, capacity))
    first = seed_total + seed * fanout
    is_seed = jnp.where(row == seed, 1.0, 0.0).astype(jnp.bfloat16)
    is_near = jnp.where((row >= first) & (row < first + fanout), 1.0, 0.0).astype(jnp.bfloat16)
    preact = jnp.zeros((capacity, hidden_width), jnp.float32)
    for place, inputs_ref in enumerate(inputs_refs):
        source = turn_ref[len(inputs_refs) + place]
        preact = preact + jnp.dot(inputs_ref[...], weights_ref[source], preferred_element_type=jnp.float32)
    hidden = jnp.maximum(preact, 0.0).astype(jnp.bfloat16)
    counts = seed_ref[0][:, :1].astype(jnp.float32)
    last = (((1,), (1,)), ((), ()))
    seed_hidden = jnp.dot(is_seed, hidden, preferred_element_type=jnp.float32).astype(jnp.bfloat16)
    near_mean = (jnp.dot(is_near, hidden, preferred_element_type=jnp.float32) / counts).astype(jnp.bfloat16)
    logits = lax.dot_general(seed_hidden, layer_ref[0], last, preferred_element_type=jnp.float32)
    logits = logits + lax.dot_general(near_mean, layer_ref[1], last, preferred_element_type=jnp.float32)
    exponent = jnp.exp(logits - jnp.max(logits, axis=1, keepdims=True))
    probabilities = exponent / jnp.sum(exponent, axis=1, keepdims=True)
    label = jnp.broadcast_to(seed_ref[1][:, :1], (seed_total, classes))
    onehot = jnp.where(label == lax.broadcasted_iota(jnp.int32, (seed_total, classes), 1), 1.0, 0.0)
    valid = lax.broadcasted_iota(jnp.int32, (seed_total, classes), 0) < size
    dlogits = jnp.where(valid, (probabilities - onehot) / size.astype(jnp.float32), 0.0).astype(jnp.bfloat16)
    back_seed = jnp.dot(dlogits, layer_ref[0], preferred_element_type=jnp.float32)
    back_near = jnp.dot(dlogits, layer_ref[1], preferred_element_type=jnp.float32) / counts
    rows = (((0,), (0,)), ((), ()))
    spread = lax.dot_general(is_seed, back_seed.astype(jnp.bfloat16), rows, preferred_element_type=jnp.float32)
    spread = spread + lax.dot_general(
        is_near, back_near.astype(jnp.bfloat16), rows, preferred_element_type=jnp.float32
    )
    out_ref[:capacity] = jnp.where(preact > 0, spread, 0.0).astype(jnp.bfloat16)
    out_ref[capacity : capacity + seed_total] = seed_hidden
    out_ref[capacity + seed_total : capacity + 2 * seed_total] = near_mean
    out_ref[capacity + 2 * seed_total :] = jnp.zeros((seed_total, hidden_width), jnp.bfloat16)
    out_ref[capacity + 2 * seed_total :, :classes] = dlogits


def upper_layers(inputs, size, turn, weights, layer, row, seeds, fanout):
    seed_total = seeds.shape[1]
    capacity = inputs[0].shape[0]
    hidden_width = weights.shape[2]
    smem = pl.BlockSpec(memory_space=pltpu.SMEM)
    vmem = pl.BlockSpec(memory_space=pltpu.VMEM)
    return pl.pallas_call(
        functools.partial(upper_kernel, fanout),
        in_specs=[smem] * 2 + [vmem] * (4 + len(inputs)),
        out_specs=vmem,
        out_shape=jax.ShapeDtypeStruct((capacity + 3 * seed_total, hidden_width), jnp.bfloat16),
        compiler_params=pltpu.CompilerParams(vmem_limit_bytes=32 * 2**20),
        name="upper_layers",
    )(size, turn, weights, layer, row, seeds, *inputs)


def grad_kernel(seed_total, classes, source_ref, *rest):
    count = (len(rest) - 2) // 2
    inputs_refs, sent_refs = rest[:count], rest[count : 2 * count]
    out_ref, units_ref = rest[2 * count :]
    capacity, double = inputs_refs[0].shape
    hidden_width = out_ref.shape[1]
    rows = (((0,), (0,)), ((), ()))
    first = jnp.zeros((double, hidden_width), jnp.float32)
    for place in range(count):
        first = first + lax.dot_general(
            inputs_refs[place][...], sent_refs[place][:capacity], rows, preferred_element_type=jnp.float32
        )
        start = pl.multiple_of(source_ref[place] * seed_total, seed_total)
        for part in range(3):
            units_ref[part, pl.ds(start, seed_total), :] = sent_refs[place][
                capacity + part * seed_total : capacity + (part + 1) * seed_total
            ]
    out_ref[:double] = first
    for layer in range(2):
        second = lax.dot_general(units_ref[2], units_ref[layer], rows, preferred_element_type=jnp.float32)
        start = double + layer * round_up(classes, 8)
        out_ref[start : start + round_up(classes, 8)] = second[: round_up(classes, 8)]


def grad_layer(inputs, sent, sources, seed_total, classes):
    capacity, double = inputs[0].shape
    hidden_width = sent[0].shape[1]
    vmem = pl.BlockSpec(memory_space=pltpu.VMEM)
    return pl.pallas_call(
        functools.partial(grad_kernel, seed_total, classes),
        in_specs=[pl.BlockSpec(memory_space=pltpu.SMEM)] + [vmem] * (2 * len(inputs)),
        out_specs=vmem,
        out_shape=jax.ShapeDtypeStruct((double + 2 * round_up(classes, 8), hidden_width), jnp.float32),
        scratch_shapes=[pltpu.VMEM((3, len(inputs) * seed_total, hidden_width), jnp.bfloat16)],
        compiler_params=pltpu.CompilerParams(vmem_limit_bytes=40 * 2**20),
        name="grad_layer",
    )(sources, *inputs, *sent)


def final_kernel(mine_ref, other_ref, first_ref, second_ref):
    width = first_ref.shape[1]
    classes = second_ref.shape[0]
    total = mine_ref[...].astype(jnp.float32) + other_ref[...].astype(jnp.float32)
    for layer in range(2):
        first_ref[layer] = total[layer * width : (layer + 1) * width]
        start = 2 * width + layer * round_up(classes, 8)
        second_ref[:, layer, :] = total[start : start + classes]


def final_sum(mine, other, width, classes):
    hidden_width = mine.shape[1]
    first, second = pl.pallas_call(
        final_kernel,
        out_shape=[
            jax.ShapeDtypeStruct((2, width, hidden_width), jnp.float32),
            jax.ShapeDtypeStruct((classes, 2, hidden_width), jnp.float32),
        ],
        name="final_sum",
    )(mine, other)
    return first, jnp.transpose(second, (1, 2, 0))


def ring_of(count):
    if count % 2:
        return list(range(count))
    return list(range(0, count, 2)) + list(range(count - 1, 0, -2))


def send_along(array, ring, shift):
    count = len(ring)
    return lax.ppermute(array, "feat", [(ring[i], ring[(i + shift) % count]) for i in range(count)])


def ring_gather(array, ring):
    count = len(ring)
    result = [array] + [None] * (count - 1)
    ahead = behind = array
    for hop in range(1, count // 2 + 1):
        behind = send_along(behind, ring, 1)
        result[count - hop] = behind
        if 2 * hop < count:
            ahead = send_along(ahead, ring, -1)
            result[hop] = ahead
    return result


def group_sum(grads, width, classes):
    count = lax.axis_size("dp")
    mine = grads
    stride = 1
    while 2 * stride < count:
        mine = mine + lax.ppermute(mine, "dp", [(i, i ^ stride) for i in range(count)])
        stride *= 2
    mine = mine.astype(jnp.bfloat16)
    if count > 1:
        other = lax.ppermute(mine, "dp", [(i, i ^ stride) for i in range(count)])
    else:
        other = jnp.zeros_like(mine)
    return final_sum(mine, other, width, classes)


def shards(
    node_feats,
    first_layer,
    second_layer,
    seed_ids,
    hop1_ids,
    hop1_count,
    hop2_ids,
    hop2_count,
    batch_sizes,
    label_ids,
):
    groups, seed_total = seed_ids.shape
    row_total = hop2_count.shape[1]
    fanout = hop1_ids.shape[1] // seed_total
    slice_width = node_feats.shape[0]
    hidden_width = first_layer.shape[2]
    classes = second_layer.shape[2]
    capacity = round_up(seed_total + row_total // 2, 16)
    kept = round_up(capacity, LANES)
    column_rank = lax.axis_index("feat")
    group_start = lax.axis_index("dp") * groups
    sizes = lax.dynamic_slice_in_dim(batch_sizes, group_start, groups)
    order, enough = plan_rows(hop1_count, hop2_count, sizes, kept)
    count = lax.axis_size("feat")
    ring = ring_of(count)
    places = sorted(range(count), key=lambda t: -min(t, count - t))
    turns = [
        [ring[(ring.index(i) + sign * t) % count] for sign in (1, -1) for t in places] for i in range(count)
    ]
    turn = lax.dynamic_index_in_dim(jnp.array(turns, jnp.int32), column_rank, 0, keepdims=False)
    weights = lax.all_gather(first_layer.reshape(2 * slice_width, hidden_width), "feat", axis=0)
    lists = [
        enough[:, None, :],
        order[:, None, :],
        jnp.maximum(order % 16, 1).astype(jnp.float32)[:, None, :],
        jnp.concatenate([seed_ids, hop1_ids], axis=1)[:, None, :],
        hop2_ids[:, None, :],
    ]

    def own(array):
        return lax.dynamic_index_in_dim(array, column_rank, 0, keepdims=False)

    own_order = own(order)[None, :capacity]
    row = jnp.where(own_order % 16 > 0, own_order // 16, -1)
    seeds = jnp.stack([own(hop1_count), own(label_ids)])
    seeds = jnp.broadcast_to(seeds[:, :, None], (2, seed_total, LANES))
    size = lax.dynamic_slice_in_dim(sizes, column_rank, 1)
    layer = jnp.transpose(second_layer, (0, 2, 1))
    node_feats, turn, size, layer, row, seeds, *lists = lax.optimization_barrier(
        (node_feats, turn, size, layer, row, seeds, *lists)
    )
    table = build_table(node_feats)
    inputs, received, arrived = [], [], []
    for call in range(CALLS):
        begin, end = -(-call * count // CALLS), -(-(call + 1) * count // CALLS)
        *blocks, table = gather_layer(table, turn, begin, end, *lists, slice_width, capacity)
        table, blocks, arrived = lax.optimization_barrier((table, blocks, arrived))
        inputs += blocks
        received += arrived
        arrived = [send_along(block, ring, t) if t else block for t, block in zip(places[begin:end], blocks)]
    received += arrived

    sent = upper_layers(received, size, turn, weights, layer, row, seeds, fanout)
    every = ring_gather(sent, ring)
    grads = grad_layer(inputs, [every[t] for t in places], turn, seed_total, classes)
    return tuple(group_sum(grads, slice_width, classes))


def solution(mesh):
    return jax.shard_map(
        shards,
        mesh=mesh,
        in_specs=(
            P("feat", None),
            P(None, "feat", None),
            P(),
            P("dp", None),
            P("dp", None),
            P("dp", None),
            P("dp", None),
            P("dp", None),
            P(),
            P("dp", None),
        ),
        out_specs=(P(None, "feat", None), P()),
        check_vma=False,
    )
```

```python
import functools

import jax
import jax.numpy as jnp
from jax import lax
from jax.experimental import pallas as pl
from jax.experimental.pallas import tpu as pltpu
from jax.sharding import PartitionSpec as P

LANES = 128
TILE = 16
TILE_BITS = 4
UNROLL = 4
CALLS = 3
BLOCK = 256


def round_up(value, step):
    return (value + step - 1) // step * step


def plan_rows(hop1_count, hop2_count, sizes, kept):
    groups, seed_total = hop1_count.shape
    row_total = hop2_count.shape[1]
    fanout = (row_total - seed_total) // seed_total
    live = jnp.arange(seed_total)[None, :] < sizes[:, None]
    near = jnp.arange(fanout)[None, None, :] < jnp.where(live, hop1_count, 0)[:, :, None]
    used = jnp.concatenate([live, near.reshape(groups, -1)], axis=1)
    count = jnp.where(used, hop2_count, 0)
    row = jnp.arange(row_total)[None, :]
    mixed = count * row_total + (row_total - 1 - row)
    place = jnp.sum((mixed[:, None, :] > mixed[:, :, None]).astype(jnp.int32), axis=2)
    packed = row * 16 + count
    order = jnp.sum(
        jnp.where(place[:, None, :] == jnp.arange(kept)[None, :, None], packed[:, None, :], 0), axis=2
    )
    enough = jnp.sum(
        (count[:, None, :] >= jnp.arange(16)[None, :, None]).astype(jnp.int32), axis=2
    )
    return order, enough


def table_kernel(feats_ref, table_ref):
    step = pl.program_id(0)
    width, chunk = feats_ref.shape
    padded = table_ref.shape[1]
    down = lax.broadcasted_iota(jnp.int32, (BLOCK, BLOCK), 0)
    across = lax.broadcasted_iota(jnp.int32, (BLOCK, BLOCK), 1)
    identity = jnp.where(down == across, 1.0, 0.0).astype(jnp.bfloat16)
    filler = jnp.zeros((padded - width, BLOCK), feats_ref.dtype)
    for part in range(0, chunk // BLOCK, 2):
        pieces = []
        for at in (part * BLOCK, (part + 1) * BLOCK):
            pieces.append(feats_ref[:, at : at + BLOCK])
            if padded > width:
                pieces.append(filler)
        turned = lax.dot_general(
            identity, jnp.concatenate(pieces, axis=0), (((1,), (1,)), ((), ())),
            preferred_element_type=jnp.float32,
        ).astype(jnp.bfloat16)
        for side in range(2):
            start = pl.multiple_of(step * chunk + (part + side) * BLOCK, BLOCK)
            table_ref[pl.ds(start, BLOCK), :] = turned[:, side * padded : (side + 1) * padded]


def build_table(node_feats):
    width, nodes = node_feats.shape
    padded = max(width, LANES)
    chunk = min(nodes, 8192)
    return pl.pallas_call(
        table_kernel,
        grid=(nodes // chunk,),
        in_specs=[pl.BlockSpec((width, chunk), lambda step: (0, step))],
        out_specs=pl.BlockSpec(memory_space=pltpu.VMEM),
        out_shape=pltpu.VMEM((nodes, padded), jnp.bfloat16),
        compiler_params=pltpu.CompilerParams(vmem_limit_bytes=8 * 2**20),
        name="build_table",
    )(node_feats)


def gather_kernel(
    fanout, capacity, turn_ref, enough_ref, order_ref, own_ref, near_ref, count_ref, table_ref, *rest
):
    *inputs_refs, _, own_sum_ref, near_sum_ref = rest
    step = pl.program_id(0)
    width = inputs_refs[0].shape[1] // 2
    padded = table_ref.shape[1]

    tiles = table_ref.reshape(table_ref.shape[0] // TILE, TILE, padded)
    half = TILE // 2
    low = lax.broadcasted_iota(jnp.int32, (half, padded), 0)
    high = low + half

    def fetch(node):
        tile = tiles[node >> TILE_BITS].astype(jnp.float32)
        line = jnp.full((half, padded), node, jnp.int32) & (TILE - 1)
        return jnp.where(line == low, tile[:half], jnp.where(line == high, tile[half:], 0.0))

    def gather_rows(slots, first, number):
        rows = [order_ref[0, 0, first + i] >> 4 for i in range(number)]
        starts = [row * fanout for row in rows]
        owns = [fetch(own_ref[0, 0, row]) for row in rows]
        nears = [fetch(near_ref[0, 0, start]) for start in starts]
        for slot in range(1, slots):
            nears = [near + fetch(near_ref[0, 0, start + slot]) for near, start in zip(nears, starts)]
        for i in range(number):
            place = pl.multiple_of((first + i) * half, half)
            own_sum_ref[pl.ds(place, half), :] = owns[i]
            near_sum_ref[pl.ds(place, half), :] = nears[i]

    begin = 0
    for slots in range(fanout, 0, -1):
        end = enough_ref[0, 0, slots]
        whole = end - begin >= UNROLL

        def chunk_of(number, carry, slots=slots, begin=begin, end=end):
            gather_rows(slots, jnp.minimum(begin + number * UNROLL, end - UNROLL), UNROLL)
            return carry

        def one_of(at, carry, slots=slots):
            gather_rows(slots, at, 1)
            return carry

        lax.fori_loop(0, jnp.where(whole, lax.div(end - begin + UNROLL - 1, UNROLL), 0), chunk_of, 0)
        lax.fori_loop(begin, jnp.where(whole, begin, end), one_of, 0)
        begin = end

    def clear(at, carry):
        start = pl.multiple_of(at * 8, 8)
        own_sum_ref[pl.ds(start, 8), :] = jnp.zeros((8, padded), jnp.float32)
        near_sum_ref[pl.ds(start, 8), :] = jnp.zeros((8, padded), jnp.float32)
        return carry

    lax.fori_loop(begin, capacity, clear, 0)

    def collect(ref):
        total = ref[pl.ds(0, capacity, stride=8), :]
        for line in range(1, 8):
            total = total + ref[pl.ds(line, capacity, stride=8), :]
        return total

    counts = jnp.transpose(jnp.broadcast_to(count_ref[0], (padded, count_ref.shape[2])))[:capacity]
    own = collect(own_sum_ref).astype(jnp.bfloat16)[:, :width]
    near = (collect(near_sum_ref) / counts).astype(jnp.bfloat16)[:, :width]
    both = jnp.concatenate([own, near], axis=1)
    for place, inputs_ref in enumerate(inputs_refs):

        @pl.when(step == place)
        def _():
            inputs_ref[...] = both


def gather_layer(table, turn, begin, end, enough, order, counts, own_ids, near_ids, width, capacity):
    nodes, padded = table.shape
    groups = end - begin
    kept = order.shape[2]
    row_total = own_ids.shape[2]
    fanout = near_ids.shape[2] // row_total

    def group_of(step, turn_ref):
        return (turn_ref[begin + step], 0, 0)

    def per_group(length):
        return pl.BlockSpec((1, 1, length), group_of, memory_space=pltpu.SMEM)

    return pl.pallas_call(
        functools.partial(gather_kernel, fanout, capacity),
        grid_spec=pltpu.PrefetchScalarGridSpec(
            num_scalar_prefetch=1,
            grid=(groups,),
            in_specs=[
                per_group(16),
                per_group(kept),
                per_group(row_total),
                per_group(row_total * fanout),
                pl.BlockSpec((1, 1, kept), group_of),
                pl.BlockSpec(memory_space=pltpu.VMEM),
            ],
            out_specs=[pl.BlockSpec((capacity, 2 * width), lambda step, turn_ref: (0, 0))] * groups
            + [pl.BlockSpec(memory_space=pltpu.VMEM)],
            scratch_shapes=[
                pltpu.VMEM((capacity * 8, padded), jnp.float32),
                pltpu.VMEM((capacity * 8, padded), jnp.float32),
            ],
        ),
        out_shape=[jax.ShapeDtypeStruct((capacity, 2 * width), jnp.bfloat16)] * groups
        + [pltpu.VMEM((nodes, padded), jnp.bfloat16)],
        input_output_aliases={6: groups},
        cost_estimate=pl.CostEstimate(
            flops=0, bytes_accessed=groups * capacity * fanout * TILE * padded * 2, transcendentals=0
        ),
        compiler_params=pltpu.CompilerParams(vmem_limit_bytes=14 * 2**20),
        name="gather_layer",
    )(
        turn, enough, order, own_ids, near_ids, counts,
        pltpu.with_memory_space_constraint(table, pltpu.VMEM),
    )


def upper_kernel(fanout, size_ref, turn_ref, weights_ref, layer_ref, row_ref, seed_ref, *rest):
    *inputs_refs, upper_ref, lower_ref = rest
    seed_total = seed_ref.shape[1]
    capacity = inputs_refs[0].shape[0]
    hidden_width = weights_ref.shape[2]
    classes = layer_ref.shape[1]
    size = size_ref[0]
    seed = lax.broadcasted_iota(jnp.int32, (seed_total, capacity), 0)
    row = jnp.broadcast_to(row_ref[...], (seed_total, capacity))
    first = seed_total + seed * fanout
    is_seed = jnp.where(row == seed, 1.0, 0.0).astype(jnp.bfloat16)
    is_near = jnp.where((row >= first) & (row < first + fanout), 1.0, 0.0).astype(jnp.bfloat16)
    preact = jnp.zeros((capacity, hidden_width), jnp.float32)
    for place, inputs_ref in enumerate(inputs_refs):
        source = turn_ref[len(inputs_refs) + place]
        preact = preact + jnp.dot(inputs_ref[...], weights_ref[source], preferred_element_type=jnp.float32)
    hidden = jnp.maximum(preact, 0.0).astype(jnp.bfloat16)
    counts = seed_ref[0][:, :1].astype(jnp.float32)
    last = (((1,), (1,)), ((), ()))
    seed_hidden = jnp.dot(is_seed, hidden, preferred_element_type=jnp.float32).astype(jnp.bfloat16)
    near_mean = (jnp.dot(is_near, hidden, preferred_element_type=jnp.float32) / counts).astype(jnp.bfloat16)
    logits = lax.dot_general(seed_hidden, layer_ref[0], last, preferred_element_type=jnp.float32)
    logits = logits + lax.dot_general(near_mean, layer_ref[1], last, preferred_element_type=jnp.float32)
    exponent = jnp.exp(logits - jnp.max(logits, axis=1, keepdims=True))
    probabilities = exponent / jnp.sum(exponent, axis=1, keepdims=True)
    label = jnp.broadcast_to(seed_ref[1][:, :1], (seed_total, classes))
    onehot = jnp.where(label == lax.broadcasted_iota(jnp.int32, (seed_total, classes), 1), 1.0, 0.0)
    valid = lax.broadcasted_iota(jnp.int32, (seed_total, classes), 0) < size
    dlogits = jnp.where(valid, (probabilities - onehot) / size.astype(jnp.float32), 0.0).astype(jnp.bfloat16)
    back_seed = jnp.dot(dlogits, layer_ref[0], preferred_element_type=jnp.float32)
    back_near = jnp.dot(dlogits, layer_ref[1], preferred_element_type=jnp.float32) / counts
    rows = (((0,), (0,)), ((), ()))
    spread = lax.dot_general(is_seed, back_seed.astype(jnp.bfloat16), rows, preferred_element_type=jnp.float32)
    spread = spread + lax.dot_general(
        is_near, back_near.astype(jnp.bfloat16), rows, preferred_element_type=jnp.float32
    )
    dpreact = jnp.where(preact > 0, spread, 0.0).astype(jnp.bfloat16)
    split = upper_ref.shape[0]
    upper_ref[...] = dpreact[:split]
    lower_ref[: capacity - split] = dpreact[split:]
    units = [seed_hidden, near_mean, jnp.zeros((seed_total, hidden_width), jnp.bfloat16)]
    for part, unit in enumerate(units):
        start = capacity - split + part * seed_total
        lower_ref[start : start + seed_total] = unit
    lower_ref[capacity - split + 2 * seed_total :, :classes] = dlogits


def upper_layers(inputs, size, turn, weights, layer, row, seeds, fanout):
    seed_total = seeds.shape[1]
    capacity = inputs[0].shape[0]
    hidden_width = weights.shape[2]
    total = capacity + 3 * seed_total
    split = round_up(total // 2, 16)
    smem = pl.BlockSpec(memory_space=pltpu.SMEM)
    vmem = pl.BlockSpec(memory_space=pltpu.VMEM)
    return pl.pallas_call(
        functools.partial(upper_kernel, fanout),
        in_specs=[smem] * 2 + [vmem] * (4 + len(inputs)),
        out_specs=[vmem] * 2,
        out_shape=[jax.ShapeDtypeStruct((length, hidden_width), jnp.bfloat16) for length in (split, total - split)],
        compiler_params=pltpu.CompilerParams(vmem_limit_bytes=32 * 2**20),
        name="upper_layers",
    )(size, turn, weights, layer, row, seeds, *inputs)


def grad_kernel(seed_total, classes, source_ref, *rest):
    count = (len(rest) - 2) // 3
    inputs_refs, upper_refs, lower_refs = rest[:count], rest[count : 2 * count], rest[2 * count : 3 * count]
    out_ref, units_ref = rest[3 * count :]
    capacity, double = inputs_refs[0].shape
    hidden_width = out_ref.shape[1]
    split = upper_refs[0].shape[0]
    rows = (((0,), (0,)), ((), ()))
    first = jnp.zeros((double, hidden_width), jnp.float32)
    for place in range(count):
        inputs_ref, upper_ref, lower_ref = inputs_refs[place], upper_refs[place], lower_refs[place]
        first = first + lax.dot_general(
            inputs_ref[:split], upper_ref[...], rows, preferred_element_type=jnp.float32
        )
        first = first + lax.dot_general(
            inputs_ref[split:], lower_ref[: capacity - split], rows, preferred_element_type=jnp.float32
        )
        start = pl.multiple_of(source_ref[place] * seed_total, seed_total)
        for part in range(3):
            begin = capacity - split + part * seed_total
            units_ref[part, pl.ds(start, seed_total), :] = lower_ref[begin : begin + seed_total]
    out_ref[:double] = first
    for layer in range(2):
        second = lax.dot_general(units_ref[2], units_ref[layer], rows, preferred_element_type=jnp.float32)
        start = double + layer * round_up(classes, 8)
        out_ref[start : start + round_up(classes, 8)] = second[: round_up(classes, 8)]


def grad_layer(inputs, upper, lower, sources, seed_total, classes):
    capacity, double = inputs[0].shape
    hidden_width = upper[0].shape[1]
    vmem = pl.BlockSpec(memory_space=pltpu.VMEM)
    return pl.pallas_call(
        functools.partial(grad_kernel, seed_total, classes),
        in_specs=[pl.BlockSpec(memory_space=pltpu.SMEM)] + [vmem] * (3 * len(inputs)),
        out_specs=vmem,
        out_shape=jax.ShapeDtypeStruct((double + 2 * round_up(classes, 8), hidden_width), jnp.float32),
        scratch_shapes=[pltpu.VMEM((3, len(inputs) * seed_total, hidden_width), jnp.bfloat16)],
        compiler_params=pltpu.CompilerParams(vmem_limit_bytes=40 * 2**20),
        name="grad_layer",
    )(sources, *inputs, *upper, *lower)


def final_kernel(mine_ref, other_ref, first_ref, second_ref):
    width = first_ref.shape[1]
    classes = second_ref.shape[0]
    total = mine_ref[...].astype(jnp.float32) + other_ref[...].astype(jnp.float32)
    for layer in range(2):
        first_ref[layer] = total[layer * width : (layer + 1) * width]
        start = 2 * width + layer * round_up(classes, 8)
        second_ref[:, layer, :] = total[start : start + classes]


def final_sum(mine, other, width, classes):
    hidden_width = mine.shape[1]
    first, second = pl.pallas_call(
        final_kernel,
        out_shape=[
            jax.ShapeDtypeStruct((2, width, hidden_width), jnp.float32),
            jax.ShapeDtypeStruct((classes, 2, hidden_width), jnp.float32),
        ],
        name="final_sum",
    )(mine, other)
    return first, jnp.transpose(second, (1, 2, 0))


def ring_of(count):
    if count % 2:
        return list(range(count))
    return list(range(0, count, 2)) + list(range(count - 1, 0, -2))


def send_along(array, ring, shift):
    count = len(ring)
    return lax.ppermute(array, "feat", [(ring[i], ring[(i + shift) % count]) for i in range(count)])


def ring_gather(upper, lower, ring):
    count = len(ring)
    halves = [[half] + [None] * (count - 1) for half in (upper, lower)]
    moving = [[half, half] for half in (upper, lower)]
    for hop in range(1, count // 2 + 1):
        for half in range(2):
            for way, sign in enumerate((1, -1)):
                if 2 * hop < count or half == way:
                    moving[half][way] = send_along(moving[half][way], ring, sign)
                    halves[half][-sign * hop % count] = moving[half][way]
    return halves


def group_sum(grads, width, classes):
    count = lax.axis_size("dp")
    mine = grads
    stride = 1
    while 2 * stride < count:
        mine = mine + lax.ppermute(mine, "dp", [(i, i ^ stride) for i in range(count)])
        stride *= 2
    mine = mine.astype(jnp.bfloat16)
    if count > 1:
        other = lax.ppermute(mine, "dp", [(i, i ^ stride) for i in range(count)])
    else:
        other = jnp.zeros_like(mine)
    return final_sum(mine, other, width, classes)


def shards(
    node_feats,
    first_layer,
    second_layer,
    seed_ids,
    hop1_ids,
    hop1_count,
    hop2_ids,
    hop2_count,
    batch_sizes,
    label_ids,
):
    groups, seed_total = seed_ids.shape
    row_total = hop2_count.shape[1]
    fanout = hop1_ids.shape[1] // seed_total
    slice_width = node_feats.shape[0]
    hidden_width = first_layer.shape[2]
    classes = second_layer.shape[2]
    capacity = round_up(seed_total + row_total // 2, 16)
    kept = round_up(capacity, LANES)
    column_rank = lax.axis_index("feat")
    group_start = lax.axis_index("dp") * groups
    sizes = lax.dynamic_slice_in_dim(batch_sizes, group_start, groups)
    order, enough = plan_rows(hop1_count, hop2_count, sizes, kept)
    count = lax.axis_size("feat")
    ring = ring_of(count)
    places = sorted(range(count), key=lambda t: -min(t, count - t))
    turns = [
        [ring[(ring.index(i) + sign * t) % count] for sign in (1, -1) for t in places] for i in range(count)
    ]
    turn = lax.dynamic_index_in_dim(jnp.array(turns, jnp.int32), column_rank, 0, keepdims=False)
    weights = lax.all_gather(first_layer.reshape(2 * slice_width, hidden_width), "feat", axis=0)
    lists = [
        enough[:, None, :],
        order[:, None, :],
        jnp.maximum(order % 16, 1).astype(jnp.float32)[:, None, :],
        jnp.concatenate([seed_ids, hop1_ids], axis=1)[:, None, :],
        hop2_ids[:, None, :],
    ]
    node_feats, turn, *lists = lax.optimization_barrier((node_feats, turn, *lists))
    table = build_table(node_feats)
    inputs, received, arrived = [], [], []
    for call in range(CALLS):
        begin, end = -(-call * count // CALLS), -(-(call + 1) * count // CALLS)
        *blocks, table = gather_layer(table, turn, begin, end, *lists, slice_width, capacity)
        if call < CALLS - 1:
            table, blocks, arrived = lax.optimization_barrier((table, blocks, arrived))
        else:
            blocks, arrived, order, hop1_count, label_ids, sizes, second_layer = lax.optimization_barrier(
                (blocks, arrived, order, hop1_count, label_ids, sizes, second_layer)
            )
        inputs += blocks
        received += arrived
        arrived = [send_along(block, ring, t) if t else block for t, block in zip(places[begin:end], blocks)]
    received += arrived

    def own(array):
        return lax.dynamic_index_in_dim(array, column_rank, 0, keepdims=False)

    own_order = own(order)[None, :capacity]
    row = jnp.where(own_order % 16 > 0, own_order // 16, -1)
    seeds = jnp.stack([own(hop1_count), own(label_ids)])
    seeds = jnp.broadcast_to(seeds[:, :, None], (2, seed_total, LANES))
    size = lax.dynamic_slice_in_dim(sizes, column_rank, 1)
    layer = jnp.transpose(second_layer, (0, 2, 1))
    halves = upper_layers(received, size, turn, weights, layer, row, seeds, fanout)
    upper, lower = ring_gather(*halves, ring)
    grads = grad_layer(
        inputs, [upper[t] for t in places], [lower[t] for t in places], turn, seed_total, classes
    )
    return tuple(group_sum(grads, slice_width, classes))


def solution(mesh):
    return jax.shard_map(
        shards,
        mesh=mesh,
        in_specs=(
            P("feat", None),
            P(None, "feat", None),
            P(),
            P("dp", None),
            P("dp", None),
            P("dp", None),
            P("dp", None),
            P("dp", None),
            P(),
            P("dp", None),
        ),
        out_specs=(P(None, "feat", None), P()),
        check_vma=False,
    )
```

```python
import functools

import jax
import jax.numpy as jnp
from jax import lax
from jax.experimental import pallas as pl
from jax.experimental.pallas import tpu as pltpu
from jax.sharding import PartitionSpec as P

LANES = 128
TILE = 16
TILE_BITS = 4
UNROLL = TILE // 4
CALLS = 3
BLOCK = 256


def round_up(value, step):
    return (value + step - 1) // step * step


def plan_rows(hop1_count, hop2_count, sizes, kept):
    groups, seed_total = hop1_count.shape
    row_total = hop2_count.shape[1]
    fanout = (row_total - seed_total) // seed_total
    live = jnp.arange(seed_total)[None, :] < sizes[:, None]
    near = jnp.arange(fanout)[None, None, :] < jnp.where(live, hop1_count, 0)[:, :, None]
    used = jnp.concatenate([live, near.reshape(groups, -1)], axis=1)
    count = jnp.where(used, hop2_count, 0)
    row = jnp.arange(row_total)[None, :]
    mixed = count * row_total + (row_total - 1 - row)
    place = jnp.sum((mixed[:, None, :] > mixed[:, :, None]).astype(jnp.int32), axis=2)
    packed = row * 16 + count
    order = jnp.sum(
        jnp.where(place[:, None, :] == jnp.arange(kept)[None, :, None], packed[:, None, :], 0), axis=2
    )
    enough = jnp.sum(
        (count[:, None, :] >= jnp.arange(16)[None, :, None]).astype(jnp.int32), axis=2
    )
    return order, enough


def table_kernel(feats_ref, table_ref):
    step = pl.program_id(0)
    width, chunk = feats_ref.shape
    padded = table_ref.shape[1]
    down = lax.broadcasted_iota(jnp.int32, (BLOCK, BLOCK), 0)
    across = lax.broadcasted_iota(jnp.int32, (BLOCK, BLOCK), 1)
    identity = jnp.where(down == across, 1.0, 0.0).astype(jnp.bfloat16)
    filler = jnp.zeros((padded - width, BLOCK), feats_ref.dtype)
    for part in range(0, chunk // BLOCK, 2):
        pieces = []
        for at in (part * BLOCK, (part + 1) * BLOCK):
            pieces.append(feats_ref[:, at : at + BLOCK])
            if padded > width:
                pieces.append(filler)
        both = jnp.concatenate(pieces, axis=0)
        if part % 4:
            turned = jnp.transpose(both)
        else:
            turned = lax.dot_general(
                identity, both, (((1,), (1,)), ((), ())), preferred_element_type=jnp.float32
            ).astype(jnp.bfloat16)
        for side in range(2):
            start = pl.multiple_of(step * chunk + (part + side) * BLOCK, BLOCK)
            table_ref[pl.ds(start, BLOCK), :] = turned[:, side * padded : (side + 1) * padded]


def build_table(node_feats):
    width, nodes = node_feats.shape
    padded = max(width, LANES)
    chunk = min(nodes, 8192)
    return pl.pallas_call(
        table_kernel,
        grid=(nodes // chunk,),
        in_specs=[pl.BlockSpec((width, chunk), lambda step: (0, step))],
        out_specs=pl.BlockSpec(memory_space=pltpu.VMEM),
        out_shape=pltpu.VMEM((nodes, padded), jnp.bfloat16),
        compiler_params=pltpu.CompilerParams(vmem_limit_bytes=8 * 2**20),
        name="build_table",
    )(node_feats)


def gather_kernel(
    fanout, capacity, turn_ref, enough_ref, order_ref, own_ref, near_ref, count_ref, table_ref, *rest
):
    *inputs_refs, _, own_sum_ref, near_sum_ref = rest
    step = pl.program_id(0)
    width = inputs_refs[0].shape[1] // 2
    padded = table_ref.shape[1]

    tiles = table_ref.reshape(table_ref.shape[0] // TILE, TILE, padded)
    half = TILE // 2
    low = lax.broadcasted_iota(jnp.int32, (half, padded), 0)
    high = low + half

    def fetch(node):
        tile = tiles[node >> TILE_BITS].astype(jnp.float32)
        line = jnp.full((half, padded), node, jnp.int32) & (TILE - 1)
        return jnp.where(line == low, tile[:half], jnp.where(line == high, tile[half:], 0.0))

    def add_lines(values):
        step = 1
        while step < half:
            chosen = (low & step) == 0
            values = [
                jnp.where(chosen, one, two) + pltpu.roll(jnp.where(chosen, two, one), half - step, 0)
                for one, two in zip(values[::2], values[1::2])
            ]
            step *= 2
        return values[0]

    def gather_rows(slots, first, number):
        rows = [order_ref[0, 0, first + i] >> 4 for i in range(number)]
        starts = [row * fanout for row in rows]
        owns = [fetch(own_ref[0, 0, row]) for row in rows]
        nears = [fetch(near_ref[0, 0, start]) for start in starts]
        for slot in range(1, slots):
            nears = [near + fetch(near_ref[0, 0, start + slot]) for near, start in zip(nears, starts)]
        empty = [jnp.zeros((half, padded), jnp.float32)] * (UNROLL - number)
        totals = add_lines(owns + empty + nears + empty)
        own_sum_ref[pl.ds(first, number), :] = totals[:number]
        near_sum_ref[pl.ds(first, number), :] = totals[UNROLL : UNROLL + number]

    begin = 0
    for slots in range(fanout, 0, -1):
        end = enough_ref[0, 0, slots]
        whole = end - begin >= UNROLL

        def chunk_of(number, carry, slots=slots, begin=begin, end=end):
            gather_rows(slots, jnp.minimum(begin + number * UNROLL, end - UNROLL), UNROLL)
            return carry

        def one_of(at, carry, slots=slots):
            gather_rows(slots, at, 1)
            return carry

        lax.fori_loop(0, jnp.where(whole, lax.div(end - begin + UNROLL - 1, UNROLL), 0), chunk_of, 0)
        lax.fori_loop(begin, jnp.where(whole, begin, end), one_of, 0)
        begin = end

    def clear(at, carry):
        own_sum_ref[pl.ds(at, 1), :] = jnp.zeros((1, padded), jnp.float32)
        near_sum_ref[pl.ds(at, 1), :] = jnp.zeros((1, padded), jnp.float32)
        return carry

    lax.fori_loop(begin, capacity, clear, 0)
    counts = jnp.transpose(jnp.broadcast_to(count_ref[0], (padded, count_ref.shape[2])))[:capacity]
    own = own_sum_ref[...].astype(jnp.bfloat16)[:, :width]
    near = (near_sum_ref[...] / counts).astype(jnp.bfloat16)[:, :width]
    both = jnp.concatenate([own, near], axis=1)
    for place, inputs_ref in enumerate(inputs_refs):

        @pl.when(step == place)
        def _():
            inputs_ref[...] = both


def gather_layer(table, turn, begin, end, enough, order, counts, own_ids, near_ids, width, capacity):
    nodes, padded = table.shape
    groups = end - begin
    kept = order.shape[2]
    row_total = own_ids.shape[2]
    fanout = near_ids.shape[2] // row_total

    def group_of(step, turn_ref):
        return (turn_ref[begin + step], 0, 0)

    def per_group(length):
        return pl.BlockSpec((1, 1, length), group_of, memory_space=pltpu.SMEM)

    return pl.pallas_call(
        functools.partial(gather_kernel, fanout, capacity),
        grid_spec=pltpu.PrefetchScalarGridSpec(
            num_scalar_prefetch=1,
            grid=(groups,),
            in_specs=[
                per_group(16),
                per_group(kept),
                per_group(row_total),
                per_group(row_total * fanout),
                pl.BlockSpec((1, 1, kept), group_of),
                pl.BlockSpec(memory_space=pltpu.VMEM),
            ],
            out_specs=[pl.BlockSpec((capacity, 2 * width), lambda step, turn_ref: (0, 0))] * groups
            + [pl.BlockSpec(memory_space=pltpu.VMEM)],
            scratch_shapes=[
                pltpu.VMEM((capacity, padded), jnp.float32),
                pltpu.VMEM((capacity, padded), jnp.float32),
            ],
        ),
        out_shape=[jax.ShapeDtypeStruct((capacity, 2 * width), jnp.bfloat16)] * groups
        + [pltpu.VMEM((nodes, padded), jnp.bfloat16)],
        input_output_aliases={6: groups},
        cost_estimate=pl.CostEstimate(
            flops=0, bytes_accessed=groups * capacity * fanout * TILE * padded * 2, transcendentals=0
        ),
        compiler_params=pltpu.CompilerParams(vmem_limit_bytes=14 * 2**20),
        name="gather_layer",
    )(
        turn, enough, order, own_ids, near_ids, counts,
        pltpu.with_memory_space_constraint(table, pltpu.VMEM),
    )


def upper_kernel(fanout, size_ref, turn_ref, weights_ref, layer_ref, row_ref, seed_ref, *rest):
    *inputs_refs, upper_ref, lower_ref = rest
    seed_total = seed_ref.shape[1]
    capacity = inputs_refs[0].shape[0]
    hidden_width = weights_ref.shape[2]
    classes = layer_ref.shape[1]
    size = size_ref[0]
    seed = lax.broadcasted_iota(jnp.int32, (seed_total, capacity), 0)
    row = jnp.broadcast_to(row_ref[...], (seed_total, capacity))
    first = seed_total + seed * fanout
    is_seed = jnp.where(row == seed, 1.0, 0.0).astype(jnp.bfloat16)
    is_near = jnp.where((row >= first) & (row < first + fanout), 1.0, 0.0).astype(jnp.bfloat16)
    preact = jnp.zeros((capacity, hidden_width), jnp.float32)
    for place, inputs_ref in enumerate(inputs_refs):
        source = turn_ref[len(inputs_refs) + place]
        preact = preact + jnp.dot(inputs_ref[...], weights_ref[source], preferred_element_type=jnp.float32)
    hidden = jnp.maximum(preact, 0.0).astype(jnp.bfloat16)
    counts = seed_ref[0][:, :1].astype(jnp.float32)
    last = (((1,), (1,)), ((), ()))
    seed_hidden = jnp.dot(is_seed, hidden, preferred_element_type=jnp.float32).astype(jnp.bfloat16)
    near_mean = (jnp.dot(is_near, hidden, preferred_element_type=jnp.float32) / counts).astype(jnp.bfloat16)
    logits = lax.dot_general(seed_hidden, layer_ref[0], last, preferred_element_type=jnp.float32)
    logits = logits + lax.dot_general(near_mean, layer_ref[1], last, preferred_element_type=jnp.float32)
    exponent = jnp.exp(logits - jnp.max(logits, axis=1, keepdims=True))
    probabilities = exponent / jnp.sum(exponent, axis=1, keepdims=True)
    label = jnp.broadcast_to(seed_ref[1][:, :1], (seed_total, classes))
    onehot = jnp.where(label == lax.broadcasted_iota(jnp.int32, (seed_total, classes), 1), 1.0, 0.0)
    valid = lax.broadcasted_iota(jnp.int32, (seed_total, classes), 0) < size
    dlogits = jnp.where(valid, (probabilities - onehot) / size.astype(jnp.float32), 0.0).astype(jnp.bfloat16)
    back_seed = jnp.dot(dlogits, layer_ref[0], preferred_element_type=jnp.float32)
    back_near = jnp.dot(dlogits, layer_ref[1], preferred_element_type=jnp.float32) / counts
    rows = (((0,), (0,)), ((), ()))
    spread = lax.dot_general(is_seed, back_seed.astype(jnp.bfloat16), rows, preferred_element_type=jnp.float32)
    spread = spread + lax.dot_general(
        is_near, back_near.astype(jnp.bfloat16), rows, preferred_element_type=jnp.float32
    )
    dpreact = jnp.where(preact > 0, spread, 0.0).astype(jnp.bfloat16)
    split = upper_ref.shape[0]
    upper_ref[...] = dpreact[:split]
    lower_ref[: capacity - split] = dpreact[split:]
    units = [seed_hidden, near_mean, jnp.zeros((seed_total, hidden_width), jnp.bfloat16)]
    for part, unit in enumerate(units):
        start = capacity - split + part * seed_total
        lower_ref[start : start + seed_total] = unit
    lower_ref[capacity - split + 2 * seed_total :, :classes] = dlogits


def upper_layers(inputs, size, turn, weights, layer, row, seeds, fanout):
    seed_total = seeds.shape[1]
    capacity = inputs[0].shape[0]
    hidden_width = weights.shape[2]
    total = capacity + 3 * seed_total
    split = round_up(total // 2, 16)
    smem = pl.BlockSpec(memory_space=pltpu.SMEM)
    vmem = pl.BlockSpec(memory_space=pltpu.VMEM)
    return pl.pallas_call(
        functools.partial(upper_kernel, fanout),
        in_specs=[smem] * 2 + [vmem] * (4 + len(inputs)),
        out_specs=[vmem] * 2,
        out_shape=[jax.ShapeDtypeStruct((length, hidden_width), jnp.bfloat16) for length in (split, total - split)],
        compiler_params=pltpu.CompilerParams(vmem_limit_bytes=32 * 2**20),
        name="upper_layers",
    )(size, turn, weights, layer, row, seeds, *inputs)


def grad_kernel(seed_total, classes, source_ref, *rest):
    count = (len(rest) - 2) // 3
    inputs_refs, upper_refs, lower_refs = rest[:count], rest[count : 2 * count], rest[2 * count : 3 * count]
    out_ref, units_ref = rest[3 * count :]
    capacity, double = inputs_refs[0].shape
    hidden_width = out_ref.shape[1]
    split = upper_refs[0].shape[0]
    rows = (((0,), (0,)), ((), ()))
    first = jnp.zeros((double, hidden_width), jnp.float32)
    for place in range(count):
        inputs_ref, upper_ref, lower_ref = inputs_refs[place], upper_refs[place], lower_refs[place]
        first = first + lax.dot_general(
            inputs_ref[:split], upper_ref[...], rows, preferred_element_type=jnp.float32
        )
        first = first + lax.dot_general(
            inputs_ref[split:], lower_ref[: capacity - split], rows, preferred_element_type=jnp.float32
        )
        start = pl.multiple_of(source_ref[place] * seed_total, seed_total)
        for part in range(3):
            begin = capacity - split + part * seed_total
            units_ref[part, pl.ds(start, seed_total), :] = lower_ref[begin : begin + seed_total]
    out_ref[:double] = first
    for layer in range(2):
        second = lax.dot_general(units_ref[2], units_ref[layer], rows, preferred_element_type=jnp.float32)
        start = double + layer * round_up(classes, 8)
        out_ref[start : start + round_up(classes, 8)] = second[: round_up(classes, 8)]


def grad_layer(inputs, upper, lower, sources, seed_total, classes):
    capacity, double = inputs[0].shape
    hidden_width = upper[0].shape[1]
    vmem = pl.BlockSpec(memory_space=pltpu.VMEM)
    return pl.pallas_call(
        functools.partial(grad_kernel, seed_total, classes),
        in_specs=[pl.BlockSpec(memory_space=pltpu.SMEM)] + [vmem] * (3 * len(inputs)),
        out_specs=vmem,
        out_shape=jax.ShapeDtypeStruct((double + 2 * round_up(classes, 8), hidden_width), jnp.float32),
        scratch_shapes=[pltpu.VMEM((3, len(inputs) * seed_total, hidden_width), jnp.bfloat16)],
        compiler_params=pltpu.CompilerParams(vmem_limit_bytes=40 * 2**20),
        name="grad_layer",
    )(sources, *inputs, *upper, *lower)


def final_kernel(mine_ref, other_ref, first_ref, second_ref):
    width = first_ref.shape[1]
    classes = second_ref.shape[0]
    total = mine_ref[...].astype(jnp.float32) + other_ref[...].astype(jnp.float32)
    for layer in range(2):
        first_ref[layer] = total[layer * width : (layer + 1) * width]
        start = 2 * width + layer * round_up(classes, 8)
        second_ref[:, layer, :] = total[start : start + classes]


def final_sum(mine, other, width, classes):
    hidden_width = mine.shape[1]
    first, second = pl.pallas_call(
        final_kernel,
        out_shape=[
            jax.ShapeDtypeStruct((2, width, hidden_width), jnp.float32),
            jax.ShapeDtypeStruct((classes, 2, hidden_width), jnp.float32),
        ],
        name="final_sum",
    )(mine, other)
    return first, jnp.transpose(second, (1, 2, 0))


def ring_of(count):
    if count % 2:
        return list(range(count))
    return list(range(0, count, 2)) + list(range(count - 1, 0, -2))


def send_along(array, ring, shift):
    count = len(ring)
    return lax.ppermute(array, "feat", [(ring[i], ring[(i + shift) % count]) for i in range(count)])


def ring_gather(upper, lower, ring):
    count = len(ring)
    halves = [[half] + [None] * (count - 1) for half in (upper, lower)]
    moving = [[half, half] for half in (upper, lower)]
    for hop in range(1, count // 2 + 1):
        for half in range(2):
            for way, sign in enumerate((1, -1)):
                if 2 * hop < count or half == way:
                    moving[half][way] = send_along(moving[half][way], ring, sign)
                    halves[half][-sign * hop % count] = moving[half][way]
    return halves


def group_sum(grads, width, classes):
    count = lax.axis_size("dp")
    mine = grads
    stride = 1
    while 2 * stride < count:
        mine = mine + lax.ppermute(mine, "dp", [(i, i ^ stride) for i in range(count)])
        stride *= 2
    mine = mine.astype(jnp.bfloat16)
    if count > 1:
        other = lax.ppermute(mine, "dp", [(i, i ^ stride) for i in range(count)])
    else:
        other = jnp.zeros_like(mine)
    return final_sum(mine, other, width, classes)


def shards(
    node_feats,
    first_layer,
    second_layer,
    seed_ids,
    hop1_ids,
    hop1_count,
    hop2_ids,
    hop2_count,
    batch_sizes,
    label_ids,
):
    groups, seed_total = seed_ids.shape
    row_total = hop2_count.shape[1]
    fanout = hop1_ids.shape[1] // seed_total
    slice_width = node_feats.shape[0]
    hidden_width = first_layer.shape[2]
    classes = second_layer.shape[2]
    capacity = round_up(seed_total + row_total // 2, 16)
    kept = round_up(capacity, LANES)
    column_rank = lax.axis_index("feat")
    group_start = lax.axis_index("dp") * groups
    sizes = lax.dynamic_slice_in_dim(batch_sizes, group_start, groups)
    order, enough = plan_rows(hop1_count, hop2_count, sizes, kept)
    count = lax.axis_size("feat")
    ring = ring_of(count)
    places = sorted(range(count), key=lambda t: -min(t, count - t))
    turns = [
        [ring[(ring.index(i) + sign * t) % count] for sign in (1, -1) for t in places] for i in range(count)
    ]
    turn = lax.dynamic_index_in_dim(jnp.array(turns, jnp.int32), column_rank, 0, keepdims=False)
    weights = lax.all_gather(first_layer.reshape(2 * slice_width, hidden_width), "feat", axis=0)
    lists = [
        enough[:, None, :],
        order[:, None, :],
        jnp.maximum(order % 16, 1).astype(jnp.float32)[:, None, :],
        jnp.concatenate([seed_ids, hop1_ids], axis=1)[:, None, :],
        hop2_ids[:, None, :],
    ]
    node_feats, turn, *lists = lax.optimization_barrier((node_feats, turn, *lists))
    table = build_table(node_feats)
    inputs, received, arrived = [], [], []
    for call in range(CALLS):
        begin, end = -(-call * count // CALLS), -(-(call + 1) * count // CALLS)
        *blocks, table = gather_layer(table, turn, begin, end, *lists, slice_width, capacity)
        if call < CALLS - 1:
            table, blocks, arrived = lax.optimization_barrier((table, blocks, arrived))
        else:
            blocks, arrived, order, hop1_count, label_ids, sizes, second_layer = lax.optimization_barrier(
                (blocks, arrived, order, hop1_count, label_ids, sizes, second_layer)
            )
        inputs += blocks
        received += arrived
        arrived = [send_along(block, ring, t) if t else block for t, block in zip(places[begin:end], blocks)]
    received += arrived

    def own(array):
        return lax.dynamic_index_in_dim(array, column_rank, 0, keepdims=False)

    own_order = own(order)[None, :capacity]
    row = jnp.where(own_order % 16 > 0, own_order // 16, -1)
    seeds = jnp.stack([own(hop1_count), own(label_ids)])
    seeds = jnp.broadcast_to(seeds[:, :, None], (2, seed_total, LANES))
    size = lax.dynamic_slice_in_dim(sizes, column_rank, 1)
    layer = jnp.transpose(second_layer, (0, 2, 1))
    halves = upper_layers(received, size, turn, weights, layer, row, seeds, fanout)
    upper, lower = ring_gather(*halves, ring)
    grads = grad_layer(
        inputs, [upper[t] for t in places], [lower[t] for t in places], turn, seed_total, classes
    )
    return tuple(group_sum(grads, slice_width, classes))


def solution(mesh):
    return jax.shard_map(
        shards,
        mesh=mesh,
        in_specs=(
            P("feat", None),
            P(None, "feat", None),
            P(),
            P("dp", None),
            P("dp", None),
            P("dp", None),
            P("dp", None),
            P("dp", None),
            P(),
            P("dp", None),
        ),
        out_specs=(P(None, "feat", None), P()),
        check_vma=False,
    )
```

```python
import functools

import jax
import jax.numpy as jnp
from jax import lax
from jax.experimental import pallas as pl
from jax.experimental.pallas import tpu as pltpu
from jax.sharding import PartitionSpec as P

LANES = 128
TILE = 16
TILE_BITS = 4
CALLS = 3
BLOCK = 256


def round_up(value, step):
    return (value + step - 1) // step * step


def plan_rows(hop1_count, hop2_count, sizes, kept):
    groups, seed_total = hop1_count.shape
    row_total = hop2_count.shape[1]
    fanout = (row_total - seed_total) // seed_total
    live = jnp.arange(seed_total)[None, :] < sizes[:, None]
    near = jnp.arange(fanout)[None, None, :] < jnp.where(live, hop1_count, 0)[:, :, None]
    used = jnp.concatenate([live, near.reshape(groups, -1)], axis=1)
    count = jnp.where(used, hop2_count, 0)
    row = jnp.arange(row_total)[None, :]
    mixed = count * row_total + (row_total - 1 - row)
    place = jnp.sum((mixed[:, None, :] > mixed[:, :, None]).astype(jnp.int32), axis=2)
    packed = row * 16 + count
    order = jnp.sum(
        jnp.where(place[:, None, :] == jnp.arange(kept)[None, :, None], packed[:, None, :], 0), axis=2
    )
    enough = jnp.sum(
        (count[:, None, :] >= jnp.arange(16)[None, :, None]).astype(jnp.int32), axis=2
    )
    return order, enough


def table_kernel(*refs):
    *feats_refs, table_ref = refs
    step = pl.program_id(0)
    chunk = feats_refs[0].shape[1]
    width = sum(ref.shape[0] for ref in feats_refs)
    padded = table_ref.shape[1]
    down = lax.broadcasted_iota(jnp.int32, (BLOCK, BLOCK), 0)
    across = lax.broadcasted_iota(jnp.int32, (BLOCK, BLOCK), 1)
    identity = jnp.where(down == across, 1.0, 0.0).astype(jnp.bfloat16)
    filler = jnp.zeros((padded - width, BLOCK), jnp.bfloat16)
    for part in range(0, chunk // BLOCK, 2):
        pieces = []
        for at in (part * BLOCK, (part + 1) * BLOCK):
            pieces += [feats_ref[:, at : at + BLOCK] for feats_ref in feats_refs]
            if padded > width:
                pieces.append(filler)
        both = jnp.concatenate(pieces, axis=0)
        if part % 4:
            turned = jnp.transpose(both)
        else:
            turned = lax.dot_general(
                identity, both, (((1,), (1,)), ((), ())), preferred_element_type=jnp.float32
            ).astype(jnp.bfloat16)
        for side in range(2):
            start = pl.multiple_of(step * chunk + (part + side) * BLOCK, BLOCK)
            table_ref[pl.ds(start, BLOCK), :] = turned[:, side * padded : (side + 1) * padded]


def build_table(node_feats):
    width, nodes = node_feats.shape
    padded = max(width, LANES)
    chunk = min(nodes, 8192)
    streams = max(1, width // 32)
    return pl.pallas_call(
        table_kernel,
        grid=(nodes // chunk,),
        in_specs=[pl.BlockSpec((width // streams, chunk), lambda step, at=at: (at, step)) for at in range(streams)],
        out_specs=pl.BlockSpec(memory_space=pltpu.VMEM),
        out_shape=pltpu.VMEM((nodes, padded), jnp.bfloat16),
        compiler_params=pltpu.CompilerParams(vmem_limit_bytes=8 * 2**20),
        name="build_table",
    )(*[node_feats] * streams)


def gather_kernel(
    fanout, capacity, turn_ref, enough_ref, order_ref, own_ref, near_ref, count_ref, table_ref, *rest
):
    *inputs_refs, _, own_sum_ref, near_sum_ref = rest
    step = pl.program_id(0)
    width = inputs_refs[0].shape[1] // 2
    padded = table_ref.shape[1]

    tiles = table_ref.reshape(table_ref.shape[0] // TILE, TILE, padded)
    half = TILE // 2
    low = lax.broadcasted_iota(jnp.int32, (half, padded), 0)
    high = low + half

    def fetch(node, wanted=None):
        tile = tiles[node >> TILE_BITS].astype(jnp.float32)
        if wanted is None:
            line = jnp.full((half, padded), node, jnp.int32) & (TILE - 1)
        else:
            line = jnp.full((half, padded), jnp.where(wanted, node & (TILE - 1), TILE), jnp.int32)
        return jnp.where(line == low, tile[:half], jnp.where(line == high, tile[half:], 0.0))

    def add_lines(values):
        step = 1
        while step < half:
            chosen = (low & step) == 0
            values = [
                jnp.where(chosen, one, two) + pltpu.roll(jnp.where(chosen, two, one), half - step, 0)
                for one, two in zip(values[::2], values[1::2])
            ]
            step *= 2
        return values[0]

    def gather_rows(slots, exact, number, carry):
        first = pl.multiple_of(number * half, half)
        entries = [order_ref[0, 0, first + i] for i in range(half)]
        rows = [entry >> 4 for entry in entries]
        starts = [row * fanout for row in rows]

        def near(i, slot):
            node = near_ref[0, 0, starts[i] + slot]
            return fetch(node) if exact else fetch(node, slot < (entries[i] & 15))

        own_sum_ref[pl.ds(first, half), :] = add_lines([fetch(own_ref[0, 0, row]) for row in rows])
        nears = [near(i, 0) for i in range(half)]
        for slot in range(1, slots):
            nears = [nears[i] + near(i, slot) for i in range(half)]
        near_sum_ref[pl.ds(first, half), :] = add_lines(nears)
        return carry

    start = 0
    for slots in range(fanout, 0, -1):
        end = enough_ref[0, 0, slots]
        whole = jnp.maximum(lax.div(end, half), start)
        stop = lax.div(end + half - 1, half)
        lax.fori_loop(start, whole, functools.partial(gather_rows, slots, True), 0)
        lax.fori_loop(whole, stop, functools.partial(gather_rows, slots, False), 0)
        start = stop

    def clear(number, carry):
        first = pl.multiple_of(number * half, half)
        own_sum_ref[pl.ds(first, half), :] = jnp.zeros((half, padded), jnp.float32)
        near_sum_ref[pl.ds(first, half), :] = jnp.zeros((half, padded), jnp.float32)
        return carry

    lax.fori_loop(start, capacity // half, clear, 0)
    counts = jnp.transpose(jnp.broadcast_to(count_ref[0], (padded, count_ref.shape[2])))[:capacity]
    own = own_sum_ref[...].astype(jnp.bfloat16)[:, :width]
    near = (near_sum_ref[...] / counts).astype(jnp.bfloat16)[:, :width]
    both = jnp.concatenate([own, near], axis=1)
    for place, inputs_ref in enumerate(inputs_refs):

        @pl.when(step == place)
        def _():
            inputs_ref[...] = both


def gather_layer(table, turn, begin, end, enough, order, counts, own_ids, near_ids, width, capacity):
    nodes, padded = table.shape
    groups = end - begin
    kept = order.shape[2]
    row_total = own_ids.shape[2]
    fanout = near_ids.shape[2] // row_total

    def group_of(step, turn_ref):
        return (turn_ref[begin + step], 0, 0)

    def per_group(length):
        return pl.BlockSpec((1, 1, length), group_of, memory_space=pltpu.SMEM)

    return pl.pallas_call(
        functools.partial(gather_kernel, fanout, capacity),
        grid_spec=pltpu.PrefetchScalarGridSpec(
            num_scalar_prefetch=1,
            grid=(groups,),
            in_specs=[
                per_group(16),
                per_group(kept),
                per_group(row_total),
                per_group(row_total * fanout),
                pl.BlockSpec((1, 1, kept), group_of),
                pl.BlockSpec(memory_space=pltpu.VMEM),
            ],
            out_specs=[pl.BlockSpec((capacity, 2 * width), lambda step, turn_ref: (0, 0))] * groups
            + [pl.BlockSpec(memory_space=pltpu.VMEM)],
            scratch_shapes=[
                pltpu.VMEM((capacity, padded), jnp.float32),
                pltpu.VMEM((capacity, padded), jnp.float32),
            ],
        ),
        out_shape=[jax.ShapeDtypeStruct((capacity, 2 * width), jnp.bfloat16)] * groups
        + [pltpu.VMEM((nodes, padded), jnp.bfloat16)],
        input_output_aliases={6: groups},
        cost_estimate=pl.CostEstimate(
            flops=0, bytes_accessed=groups * capacity * fanout * TILE * padded * 2, transcendentals=0
        ),
        compiler_params=pltpu.CompilerParams(vmem_limit_bytes=14 * 2**20),
        name="gather_layer",
    )(
        turn, enough, order, own_ids, near_ids, counts,
        pltpu.with_memory_space_constraint(table, pltpu.VMEM),
    )


def upper_kernel(fanout, size_ref, turn_ref, weights_ref, layer_ref, row_ref, seed_ref, *rest):
    *inputs_refs, upper_ref, lower_ref = rest
    seed_total = seed_ref.shape[1]
    capacity = inputs_refs[0].shape[0]
    hidden_width = weights_ref.shape[2]
    classes = layer_ref.shape[1]
    size = size_ref[0]
    seed = lax.broadcasted_iota(jnp.int32, (seed_total, capacity), 0)
    row = jnp.broadcast_to(row_ref[...], (seed_total, capacity))
    first = seed_total + seed * fanout
    is_seed = jnp.where(row == seed, 1.0, 0.0).astype(jnp.bfloat16)
    is_near = jnp.where((row >= first) & (row < first + fanout), 1.0, 0.0).astype(jnp.bfloat16)
    preact = jnp.zeros((capacity, hidden_width), jnp.float32)
    for place, inputs_ref in enumerate(inputs_refs):
        source = turn_ref[len(inputs_refs) + place]
        preact = preact + jnp.dot(inputs_ref[...], weights_ref[source], preferred_element_type=jnp.float32)
    hidden = jnp.maximum(preact, 0.0).astype(jnp.bfloat16)
    counts = seed_ref[0][:, :1].astype(jnp.float32)
    last = (((1,), (1,)), ((), ()))
    seed_hidden = jnp.dot(is_seed, hidden, preferred_element_type=jnp.float32).astype(jnp.bfloat16)
    near_mean = (jnp.dot(is_near, hidden, preferred_element_type=jnp.float32) / counts).astype(jnp.bfloat16)
    logits = lax.dot_general(seed_hidden, layer_ref[0], last, preferred_element_type=jnp.float32)
    logits = logits + lax.dot_general(near_mean, layer_ref[1], last, preferred_element_type=jnp.float32)
    exponent = jnp.exp(logits - jnp.max(logits, axis=1, keepdims=True))
    probabilities = exponent / jnp.sum(exponent, axis=1, keepdims=True)
    label = jnp.broadcast_to(seed_ref[1][:, :1], (seed_total, classes))
    onehot = jnp.where(label == lax.broadcasted_iota(jnp.int32, (seed_total, classes), 1), 1.0, 0.0)
    valid = lax.broadcasted_iota(jnp.int32, (seed_total, classes), 0) < size
    dlogits = jnp.where(valid, (probabilities - onehot) / size.astype(jnp.float32), 0.0).astype(jnp.bfloat16)
    back_seed = jnp.dot(dlogits, layer_ref[0], preferred_element_type=jnp.float32)
    back_near = jnp.dot(dlogits, layer_ref[1], preferred_element_type=jnp.float32) / counts
    rows = (((0,), (0,)), ((), ()))
    spread = lax.dot_general(is_seed, back_seed.astype(jnp.bfloat16), rows, preferred_element_type=jnp.float32)
    spread = spread + lax.dot_general(
        is_near, back_near.astype(jnp.bfloat16), rows, preferred_element_type=jnp.float32
    )
    dpreact = jnp.where(preact > 0, spread, 0.0).astype(jnp.bfloat16)
    split = upper_ref.shape[0]
    upper_ref[...] = dpreact[:split]
    lower_ref[: capacity - split] = dpreact[split:]
    units = [seed_hidden, near_mean, jnp.zeros((seed_total, hidden_width), jnp.bfloat16)]
    for part, unit in enumerate(units):
        start = capacity - split + part * seed_total
        lower_ref[start : start + seed_total] = unit
    lower_ref[capacity - split + 2 * seed_total :, :classes] = dlogits


def upper_layers(inputs, size, turn, weights, layer, row, seeds, fanout):
    seed_total = seeds.shape[1]
    capacity = inputs[0].shape[0]
    hidden_width = weights.shape[2]
    total = capacity + 3 * seed_total
    split = round_up(total // 2, 16)
    smem = pl.BlockSpec(memory_space=pltpu.SMEM)
    vmem = pl.BlockSpec(memory_space=pltpu.VMEM)
    return pl.pallas_call(
        functools.partial(upper_kernel, fanout),
        in_specs=[smem] * 2 + [vmem] * (4 + len(inputs)),
        out_specs=[vmem] * 2,
        out_shape=[jax.ShapeDtypeStruct((length, hidden_width), jnp.bfloat16) for length in (split, total - split)],
        compiler_params=pltpu.CompilerParams(vmem_limit_bytes=32 * 2**20),
        name="upper_layers",
    )(size, turn, weights, layer, row, seeds, *inputs)


def grad_kernel(seed_total, classes, source_ref, *rest):
    count = (len(rest) - 2) // 3
    inputs_refs, upper_refs, lower_refs = rest[:count], rest[count : 2 * count], rest[2 * count : 3 * count]
    out_ref, units_ref = rest[3 * count :]
    capacity, double = inputs_refs[0].shape
    hidden_width = out_ref.shape[1]
    split = upper_refs[0].shape[0]
    rows = (((0,), (0,)), ((), ()))
    first = jnp.zeros((double, hidden_width), jnp.float32)
    for place in range(count):
        inputs_ref, upper_ref, lower_ref = inputs_refs[place], upper_refs[place], lower_refs[place]
        first = first + lax.dot_general(
            inputs_ref[:split], upper_ref[...], rows, preferred_element_type=jnp.float32
        )
        first = first + lax.dot_general(
            inputs_ref[split:], lower_ref[: capacity - split], rows, preferred_element_type=jnp.float32
        )
        start = pl.multiple_of(source_ref[place] * seed_total, seed_total)
        for part in range(3):
            begin = capacity - split + part * seed_total
            units_ref[part, pl.ds(start, seed_total), :] = lower_ref[begin : begin + seed_total]
    out_ref[:double] = first
    for layer in range(2):
        second = lax.dot_general(units_ref[2], units_ref[layer], rows, preferred_element_type=jnp.float32)
        start = double + layer * round_up(classes, 8)
        out_ref[start : start + round_up(classes, 8)] = second[: round_up(classes, 8)]


def grad_layer(inputs, upper, lower, sources, seed_total, classes):
    capacity, double = inputs[0].shape
    hidden_width = upper[0].shape[1]
    vmem = pl.BlockSpec(memory_space=pltpu.VMEM)
    return pl.pallas_call(
        functools.partial(grad_kernel, seed_total, classes),
        in_specs=[pl.BlockSpec(memory_space=pltpu.SMEM)] + [vmem] * (3 * len(inputs)),
        out_specs=vmem,
        out_shape=jax.ShapeDtypeStruct((double + 2 * round_up(classes, 8), hidden_width), jnp.float32),
        scratch_shapes=[pltpu.VMEM((3, len(inputs) * seed_total, hidden_width), jnp.bfloat16)],
        compiler_params=pltpu.CompilerParams(vmem_limit_bytes=40 * 2**20),
        name="grad_layer",
    )(sources, *inputs, *upper, *lower)


def final_kernel(mine_ref, other_ref, first_ref, second_ref):
    width = first_ref.shape[1]
    classes = second_ref.shape[0]
    total = mine_ref[...].astype(jnp.float32) + other_ref[...].astype(jnp.float32)
    for layer in range(2):
        first_ref[layer] = total[layer * width : (layer + 1) * width]
        start = 2 * width + layer * round_up(classes, 8)
        second_ref[:, layer, :] = total[start : start + classes]


def final_sum(mine, other, width, classes):
    hidden_width = mine.shape[1]
    first, second = pl.pallas_call(
        final_kernel,
        out_shape=[
            jax.ShapeDtypeStruct((2, width, hidden_width), jnp.float32),
            jax.ShapeDtypeStruct((classes, 2, hidden_width), jnp.float32),
        ],
        name="final_sum",
    )(mine, other)
    return first, jnp.transpose(second, (1, 2, 0))


def ring_of(count):
    if count % 2:
        return list(range(count))
    return list(range(0, count, 2)) + list(range(count - 1, 0, -2))


def send_along(array, ring, shift):
    count = len(ring)
    return lax.ppermute(array, "feat", [(ring[i], ring[(i + shift) % count]) for i in range(count)])


def ring_gather(upper, lower, ring):
    count = len(ring)
    halves = [[half] + [None] * (count - 1) for half in (upper, lower)]
    moving = [[half, half] for half in (upper, lower)]
    for hop in range(1, count // 2 + 1):
        for half in range(2):
            for way, sign in enumerate((1, -1)):
                if 2 * hop < count or half == way:
                    moving[half][way] = send_along(moving[half][way], ring, sign)
                    halves[half][-sign * hop % count] = moving[half][way]
    return halves


def group_sum(grads, width, classes):
    count = lax.axis_size("dp")
    mine = grads
    stride = 1
    while 2 * stride < count:
        mine = mine + lax.ppermute(mine, "dp", [(i, i ^ stride) for i in range(count)])
        stride *= 2
    mine = mine.astype(jnp.bfloat16)
    if count > 1:
        other = lax.ppermute(mine, "dp", [(i, i ^ stride) for i in range(count)])
    else:
        other = jnp.zeros_like(mine)
    return final_sum(mine, other, width, classes)


def shards(
    node_feats,
    first_layer,
    second_layer,
    seed_ids,
    hop1_ids,
    hop1_count,
    hop2_ids,
    hop2_count,
    batch_sizes,
    label_ids,
):
    groups, seed_total = seed_ids.shape
    row_total = hop2_count.shape[1]
    fanout = hop1_ids.shape[1] // seed_total
    slice_width = node_feats.shape[0]
    hidden_width = first_layer.shape[2]
    classes = second_layer.shape[2]
    capacity = round_up(seed_total + row_total // 2, 16)
    kept = round_up(capacity, LANES)
    column_rank = lax.axis_index("feat")
    group_start = lax.axis_index("dp") * groups
    sizes = lax.dynamic_slice_in_dim(batch_sizes, group_start, groups)
    order, enough = plan_rows(hop1_count, hop2_count, sizes, kept)
    count = lax.axis_size("feat")
    ring = ring_of(count)
    places = sorted(range(count), key=lambda t: -min(t, count - t))
    turns = [
        [ring[(ring.index(i) + sign * t) % count] for sign in (1, -1) for t in places] for i in range(count)
    ]
    turn = lax.dynamic_index_in_dim(jnp.array(turns, jnp.int32), column_rank, 0, keepdims=False)
    weights = lax.all_gather(first_layer.reshape(2 * slice_width, hidden_width), "feat", axis=0)
    lists = [
        enough[:, None, :],
        order[:, None, :],
        jnp.maximum(order % 16, 1).astype(jnp.float32)[:, None, :],
        jnp.concatenate([seed_ids, hop1_ids], axis=1)[:, None, :],
        hop2_ids[:, None, :],
    ]
    node_feats, turn, *lists = lax.optimization_barrier((node_feats, turn, *lists))
    table = build_table(node_feats)
    inputs, received, arrived = [], [], []
    for call in range(CALLS):
        begin, end = -(-call * count // CALLS), -(-(call + 1) * count // CALLS)
        *blocks, table = gather_layer(table, turn, begin, end, *lists, slice_width, capacity)
        if call < CALLS - 1:
            table, blocks, arrived = lax.optimization_barrier((table, blocks, arrived))
        else:
            blocks, arrived, order, hop1_count, label_ids, sizes, second_layer = lax.optimization_barrier(
                (blocks, arrived, order, hop1_count, label_ids, sizes, second_layer)
            )
        inputs += blocks
        received += arrived
        arrived = [send_along(block, ring, t) if t else block for t, block in zip(places[begin:end], blocks)]
    received += arrived

    def own(array):
        return lax.dynamic_index_in_dim(array, column_rank, 0, keepdims=False)

    own_order = own(order)[None, :capacity]
    row = jnp.where(own_order % 16 > 0, own_order // 16, -1)
    seeds = jnp.stack([own(hop1_count), own(label_ids)])
    seeds = jnp.broadcast_to(seeds[:, :, None], (2, seed_total, LANES))
    size = lax.dynamic_slice_in_dim(sizes, column_rank, 1)
    layer = jnp.transpose(second_layer, (0, 2, 1))
    halves = upper_layers(received, size, turn, weights, layer, row, seeds, fanout)
    upper, lower = ring_gather(*halves, ring)
    grads = grad_layer(
        inputs, [upper[t] for t in places], [lower[t] for t in places], turn, seed_total, classes
    )
    return tuple(group_sum(grads, slice_width, classes))


def solution(mesh):
    return jax.shard_map(
        shards,
        mesh=mesh,
        in_specs=(
            P("feat", None),
            P(None, "feat", None),
            P(),
            P("dp", None),
            P("dp", None),
            P("dp", None),
            P("dp", None),
            P("dp", None),
            P(),
            P("dp", None),
        ),
        out_specs=(P(None, "feat", None), P()),
        check_vma=False,
    )
```

```python
import functools

import jax
import jax.numpy as jnp
from jax import lax
from jax.experimental import pallas as pl
from jax.experimental.pallas import tpu as pltpu
from jax.sharding import PartitionSpec as P

LANES = 128
TILE = 16
TILE_BITS = 4
CALLS = 3
BLOCK = 256


def round_up(value, step):
    return (value + step - 1) // step * step


def plan_rows(seed_total, fanout, size, hop1_row, hop2_row, lower_ref, equal_ref):
    row_total = hop2_row.shape[1]
    kept = round_up(capacity_of(seed_total, row_total), LANES)

    def flags(condition):
        return jnp.where(condition, 1.0, 0.0).astype(jnp.bfloat16)

    def iota(shape, dim):
        return lax.broadcasted_iota(jnp.int32, shape, dim)

    def product(one, two):
        return jnp.dot(one, two, preferred_element_type=jnp.float32)

    def spread(row):
        return jnp.broadcast_to(row, (row_total, row.shape[1]))

    ones = jnp.ones((row_total, LANES), jnp.bfloat16)
    count = product(equal_ref[...] * spread(hop2_row.astype(jnp.float32).astype(jnp.bfloat16)), ones)
    shape = (row_total, seed_total)
    seed, row = iota(shape, 1), iota(shape, 0)
    first = seed_total + seed * fanout
    live = seed < size
    last = first + jnp.where(live, spread(hop1_row), 0)
    used = ((row >= first) & (row < last)) | ((row == seed) & live)
    key = count * product(flags(used), ones[:seed_total])
    rank = iota(key.shape, 1).astype(jnp.float32)
    mine = key == rank
    before = product(lower_ref[...], flags(mine))
    above = product(jnp.ones((16, row_total), jnp.bfloat16), flags(key > rank))
    enough = product(jnp.ones((16, row_total), jnp.bfloat16), flags(key >= rank))
    place = jnp.sum(jnp.where(mine, before + spread(above[:1]), 0.0), axis=1, keepdims=True)
    there = jnp.broadcast_to(place, (row_total, kept)) == iota((row_total, kept), 1).astype(jnp.float32)
    number = iota((16, row_total), 1)
    high = product((number >> 5).astype(jnp.float32).astype(jnp.bfloat16), flags(there))
    low = product((number & 31).astype(jnp.float32).astype(jnp.bfloat16), flags(there))
    held = product(
        jnp.ones((16, row_total), jnp.bfloat16),
        jnp.where(there, jnp.broadcast_to(key[:, :1], there.shape), 0.0).astype(jnp.bfloat16),
    )
    order = (high * 32 + low) * 16 + held
    return order[:1].astype(jnp.int32), jnp.maximum(held[:1], 1.0), enough[:1].astype(jnp.int32)


def capacity_of(seed_total, row_total):
    return round_up(seed_total + row_total // 2, 16)


def table_kernel(steps, seed_total, fanout, turn_ref, size_ref, hop1_ref, hop2_ref, *refs):
    *feats_refs, table_ref, order_ref, count_ref, enough_ref, lower_ref, equal_ref = refs
    step = pl.program_id(0)
    chunk = feats_refs[0].shape[1]
    width = sum(ref.shape[0] for ref in feats_refs)
    padded = table_ref.shape[1]
    down = lax.broadcasted_iota(jnp.int32, (BLOCK, BLOCK), 0)
    across = lax.broadcasted_iota(jnp.int32, (BLOCK, BLOCK), 1)
    identity = jnp.where(down == across, 1.0, 0.0).astype(jnp.bfloat16)
    filler = jnp.zeros((padded - width, BLOCK), jnp.bfloat16)

    def turn_features():
        for part in range(0, chunk // BLOCK, 2):
            pieces = []
            for at in (part * BLOCK, (part + 1) * BLOCK):
                pieces += [feats_ref[:, at : at + BLOCK] for feats_ref in feats_refs]
                if padded > width:
                    pieces.append(filler)
            both = jnp.concatenate(pieces, axis=0)
            if part % 4:
                turned = jnp.transpose(both)
            else:
                turned = lax.dot_general(
                    identity, both, (((1,), (1,)), ((), ())), preferred_element_type=jnp.float32
                ).astype(jnp.bfloat16)
            for side in range(2):
                start = pl.multiple_of(step * chunk + (part + side) * BLOCK, BLOCK)
                table_ref[pl.ds(start, BLOCK), :] = turned[:, side * padded : (side + 1) * padded]

    @pl.when(step == 0)
    def _():
        shape = lower_ref.shape
        below = lax.broadcasted_iota(jnp.int32, shape, 1) - lax.broadcasted_iota(jnp.int32, shape, 0)
        lower_ref[...] = jnp.where(below < 0, 1.0, 0.0).astype(jnp.bfloat16)
        equal_ref[...] = jnp.where(below == 0, 1.0, 0.0).astype(jnp.bfloat16)

    @pl.when(lax.rem(step, steps) == 0)
    def _():
        size = size_ref[turn_ref[0] + lax.div(step, steps)]
        order_ref[0], count_ref[0], enough_ref[0] = plan_rows(
            seed_total, fanout, size, hop1_ref[0], hop2_ref[0], lower_ref, equal_ref
        )
        turn_features()

    @pl.when(lax.rem(step, steps) != 0)
    def _():
        turn_features()


def build_table(node_feats, turn, batch_sizes, hop1_count, hop2_count, fanout):
    width, nodes = node_feats.shape
    groups, seed_total = hop1_count.shape
    row_total = hop2_count.shape[1]
    kept = round_up(capacity_of(seed_total, row_total), LANES)
    padded = max(width, LANES)
    steps = 2 if groups < 16 else 1
    chunk = nodes // (groups * steps)
    streams = max(1, width // 32)
    smem = pl.BlockSpec(memory_space=pltpu.SMEM)

    def per_group(length):
        return pl.BlockSpec((1, 1, length), lambda step: (lax.div(step, steps), 0, 0))

    return pl.pallas_call(
        functools.partial(table_kernel, steps, seed_total, fanout),
        grid=(groups * steps,),
        in_specs=[smem, smem, per_group(seed_total), per_group(row_total)]
        + [pl.BlockSpec((width // streams, chunk), lambda step, at=at: (at, step)) for at in range(streams)],
        out_specs=[pl.BlockSpec(memory_space=pltpu.VMEM), per_group(kept), per_group(kept), per_group(LANES)],
        out_shape=[
            pltpu.VMEM((nodes, padded), jnp.bfloat16),
            pltpu.HBM((groups, 1, kept), jnp.int32),
            pltpu.HBM((groups, 1, kept), jnp.float32),
            pltpu.HBM((groups, 1, LANES), jnp.int32),
        ],
        scratch_shapes=[pltpu.VMEM((row_total, row_total), jnp.bfloat16)] * 2,
        compiler_params=pltpu.CompilerParams(vmem_limit_bytes=12 * 2**20),
        name="build_table",
    )(turn, batch_sizes, hop1_count[:, None, :], hop2_count[:, None, :], *[node_feats] * streams)


def gather_kernel(
    fanout, capacity, turn_ref, enough_ref, order_ref, own_ref, near_ref, count_ref, table_ref, *rest
):
    *inputs_refs, _, own_sum_ref, near_sum_ref = rest
    step = pl.program_id(0)
    width = inputs_refs[0].shape[1] // 2
    padded = table_ref.shape[1]

    tiles = table_ref.reshape(table_ref.shape[0] // TILE, TILE, padded)
    half = TILE // 2
    low = lax.broadcasted_iota(jnp.int32, (half, padded), 0)
    high = low + half

    def fetch(node, wanted=None):
        tile = tiles[node >> TILE_BITS].astype(jnp.float32)
        if wanted is None:
            line = jnp.full((half, padded), node, jnp.int32) & (TILE - 1)
        else:
            line = jnp.full((half, padded), jnp.where(wanted, node & (TILE - 1), TILE), jnp.int32)
        return jnp.where(line == low, tile[:half], jnp.where(line == high, tile[half:], 0.0))

    def add_lines(values):
        step = 1
        while step < half:
            chosen = (low & step) == 0
            values = [
                jnp.where(chosen, one, two) + pltpu.roll(jnp.where(chosen, two, one), half - step, 0)
                for one, two in zip(values[::2], values[1::2])
            ]
            step *= 2
        return values[0]

    def gather_rows(slots, exact, number, carry):
        first = pl.multiple_of(number * half, half)
        entries = [order_ref[0, 0, first + i] for i in range(half)]
        rows = [entry >> 4 for entry in entries]
        starts = [row * fanout for row in rows]

        def near(i, slot):
            node = near_ref[0, 0, starts[i] + slot]
            return fetch(node) if exact else fetch(node, slot < (entries[i] & 15))

        own_sum_ref[pl.ds(first, half), :] = add_lines([fetch(own_ref[0, 0, row]) for row in rows])
        nears = [near(i, 0) for i in range(half)]
        for slot in range(1, slots):
            nears = [nears[i] + near(i, slot) for i in range(half)]
        near_sum_ref[pl.ds(first, half), :] = add_lines(nears)
        return carry

    start = 0
    for slots in range(fanout, 0, -1):
        end = enough_ref[0, 0, slots]
        whole = jnp.maximum(lax.div(end, half), start)
        stop = lax.div(end + half - 1, half)
        lax.fori_loop(start, whole, functools.partial(gather_rows, slots, True), 0)
        lax.fori_loop(whole, stop, functools.partial(gather_rows, slots, False), 0)
        start = stop

    def clear(number, carry):
        first = pl.multiple_of(number * half, half)
        own_sum_ref[pl.ds(first, half), :] = jnp.zeros((half, padded), jnp.float32)
        near_sum_ref[pl.ds(first, half), :] = jnp.zeros((half, padded), jnp.float32)
        return carry

    lax.fori_loop(start, capacity // half, clear, 0)
    counts = jnp.transpose(jnp.broadcast_to(count_ref[0], (padded, count_ref.shape[2])))[:capacity]
    own = own_sum_ref[...].astype(jnp.bfloat16)[:, :width]
    near = (near_sum_ref[...] / counts).astype(jnp.bfloat16)[:, :width]
    both = jnp.concatenate([own, near], axis=1)
    for place, inputs_ref in enumerate(inputs_refs):

        @pl.when(step == place)
        def _():
            inputs_ref[...] = both


def gather_layer(table, turn, begin, end, enough, order, counts, own_ids, near_ids, width, capacity):
    nodes, padded = table.shape
    groups = end - begin
    kept = order.shape[2]
    row_total = own_ids.shape[2]
    fanout = near_ids.shape[2] // row_total

    def group_of(step, turn_ref):
        return (turn_ref[2 + begin + step], 0, 0)

    def per_group(length):
        return pl.BlockSpec((1, 1, length), group_of, memory_space=pltpu.SMEM)

    return pl.pallas_call(
        functools.partial(gather_kernel, fanout, capacity),
        grid_spec=pltpu.PrefetchScalarGridSpec(
            num_scalar_prefetch=1,
            grid=(groups,),
            in_specs=[
                per_group(LANES),
                per_group(kept),
                per_group(row_total),
                per_group(row_total * fanout),
                pl.BlockSpec((1, 1, kept), group_of),
                pl.BlockSpec(memory_space=pltpu.VMEM),
            ],
            out_specs=[pl.BlockSpec((capacity, 2 * width), lambda step, turn_ref: (0, 0))] * groups
            + [pl.BlockSpec(memory_space=pltpu.VMEM)],
            scratch_shapes=[
                pltpu.VMEM((capacity, padded), jnp.float32),
                pltpu.VMEM((capacity, padded), jnp.float32),
            ],
        ),
        out_shape=[jax.ShapeDtypeStruct((capacity, 2 * width), jnp.bfloat16)] * groups
        + [pltpu.VMEM((nodes, padded), jnp.bfloat16)],
        input_output_aliases={6: groups},
        cost_estimate=pl.CostEstimate(
            flops=0, bytes_accessed=groups * capacity * fanout * TILE * padded * 2, transcendentals=0
        ),
        compiler_params=pltpu.CompilerParams(vmem_limit_bytes=14 * 2**20),
        name="gather_layer",
    )(
        turn, enough, order, own_ids, near_ids, counts,
        pltpu.with_memory_space_constraint(table, pltpu.VMEM),
    )


def upper_kernel(fanout, size_ref, turn_ref, weights_ref, layer_ref, row_ref, seed_ref, *rest):
    *inputs_refs, upper_ref, lower_ref = rest
    seed_total = seed_ref.shape[1]
    capacity = inputs_refs[0].shape[0]
    hidden_width = weights_ref.shape[2]
    classes = layer_ref.shape[1]
    size = size_ref[turn_ref[1]]
    seed = lax.broadcasted_iota(jnp.int32, (seed_total, capacity), 0)
    row = jnp.broadcast_to(row_ref[...], (seed_total, capacity))
    first = seed_total + seed * fanout
    is_seed = jnp.where(row == seed, 1.0, 0.0).astype(jnp.bfloat16)
    is_near = jnp.where((row >= first) & (row < first + fanout), 1.0, 0.0).astype(jnp.bfloat16)
    preact = jnp.zeros((capacity, hidden_width), jnp.float32)
    for place, inputs_ref in enumerate(inputs_refs):
        source = turn_ref[2 + len(inputs_refs) + place]
        preact = preact + jnp.dot(inputs_ref[...], weights_ref[source], preferred_element_type=jnp.float32)
    hidden = jnp.maximum(preact, 0.0).astype(jnp.bfloat16)
    counts = seed_ref[0][:, :1].astype(jnp.float32)
    last = (((1,), (1,)), ((), ()))
    seed_hidden = jnp.dot(is_seed, hidden, preferred_element_type=jnp.float32).astype(jnp.bfloat16)
    near_mean = (jnp.dot(is_near, hidden, preferred_element_type=jnp.float32) / counts).astype(jnp.bfloat16)
    logits = lax.dot_general(seed_hidden, layer_ref[0], last, preferred_element_type=jnp.float32)
    logits = logits + lax.dot_general(near_mean, layer_ref[1], last, preferred_element_type=jnp.float32)
    exponent = jnp.exp(logits - jnp.max(logits, axis=1, keepdims=True))
    probabilities = exponent / jnp.sum(exponent, axis=1, keepdims=True)
    label = jnp.broadcast_to(seed_ref[1][:, :1], (seed_total, classes))
    onehot = jnp.where(label == lax.broadcasted_iota(jnp.int32, (seed_total, classes), 1), 1.0, 0.0)
    valid = lax.broadcasted_iota(jnp.int32, (seed_total, classes), 0) < size
    dlogits = jnp.where(valid, (probabilities - onehot) / size.astype(jnp.float32), 0.0).astype(jnp.bfloat16)
    back_seed = jnp.dot(dlogits, layer_ref[0], preferred_element_type=jnp.float32)
    back_near = jnp.dot(dlogits, layer_ref[1], preferred_element_type=jnp.float32) / counts
    rows = (((0,), (0,)), ((), ()))
    spread = lax.dot_general(is_seed, back_seed.astype(jnp.bfloat16), rows, preferred_element_type=jnp.float32)
    spread = spread + lax.dot_general(
        is_near, back_near.astype(jnp.bfloat16), rows, preferred_element_type=jnp.float32
    )
    dpreact = jnp.where(preact > 0, spread, 0.0).astype(jnp.bfloat16)
    split = upper_ref.shape[0]
    upper_ref[...] = dpreact[:split]
    lower_ref[: capacity - split] = dpreact[split:]
    units = [seed_hidden, near_mean, jnp.zeros((seed_total, hidden_width), jnp.bfloat16)]
    for part, unit in enumerate(units):
        start = capacity - split + part * seed_total
        lower_ref[start : start + seed_total] = unit
    lower_ref[capacity - split + 2 * seed_total :, :classes] = dlogits


def upper_layers(inputs, sizes, turn, weights, layer, row, seeds, fanout):
    seed_total = seeds.shape[1]
    capacity = inputs[0].shape[0]
    hidden_width = weights.shape[2]
    total = capacity + 3 * seed_total
    split = round_up(total // 2, 16)
    smem = pl.BlockSpec(memory_space=pltpu.SMEM)
    vmem = pl.BlockSpec(memory_space=pltpu.VMEM)
    return pl.pallas_call(
        functools.partial(upper_kernel, fanout),
        in_specs=[smem] * 2 + [vmem] * (4 + len(inputs)),
        out_specs=[vmem] * 2,
        out_shape=[jax.ShapeDtypeStruct((length, hidden_width), jnp.bfloat16) for length in (split, total - split)],
        compiler_params=pltpu.CompilerParams(vmem_limit_bytes=32 * 2**20),
        name="upper_layers",
    )(sizes, turn, weights, layer, row, seeds, *inputs)


def grad_kernel(seed_total, classes, source_ref, *rest):
    count = (len(rest) - 2) // 3
    inputs_refs, upper_refs, lower_refs = rest[:count], rest[count : 2 * count], rest[2 * count : 3 * count]
    out_ref, units_ref = rest[3 * count :]
    capacity, double = inputs_refs[0].shape
    hidden_width = out_ref.shape[1]
    split = upper_refs[0].shape[0]
    rows = (((0,), (0,)), ((), ()))
    first = jnp.zeros((double, hidden_width), jnp.float32)
    for place in range(count):
        inputs_ref, upper_ref, lower_ref = inputs_refs[place], upper_refs[place], lower_refs[place]
        first = first + lax.dot_general(
            inputs_ref[:split], upper_ref[...], rows, preferred_element_type=jnp.float32
        )
        first = first + lax.dot_general(
            inputs_ref[split:], lower_ref[: capacity - split], rows, preferred_element_type=jnp.float32
        )
        start = pl.multiple_of(source_ref[2 + place] * seed_total, seed_total)
        for part in range(3):
            begin = capacity - split + part * seed_total
            units_ref[part, pl.ds(start, seed_total), :] = lower_ref[begin : begin + seed_total]
    out_ref[:double] = first
    for layer in range(2):
        second = lax.dot_general(units_ref[2], units_ref[layer], rows, preferred_element_type=jnp.float32)
        start = double + layer * round_up(classes, 8)
        out_ref[start : start + round_up(classes, 8)] = second[: round_up(classes, 8)]


def grad_layer(inputs, upper, lower, sources, seed_total, classes):
    capacity, double = inputs[0].shape
    hidden_width = upper[0].shape[1]
    vmem = pl.BlockSpec(memory_space=pltpu.VMEM)
    return pl.pallas_call(
        functools.partial(grad_kernel, seed_total, classes),
        in_specs=[pl.BlockSpec(memory_space=pltpu.SMEM)] + [vmem] * (3 * len(inputs)),
        out_specs=vmem,
        out_shape=jax.ShapeDtypeStruct((double + 2 * round_up(classes, 8), hidden_width), jnp.float32),
        scratch_shapes=[pltpu.VMEM((3, len(inputs) * seed_total, hidden_width), jnp.bfloat16)],
        compiler_params=pltpu.CompilerParams(vmem_limit_bytes=40 * 2**20),
        name="grad_layer",
    )(sources, *inputs, *upper, *lower)


def final_kernel(mine_ref, other_ref, first_ref, second_ref):
    width = first_ref.shape[1]
    classes = second_ref.shape[0]
    total = mine_ref[...].astype(jnp.float32) + other_ref[...].astype(jnp.float32)
    for layer in range(2):
        first_ref[layer] = total[layer * width : (layer + 1) * width]
        start = 2 * width + layer * round_up(classes, 8)
        second_ref[:, layer, :] = total[start : start + classes]


def final_sum(mine, other, width, classes):
    hidden_width = mine.shape[1]
    first, second = pl.pallas_call(
        final_kernel,
        in_specs=[pl.BlockSpec(memory_space=pltpu.VMEM)] * 2,
        out_shape=[
            jax.ShapeDtypeStruct((2, width, hidden_width), jnp.float32),
            jax.ShapeDtypeStruct((classes, 2, hidden_width), jnp.float32),
        ],
        name="final_sum",
    )(mine, other)
    return first, jnp.transpose(second, (1, 2, 0))


def ring_of(count):
    if count % 2:
        return list(range(count))
    return list(range(0, count, 2)) + list(range(count - 1, 0, -2))


def send_along(array, ring, shift):
    count = len(ring)
    return lax.ppermute(array, "feat", [(ring[i], ring[(i + shift) % count]) for i in range(count)])


def ring_gather(upper, lower, ring):
    count = len(ring)
    halves = [[half] + [None] * (count - 1) for half in (upper, lower)]
    moving = [[half, half] for half in (upper, lower)]
    for hop in range(1, count // 2 + 1):
        for half in range(2):
            for way, sign in enumerate((1, -1)):
                if 2 * hop < count or half == way:
                    moving[half][way] = send_along(moving[half][way], ring, sign)
                    halves[half][-sign * hop % count] = moving[half][way]
    return halves


def group_sum(grads, width, classes):
    count = lax.axis_size("dp")
    mine = grads
    stride = 1
    while 2 * stride < count:
        mine = mine + lax.ppermute(mine, "dp", [(i, i ^ stride) for i in range(count)])
        stride *= 2
    mine = mine.astype(jnp.bfloat16)
    if count > 1:
        other = lax.ppermute(mine, "dp", [(i, i ^ stride) for i in range(count)])
    else:
        other = jnp.zeros_like(mine)
    return final_sum(mine, other, width, classes)


def shards(
    node_feats,
    first_layer,
    second_layer,
    seed_ids,
    hop1_ids,
    hop1_count,
    hop2_ids,
    hop2_count,
    batch_sizes,
    label_ids,
):
    groups, seed_total = seed_ids.shape
    row_total = hop2_count.shape[1]
    fanout = hop1_ids.shape[1] // seed_total
    slice_width = node_feats.shape[0]
    hidden_width = first_layer.shape[2]
    classes = second_layer.shape[2]
    capacity = capacity_of(seed_total, row_total)
    column_rank = lax.axis_index("feat")
    group_start = lax.axis_index("dp") * groups
    count = lax.axis_size("feat")
    ring = ring_of(count)
    places = sorted(range(count), key=lambda t: -min(t, count - t))
    turns = [
        [ring[(ring.index(i) + sign * t) % count] for sign in (1, -1) for t in places] for i in range(count)
    ]
    turn = lax.dynamic_index_in_dim(jnp.array(turns, jnp.int32), column_rank, 0, keepdims=False)
    turn = jnp.concatenate([jnp.stack([group_start, group_start + column_rank]), turn])
    weights = lax.all_gather(first_layer.reshape(2 * slice_width, hidden_width), "feat", axis=0)
    lists = [jnp.concatenate([seed_ids, hop1_ids], axis=1)[:, None, :], hop2_ids[:, None, :]]
    node_feats, turn, *lists = lax.optimization_barrier((node_feats, turn, *lists))
    table, order, counts, enough = build_table(node_feats, turn, batch_sizes, hop1_count, hop2_count, fanout)
    lists = [enough, order, counts, *lists]
    inputs, received, arrived = [], [], []
    for call in range(CALLS):
        begin, end = -(-call * count // CALLS), -(-(call + 1) * count // CALLS)
        *blocks, table = gather_layer(table, turn, begin, end, *lists, slice_width, capacity)
        if call < CALLS - 1:
            table, blocks, arrived = lax.optimization_barrier((table, blocks, arrived))
        else:
            blocks, arrived, order, hop1_count, label_ids, second_layer, weights = lax.optimization_barrier(
                (blocks, arrived, order, hop1_count, label_ids, second_layer, weights)
            )
        inputs += blocks
        received += arrived
        arrived = [send_along(block, ring, t) if t else block for t, block in zip(places[begin:end], blocks)]
    received += arrived

    def own(array):
        return lax.dynamic_index_in_dim(array, column_rank, 0, keepdims=False)

    own_order = own(order)[:, :capacity]
    row = jnp.where(own_order % 16 > 0, own_order // 16, -1)
    seeds = jnp.stack([own(hop1_count), own(label_ids)])
    seeds = jnp.broadcast_to(seeds[:, :, None], (2, seed_total, LANES))
    layer = jnp.transpose(second_layer, (0, 2, 1))
    halves = upper_layers(received, batch_sizes, turn, weights, layer, row, seeds, fanout)
    upper, lower = ring_gather(*halves, ring)
    grads = grad_layer(
        inputs, [upper[t] for t in places], [lower[t] for t in places], turn, seed_total, classes
    )
    return tuple(group_sum(grads, slice_width, classes))


def solution(mesh):
    return jax.shard_map(
        shards,
        mesh=mesh,
        in_specs=(
            P("feat", None),
            P(None, "feat", None),
            P(),
            P("dp", None),
            P("dp", None),
            P("dp", None),
            P("dp", None),
            P("dp", None),
            P(),
            P("dp", None),
        ),
        out_specs=(P(None, "feat", None), P()),
        check_vma=False,
    )
```

```python
import functools

import jax
import jax.numpy as jnp
from jax import lax
from jax.experimental import pallas as pl
from jax.experimental.pallas import tpu as pltpu
from jax.sharding import PartitionSpec as P

LANES = 128
TILE = 16
TILE_BITS = 4
CALLS = 3
BLOCK = 256


def round_up(value, step):
    return (value + step - 1) // step * step


def plan_rows(hop1_count, hop2_count, sizes, kept):
    groups, seed_total = hop1_count.shape
    row_total = hop2_count.shape[1]
    fanout = (row_total - seed_total) // seed_total
    live = jnp.arange(seed_total)[None, :] < sizes[:, None]
    near = jnp.arange(fanout)[None, None, :] < jnp.where(live, hop1_count, 0)[:, :, None]
    used = jnp.concatenate([live, near.reshape(groups, -1)], axis=1)
    count = jnp.where(used, hop2_count, 0)
    row = jnp.arange(row_total)[None, :]
    mixed = count * row_total + (row_total - 1 - row)
    place = jnp.sum((mixed[:, None, :] > mixed[:, :, None]).astype(jnp.int32), axis=2)
    packed = row * 16 + count
    order = jnp.sum(
        jnp.where(place[:, None, :] == jnp.arange(kept)[None, :, None], packed[:, None, :], 0), axis=2
    )
    enough = jnp.sum(
        (count[:, None, :] >= jnp.arange(16)[None, :, None]).astype(jnp.int32), axis=2
    )
    return order, enough


def table_kernel(*refs):
    *feats_refs, table_ref = refs
    step = pl.program_id(0)
    chunk = feats_refs[0].shape[1]
    width = sum(ref.shape[0] for ref in feats_refs)
    padded = table_ref.shape[1]
    down = lax.broadcasted_iota(jnp.int32, (BLOCK, BLOCK), 0)
    across = lax.broadcasted_iota(jnp.int32, (BLOCK, BLOCK), 1)
    identity = jnp.where(down == across, 1.0, 0.0).astype(jnp.bfloat16)
    filler = jnp.zeros((padded - width, BLOCK), jnp.bfloat16)
    for part in range(0, chunk // BLOCK, 2):
        pieces = []
        for at in (part * BLOCK, (part + 1) * BLOCK):
            pieces += [feats_ref[:, at : at + BLOCK] for feats_ref in feats_refs]
            if padded > width:
                pieces.append(filler)
        both = jnp.concatenate(pieces, axis=0)
        if part % 4:
            turned = jnp.transpose(both)
        else:
            turned = lax.dot_general(
                identity, both, (((1,), (1,)), ((), ())), preferred_element_type=jnp.float32
            ).astype(jnp.bfloat16)
        for side in range(2):
            start = pl.multiple_of(step * chunk + (part + side) * BLOCK, BLOCK)
            table_ref[pl.ds(start, BLOCK), :] = turned[:, side * padded : (side + 1) * padded]


def build_table(node_feats):
    width, nodes = node_feats.shape
    padded = max(width, LANES)
    chunk = min(nodes, 8192)
    streams = max(1, width // 32)
    return pl.pallas_call(
        table_kernel,
        grid=(nodes // chunk,),
        in_specs=[pl.BlockSpec((width // streams, chunk), lambda step, at=at: (at, step)) for at in range(streams)],
        out_specs=pl.BlockSpec(memory_space=pltpu.VMEM),
        out_shape=pltpu.VMEM((nodes, padded), jnp.bfloat16),
        compiler_params=pltpu.CompilerParams(vmem_limit_bytes=8 * 2**20),
        name="build_table",
    )(*[node_feats] * streams)


def gather_kernel(
    fanout, capacity, turn_ref, enough_ref, order_ref, own_ref, near_ref, count_ref, table_ref, *rest
):
    *inputs_refs, _, own_sum_ref, near_sum_ref = rest
    step = pl.program_id(0)
    width = inputs_refs[0].shape[1] // 2
    padded = table_ref.shape[1]

    tiles = table_ref.reshape(table_ref.shape[0] // TILE, TILE, padded)
    half = TILE // 2
    span = half * TILE
    line = lax.broadcasted_iota(jnp.int32, (half, span), 0)
    place = lax.broadcasted_iota(jnp.int32, (half, span), 1)
    choice = jnp.where(line == (place >> TILE_BITS), place & (TILE - 1), -1)

    def picks(nodes, wanted=None):
        if wanted is not None:
            nodes = [jnp.where(want, node & (TILE - 1), TILE) for node, want in zip(nodes, wanted)]
        value = jnp.full((half, span), nodes[0], jnp.int32)
        for i in range(1, half):
            value = jnp.where(line == i, nodes[i], value)
        if wanted is None:
            value = value & (TILE - 1)
        return jnp.where(value == choice, 1.0, 0.0).astype(jnp.bfloat16)

    def fetch(lists, wanted=None):
        left = [picks(nodes, wanted[at] if wanted else None) for at, nodes in enumerate(lists)]
        right = [tiles[node >> TILE_BITS] for nodes in lists for node in nodes]
        return jnp.dot(
            jnp.concatenate(left, axis=1), jnp.concatenate(right, axis=0), preferred_element_type=jnp.float32
        )

    def gather_rows(slots, exact, number, carry):
        first = pl.multiple_of(number * half, half)
        entries = [order_ref[0, 0, first + i] for i in range(half)]
        rows = [entry >> 4 for entry in entries]
        starts = [row * fanout for row in rows]
        own_sum_ref[pl.ds(first, half), :] = fetch([[own_ref[0, 0, row] for row in rows]])
        total = None
        for slot in range(0, slots, 2):
            pair = range(slot, min(slot + 2, slots))
            lists = [[near_ref[0, 0, start + at] for start in starts] for at in pair]
            wanted = None if exact else [[at < (entry & 15) for entry in entries] for at in pair]
            part = fetch(lists, wanted)
            total = part if total is None else total + part
        near_sum_ref[pl.ds(first, half), :] = total
        return carry

    start = 0
    for slots in range(fanout, 0, -1):
        end = enough_ref[0, 0, slots]
        whole = jnp.maximum(lax.div(end, half), start)
        stop = lax.div(end + half - 1, half)
        lax.fori_loop(start, whole, functools.partial(gather_rows, slots, True), 0)
        lax.fori_loop(whole, stop, functools.partial(gather_rows, slots, False), 0)
        start = stop

    def clear(number, carry):
        first = pl.multiple_of(number * half, half)
        own_sum_ref[pl.ds(first, half), :] = jnp.zeros((half, padded), jnp.float32)
        near_sum_ref[pl.ds(first, half), :] = jnp.zeros((half, padded), jnp.float32)
        return carry

    lax.fori_loop(start, capacity // half, clear, 0)
    counts = jnp.transpose(jnp.broadcast_to(count_ref[0], (padded, count_ref.shape[2])))[:capacity]
    own = own_sum_ref[...].astype(jnp.bfloat16)[:, :width]
    near = (near_sum_ref[...] / counts).astype(jnp.bfloat16)[:, :width]
    both = jnp.concatenate([own, near], axis=1)
    for place, inputs_ref in enumerate(inputs_refs):

        @pl.when(step == place)
        def _():
            inputs_ref[...] = both


def gather_layer(table, turn, begin, end, enough, order, counts, own_ids, near_ids, width, capacity):
    nodes, padded = table.shape
    groups = end - begin
    kept = order.shape[2]
    row_total = own_ids.shape[2]
    fanout = near_ids.shape[2] // row_total

    def group_of(step, turn_ref):
        return (turn_ref[begin + step], 0, 0)

    def per_group(length):
        return pl.BlockSpec((1, 1, length), group_of, memory_space=pltpu.SMEM)

    return pl.pallas_call(
        functools.partial(gather_kernel, fanout, capacity),
        grid_spec=pltpu.PrefetchScalarGridSpec(
            num_scalar_prefetch=1,
            grid=(groups,),
            in_specs=[
                per_group(16),
                per_group(kept),
                per_group(row_total),
                per_group(row_total * fanout),
                pl.BlockSpec((1, 1, kept), group_of),
                pl.BlockSpec(memory_space=pltpu.VMEM),
            ],
            out_specs=[pl.BlockSpec((capacity, 2 * width), lambda step, turn_ref: (0, 0))] * groups
            + [pl.BlockSpec(memory_space=pltpu.VMEM)],
            scratch_shapes=[
                pltpu.VMEM((capacity, padded), jnp.float32),
                pltpu.VMEM((capacity, padded), jnp.float32),
            ],
        ),
        out_shape=[jax.ShapeDtypeStruct((capacity, 2 * width), jnp.bfloat16)] * groups
        + [pltpu.VMEM((nodes, padded), jnp.bfloat16)],
        input_output_aliases={6: groups},
        cost_estimate=pl.CostEstimate(
            flops=0, bytes_accessed=groups * capacity * fanout * TILE * padded * 2, transcendentals=0
        ),
        compiler_params=pltpu.CompilerParams(vmem_limit_bytes=14 * 2**20),
        name="gather_layer",
    )(
        turn, enough, order, own_ids, near_ids, counts,
        pltpu.with_memory_space_constraint(table, pltpu.VMEM),
    )


def upper_kernel(fanout, size_ref, turn_ref, weights_ref, layer_ref, row_ref, seed_ref, *rest):
    *inputs_refs, upper_ref, lower_ref = rest
    seed_total = seed_ref.shape[1]
    capacity = inputs_refs[0].shape[0]
    hidden_width = weights_ref.shape[2]
    classes = layer_ref.shape[1]
    size = size_ref[0]
    seed = lax.broadcasted_iota(jnp.int32, (seed_total, capacity), 0)
    row = jnp.broadcast_to(row_ref[...], (seed_total, capacity))
    first = seed_total + seed * fanout
    is_seed = jnp.where(row == seed, 1.0, 0.0).astype(jnp.bfloat16)
    is_near = jnp.where((row >= first) & (row < first + fanout), 1.0, 0.0).astype(jnp.bfloat16)
    preact = jnp.zeros((capacity, hidden_width), jnp.float32)
    for place, inputs_ref in enumerate(inputs_refs):
        source = turn_ref[len(inputs_refs) + place]
        preact = preact + jnp.dot(inputs_ref[...], weights_ref[source], preferred_element_type=jnp.float32)
    hidden = jnp.maximum(preact, 0.0).astype(jnp.bfloat16)
    counts = seed_ref[0][:, :1].astype(jnp.float32)
    last = (((1,), (1,)), ((), ()))
    seed_hidden = jnp.dot(is_seed, hidden, preferred_element_type=jnp.float32).astype(jnp.bfloat16)
    near_mean = (jnp.dot(is_near, hidden, preferred_element_type=jnp.float32) / counts).astype(jnp.bfloat16)
    logits = lax.dot_general(seed_hidden, layer_ref[0], last, preferred_element_type=jnp.float32)
    logits = logits + lax.dot_general(near_mean, layer_ref[1], last, preferred_element_type=jnp.float32)
    exponent = jnp.exp(logits - jnp.max(logits, axis=1, keepdims=True))
    probabilities = exponent / jnp.sum(exponent, axis=1, keepdims=True)
    label = jnp.broadcast_to(seed_ref[1][:, :1], (seed_total, classes))
    onehot = jnp.where(label == lax.broadcasted_iota(jnp.int32, (seed_total, classes), 1), 1.0, 0.0)
    valid = lax.broadcasted_iota(jnp.int32, (seed_total, classes), 0) < size
    dlogits = jnp.where(valid, (probabilities - onehot) / size.astype(jnp.float32), 0.0).astype(jnp.bfloat16)
    back_seed = jnp.dot(dlogits, layer_ref[0], preferred_element_type=jnp.float32)
    back_near = jnp.dot(dlogits, layer_ref[1], preferred_element_type=jnp.float32) / counts
    rows = (((0,), (0,)), ((), ()))
    spread = lax.dot_general(is_seed, back_seed.astype(jnp.bfloat16), rows, preferred_element_type=jnp.float32)
    spread = spread + lax.dot_general(
        is_near, back_near.astype(jnp.bfloat16), rows, preferred_element_type=jnp.float32
    )
    dpreact = jnp.where(preact > 0, spread, 0.0).astype(jnp.bfloat16)
    split = upper_ref.shape[0]
    upper_ref[...] = dpreact[:split]
    lower_ref[: capacity - split] = dpreact[split:]
    units = [seed_hidden, near_mean, jnp.zeros((seed_total, hidden_width), jnp.bfloat16)]
    for part, unit in enumerate(units):
        start = capacity - split + part * seed_total
        lower_ref[start : start + seed_total] = unit
    lower_ref[capacity - split + 2 * seed_total :, :classes] = dlogits


def upper_layers(inputs, size, turn, weights, layer, row, seeds, fanout):
    seed_total = seeds.shape[1]
    capacity = inputs[0].shape[0]
    hidden_width = weights.shape[2]
    total = capacity + 3 * seed_total
    split = round_up(total // 2, 16)
    smem = pl.BlockSpec(memory_space=pltpu.SMEM)
    vmem = pl.BlockSpec(memory_space=pltpu.VMEM)
    return pl.pallas_call(
        functools.partial(upper_kernel, fanout),
        in_specs=[smem] * 2 + [vmem] * (4 + len(inputs)),
        out_specs=[vmem] * 2,
        out_shape=[jax.ShapeDtypeStruct((length, hidden_width), jnp.bfloat16) for length in (split, total - split)],
        compiler_params=pltpu.CompilerParams(vmem_limit_bytes=32 * 2**20),
        name="upper_layers",
    )(size, turn, weights, layer, row, seeds, *inputs)


def grad_kernel(seed_total, classes, source_ref, *rest):
    count = (len(rest) - 2) // 3
    inputs_refs, upper_refs, lower_refs = rest[:count], rest[count : 2 * count], rest[2 * count : 3 * count]
    out_ref, units_ref = rest[3 * count :]
    capacity, double = inputs_refs[0].shape
    hidden_width = out_ref.shape[1]
    split = upper_refs[0].shape[0]
    rows = (((0,), (0,)), ((), ()))
    first = jnp.zeros((double, hidden_width), jnp.float32)
    for place in range(count):
        inputs_ref, upper_ref, lower_ref = inputs_refs[place], upper_refs[place], lower_refs[place]
        first = first + lax.dot_general(
            inputs_ref[:split], upper_ref[...], rows, preferred_element_type=jnp.float32
        )
        first = first + lax.dot_general(
            inputs_ref[split:], lower_ref[: capacity - split], rows, preferred_element_type=jnp.float32
        )
        start = pl.multiple_of(source_ref[place] * seed_total, seed_total)
        for part in range(3):
            begin = capacity - split + part * seed_total
            units_ref[part, pl.ds(start, seed_total), :] = lower_ref[begin : begin + seed_total]
    out_ref[:double] = first
    for layer in range(2):
        second = lax.dot_general(units_ref[2], units_ref[layer], rows, preferred_element_type=jnp.float32)
        start = double + layer * round_up(classes, 8)
        out_ref[start : start + round_up(classes, 8)] = second[: round_up(classes, 8)]


def grad_layer(inputs, upper, lower, sources, seed_total, classes):
    capacity, double = inputs[0].shape
    hidden_width = upper[0].shape[1]
    vmem = pl.BlockSpec(memory_space=pltpu.VMEM)
    return pl.pallas_call(
        functools.partial(grad_kernel, seed_total, classes),
        in_specs=[pl.BlockSpec(memory_space=pltpu.SMEM)] + [vmem] * (3 * len(inputs)),
        out_specs=vmem,
        out_shape=jax.ShapeDtypeStruct((double + 2 * round_up(classes, 8), hidden_width), jnp.float32),
        scratch_shapes=[pltpu.VMEM((3, len(inputs) * seed_total, hidden_width), jnp.bfloat16)],
        compiler_params=pltpu.CompilerParams(vmem_limit_bytes=40 * 2**20),
        name="grad_layer",
    )(sources, *inputs, *upper, *lower)


def final_kernel(mine_ref, other_ref, first_ref, second_ref):
    width = first_ref.shape[1]
    classes = second_ref.shape[0]
    total = mine_ref[...].astype(jnp.float32) + other_ref[...].astype(jnp.float32)
    for layer in range(2):
        first_ref[layer] = total[layer * width : (layer + 1) * width]
        start = 2 * width + layer * round_up(classes, 8)
        second_ref[:, layer, :] = total[start : start + classes]


def final_sum(mine, other, width, classes):
    hidden_width = mine.shape[1]
    first, second = pl.pallas_call(
        final_kernel,
        out_shape=[
            jax.ShapeDtypeStruct((2, width, hidden_width), jnp.float32),
            jax.ShapeDtypeStruct((classes, 2, hidden_width), jnp.float32),
        ],
        name="final_sum",
    )(mine, other)
    return first, jnp.transpose(second, (1, 2, 0))


def ring_of(count):
    if count % 2:
        return list(range(count))
    return list(range(0, count, 2)) + list(range(count - 1, 0, -2))


def send_along(array, ring, shift):
    count = len(ring)
    return lax.ppermute(array, "feat", [(ring[i], ring[(i + shift) % count]) for i in range(count)])


def ring_gather(upper, lower, ring):
    count = len(ring)
    halves = [[half] + [None] * (count - 1) for half in (upper, lower)]
    moving = [[half, half] for half in (upper, lower)]
    for hop in range(1, count // 2 + 1):
        for half in range(2):
            for way, sign in enumerate((1, -1)):
                if 2 * hop < count or half == way:
                    moving[half][way] = send_along(moving[half][way], ring, sign)
                    halves[half][-sign * hop % count] = moving[half][way]
    return halves


def group_sum(grads, width, classes):
    count = lax.axis_size("dp")
    mine = grads
    stride = 1
    while 2 * stride < count:
        mine = mine + lax.ppermute(mine, "dp", [(i, i ^ stride) for i in range(count)])
        stride *= 2
    mine = mine.astype(jnp.bfloat16)
    if count > 1:
        other = lax.ppermute(mine, "dp", [(i, i ^ stride) for i in range(count)])
    else:
        other = jnp.zeros_like(mine)
    return final_sum(mine, other, width, classes)


def shards(
    node_feats,
    first_layer,
    second_layer,
    seed_ids,
    hop1_ids,
    hop1_count,
    hop2_ids,
    hop2_count,
    batch_sizes,
    label_ids,
):
    groups, seed_total = seed_ids.shape
    row_total = hop2_count.shape[1]
    fanout = hop1_ids.shape[1] // seed_total
    slice_width = node_feats.shape[0]
    hidden_width = first_layer.shape[2]
    classes = second_layer.shape[2]
    capacity = round_up(seed_total + row_total // 2, 16)
    kept = round_up(capacity, LANES)
    column_rank = lax.axis_index("feat")
    group_start = lax.axis_index("dp") * groups
    sizes = lax.dynamic_slice_in_dim(batch_sizes, group_start, groups)
    order, enough = plan_rows(hop1_count, hop2_count, sizes, kept)
    count = lax.axis_size("feat")
    ring = ring_of(count)
    places = sorted(range(count), key=lambda t: -min(t, count - t))
    turns = [
        [ring[(ring.index(i) + sign * t) % count] for sign in (1, -1) for t in places] for i in range(count)
    ]
    turn = lax.dynamic_index_in_dim(jnp.array(turns, jnp.int32), column_rank, 0, keepdims=False)
    weights = lax.all_gather(first_layer.reshape(2 * slice_width, hidden_width), "feat", axis=0)
    lists = [
        enough[:, None, :],
        order[:, None, :],
        jnp.maximum(order % 16, 1).astype(jnp.float32)[:, None, :],
        jnp.concatenate([seed_ids, hop1_ids], axis=1)[:, None, :],
        hop2_ids[:, None, :],
    ]
    node_feats, turn, *lists = lax.optimization_barrier((node_feats, turn, *lists))
    table = build_table(node_feats)
    inputs, received, arrived = [], [], []
    for call in range(CALLS):
        begin, end = -(-call * count // CALLS), -(-(call + 1) * count // CALLS)
        *blocks, table = gather_layer(table, turn, begin, end, *lists, slice_width, capacity)
        if call < CALLS - 1:
            table, blocks, arrived = lax.optimization_barrier((table, blocks, arrived))
        else:
            blocks, arrived, order, hop1_count, label_ids, sizes, second_layer = lax.optimization_barrier(
                (blocks, arrived, order, hop1_count, label_ids, sizes, second_layer)
            )
        inputs += blocks
        received += arrived
        arrived = [send_along(block, ring, t) if t else block for t, block in zip(places[begin:end], blocks)]
    received += arrived

    def own(array):
        return lax.dynamic_index_in_dim(array, column_rank, 0, keepdims=False)

    own_order = own(order)[None, :capacity]
    row = jnp.where(own_order % 16 > 0, own_order // 16, -1)
    seeds = jnp.stack([own(hop1_count), own(label_ids)])
    seeds = jnp.broadcast_to(seeds[:, :, None], (2, seed_total, LANES))
    size = lax.dynamic_slice_in_dim(sizes, column_rank, 1)
    layer = jnp.transpose(second_layer, (0, 2, 1))
    halves = upper_layers(received, size, turn, weights, layer, row, seeds, fanout)
    upper, lower = ring_gather(*halves, ring)
    grads = grad_layer(
        inputs, [upper[t] for t in places], [lower[t] for t in places], turn, seed_total, classes
    )
    return tuple(group_sum(grads, slice_width, classes))


def solution(mesh):
    return jax.shard_map(
        shards,
        mesh=mesh,
        in_specs=(
            P("feat", None),
            P(None, "feat", None),
            P(),
            P("dp", None),
            P("dp", None),
            P("dp", None),
            P("dp", None),
            P("dp", None),
            P(),
            P("dp", None),
        ),
        out_specs=(P(None, "feat", None), P()),
        check_vma=False,
    )
```

```python
import functools

import jax
import jax.numpy as jnp
from jax import lax
from jax.experimental import pallas as pl
from jax.experimental.pallas import tpu as pltpu
from jax.sharding import PartitionSpec as P

LANES = 128
TILE = 16
TILE_BITS = 4
CALLS = 3
BLOCK = 256


def round_up(value, step):
    return (value + step - 1) // step * step


def plan_rows(hop1_count, hop2_count, sizes, kept):
    groups, seed_total = hop1_count.shape
    row_total = hop2_count.shape[1]
    fanout = (row_total - seed_total) // seed_total
    live = jnp.arange(seed_total)[None, :] < sizes[:, None]
    near = jnp.arange(fanout)[None, None, :] < jnp.where(live, hop1_count, 0)[:, :, None]
    used = jnp.concatenate([live, near.reshape(groups, -1)], axis=1)
    count = jnp.where(used, hop2_count, 0)
    row = jnp.arange(row_total)[None, :]
    mixed = count * row_total + (row_total - 1 - row)
    place = jnp.sum((mixed[:, None, :] > mixed[:, :, None]).astype(jnp.int32), axis=2)
    packed = row * 16 + count
    order = jnp.sum(
        jnp.where(place[:, None, :] == jnp.arange(kept)[None, :, None], packed[:, None, :], 0), axis=2
    )
    enough = jnp.sum(
        (count[:, None, :] >= jnp.arange(16)[None, :, None]).astype(jnp.int32), axis=2
    )
    return order, enough


def table_kernel(*refs):
    *feats_refs, table_ref = refs
    step = pl.program_id(0)
    chunk = feats_refs[0].shape[1]
    width = sum(ref.shape[0] for ref in feats_refs)
    padded = table_ref.shape[1]
    down = lax.broadcasted_iota(jnp.int32, (BLOCK, BLOCK), 0)
    across = lax.broadcasted_iota(jnp.int32, (BLOCK, BLOCK), 1)
    identity = jnp.where(down == across, 1.0, 0.0).astype(jnp.bfloat16)
    filler = jnp.zeros((padded - width, BLOCK), jnp.bfloat16)
    for part in range(0, chunk // BLOCK, 2):
        pieces = []
        for at in (part * BLOCK, (part + 1) * BLOCK):
            pieces += [feats_ref[:, at : at + BLOCK] for feats_ref in feats_refs]
            if padded > width:
                pieces.append(filler)
        both = jnp.concatenate(pieces, axis=0)
        if part % 4:
            turned = jnp.transpose(both)
        else:
            turned = lax.dot_general(
                identity, both, (((1,), (1,)), ((), ())), preferred_element_type=jnp.float32
            ).astype(jnp.bfloat16)
        for side in range(2):
            start = pl.multiple_of(step * chunk + (part + side) * BLOCK, BLOCK)
            table_ref[pl.ds(start, BLOCK), :] = turned[:, side * padded : (side + 1) * padded]


def build_table(node_feats):
    width, nodes = node_feats.shape
    padded = max(width, LANES)
    chunk = min(nodes, 8192)
    streams = max(1, width // 32)
    return pl.pallas_call(
        table_kernel,
        grid=(nodes // chunk,),
        in_specs=[pl.BlockSpec((width // streams, chunk), lambda step, at=at: (at, step)) for at in range(streams)],
        out_specs=pl.BlockSpec(memory_space=pltpu.VMEM),
        out_shape=pltpu.VMEM((nodes, padded), jnp.bfloat16),
        compiler_params=pltpu.CompilerParams(vmem_limit_bytes=8 * 2**20),
        name="build_table",
    )(*[node_feats] * streams)


def gather_kernel(
    fanout, capacity, turn_ref, enough_ref, order_ref, own_ref, near_ref, count_ref, table_ref, *rest
):
    *inputs_refs, _, own_sum_ref, near_sum_ref = rest
    step = pl.program_id(0)
    width = inputs_refs[0].shape[1] // 2
    padded = table_ref.shape[1]

    tiles = table_ref.reshape(table_ref.shape[0] // TILE, TILE, padded)
    half = TILE // 2
    low = lax.broadcasted_iota(jnp.int32, (half, padded), 0)
    high = low + half

    def fetch(node, wanted=None):
        tile = tiles[node >> TILE_BITS].astype(jnp.float32)
        if wanted is None:
            line = jnp.full((half, padded), node, jnp.int32) & (TILE - 1)
        else:
            line = jnp.full((half, padded), jnp.where(wanted, node & (TILE - 1), TILE), jnp.int32)
        return jnp.where(line == low, tile[:half], jnp.where(line == high, tile[half:], 0.0))

    def add_lines(values):
        step = 1
        while step < half:
            chosen = (low & step) == 0
            values = [
                jnp.where(chosen, one, two) + pltpu.roll(jnp.where(chosen, two, one), half - step, 0)
                for one, two in zip(values[::2], values[1::2])
            ]
            step *= 2
        return values[0]

    def gather_rows(slots, exact, number, carry):
        first = pl.multiple_of(number * half, half)
        entries = [order_ref[0, 0, first + i] for i in range(half)]
        rows = [entry >> 4 for entry in entries]
        starts = [row * fanout for row in rows]

        def near(i, slot):
            node = near_ref[0, 0, starts[i] + slot]
            return fetch(node) if exact else fetch(node, slot < (entries[i] & 15))

        own_sum_ref[pl.ds(first, half), :] = add_lines([fetch(own_ref[0, 0, row]) for row in rows])
        nears = [near(i, 0) for i in range(half)]
        for slot in range(1, slots):
            nears = [nears[i] + near(i, slot) for i in range(half)]
        near_sum_ref[pl.ds(first, half), :] = add_lines(nears)
        return carry

    start = 0
    for slots in range(fanout, 0, -1):
        end = enough_ref[0, 0, slots]
        whole = jnp.maximum(lax.div(end, half), start)
        stop = lax.div(end + half - 1, half)
        lax.fori_loop(start, whole, functools.partial(gather_rows, slots, True), 0)
        lax.fori_loop(whole, stop, functools.partial(gather_rows, slots, False), 0)
        start = stop

    def clear(number, carry):
        first = pl.multiple_of(number * half, half)
        own_sum_ref[pl.ds(first, half), :] = jnp.zeros((half, padded), jnp.float32)
        near_sum_ref[pl.ds(first, half), :] = jnp.zeros((half, padded), jnp.float32)
        return carry

    lax.fori_loop(start, capacity // half, clear, 0)
    counts = jnp.transpose(jnp.broadcast_to(count_ref[0], (padded, count_ref.shape[2])))[:capacity]
    own = own_sum_ref[...].astype(jnp.bfloat16)[:, :width]
    near = (near_sum_ref[...] / counts).astype(jnp.bfloat16)[:, :width]
    both = jnp.concatenate([own, near], axis=1)
    for place, inputs_ref in enumerate(inputs_refs):

        @pl.when(step == place)
        def _():
            inputs_ref[...] = both


def gather_layer(table, turn, begin, end, enough, order, counts, own_ids, near_ids, width, capacity):
    nodes, padded = table.shape
    groups = end - begin
    kept = order.shape[2]
    row_total = own_ids.shape[2]
    fanout = near_ids.shape[2] // row_total

    def group_of(step, turn_ref):
        return (turn_ref[begin + step], 0, 0)

    def per_group(length):
        return pl.BlockSpec((1, 1, length), group_of, memory_space=pltpu.SMEM)

    return pl.pallas_call(
        functools.partial(gather_kernel, fanout, capacity),
        grid_spec=pltpu.PrefetchScalarGridSpec(
            num_scalar_prefetch=1,
            grid=(groups,),
            in_specs=[
                per_group(16),
                per_group(kept),
                per_group(row_total),
                per_group(row_total * fanout),
                pl.BlockSpec((1, 1, kept), group_of),
                pl.BlockSpec(memory_space=pltpu.VMEM),
            ],
            out_specs=[pl.BlockSpec((capacity, 2 * width), lambda step, turn_ref: (0, 0))] * groups
            + [pl.BlockSpec(memory_space=pltpu.VMEM)],
            scratch_shapes=[
                pltpu.VMEM((capacity, padded), jnp.float32),
                pltpu.VMEM((capacity, padded), jnp.float32),
            ],
        ),
        out_shape=[jax.ShapeDtypeStruct((capacity, 2 * width), jnp.bfloat16)] * groups
        + [pltpu.VMEM((nodes, padded), jnp.bfloat16)],
        input_output_aliases={6: groups},
        cost_estimate=pl.CostEstimate(
            flops=0, bytes_accessed=groups * capacity * fanout * TILE * padded * 2, transcendentals=0
        ),
        compiler_params=pltpu.CompilerParams(vmem_limit_bytes=14 * 2**20),
        name="gather_layer",
    )(
        turn, enough, order, own_ids, near_ids, counts,
        pltpu.with_memory_space_constraint(table, pltpu.VMEM),
    )


def upper_kernel(fanout, size_ref, turn_ref, weights_ref, layer_ref, row_ref, seed_ref, *rest):
    *inputs_refs, upper_ref, lower_ref = rest
    seed_total = seed_ref.shape[1]
    capacity = inputs_refs[0].shape[0]
    hidden_width = weights_ref.shape[2]
    classes = layer_ref.shape[1]
    size = size_ref[0]
    seed = lax.broadcasted_iota(jnp.int32, (seed_total, capacity), 0)
    row = jnp.broadcast_to(row_ref[...], (seed_total, capacity))
    first = seed_total + seed * fanout
    is_seed = jnp.where(row == seed, 1.0, 0.0).astype(jnp.bfloat16)
    is_near = jnp.where((row >= first) & (row < first + fanout), 1.0, 0.0).astype(jnp.bfloat16)
    preact = jnp.zeros((capacity, hidden_width), jnp.float32)
    for place, inputs_ref in enumerate(inputs_refs):
        source = turn_ref[len(inputs_refs) + place]
        preact = preact + jnp.dot(inputs_ref[...], weights_ref[source], preferred_element_type=jnp.float32)
    hidden = jnp.maximum(preact, 0.0).astype(jnp.bfloat16)
    counts = seed_ref[0][:, :1].astype(jnp.float32)
    last = (((1,), (1,)), ((), ()))
    seed_hidden = jnp.dot(is_seed, hidden, preferred_element_type=jnp.float32).astype(jnp.bfloat16)
    near_mean = (jnp.dot(is_near, hidden, preferred_element_type=jnp.float32) / counts).astype(jnp.bfloat16)
    logits = lax.dot_general(seed_hidden, layer_ref[0], last, preferred_element_type=jnp.float32)
    logits = logits + lax.dot_general(near_mean, layer_ref[1], last, preferred_element_type=jnp.float32)
    exponent = jnp.exp(logits - jnp.max(logits, axis=1, keepdims=True))
    probabilities = exponent / jnp.sum(exponent, axis=1, keepdims=True)
    label = jnp.broadcast_to(seed_ref[1][:, :1], (seed_total, classes))
    onehot = jnp.where(label == lax.broadcasted_iota(jnp.int32, (seed_total, classes), 1), 1.0, 0.0)
    valid = lax.broadcasted_iota(jnp.int32, (seed_total, classes), 0) < size
    dlogits = jnp.where(valid, (probabilities - onehot) / size.astype(jnp.float32), 0.0).astype(jnp.bfloat16)
    back_seed = jnp.dot(dlogits, layer_ref[0], preferred_element_type=jnp.float32)
    back_near = jnp.dot(dlogits, layer_ref[1], preferred_element_type=jnp.float32) / counts
    rows = (((0,), (0,)), ((), ()))
    spread = lax.dot_general(is_seed, back_seed.astype(jnp.bfloat16), rows, preferred_element_type=jnp.float32)
    spread = spread + lax.dot_general(
        is_near, back_near.astype(jnp.bfloat16), rows, preferred_element_type=jnp.float32
    )
    dpreact = jnp.where(preact > 0, spread, 0.0).astype(jnp.bfloat16)
    split = upper_ref.shape[0]
    upper_ref[...] = dpreact[:split]
    lower_ref[: capacity - split] = dpreact[split:]
    units = [seed_hidden, near_mean, jnp.zeros((seed_total, hidden_width), jnp.bfloat16)]
    for part, unit in enumerate(units):
        start = capacity - split + part * seed_total
        lower_ref[start : start + seed_total] = unit
    lower_ref[capacity - split + 2 * seed_total :, :classes] = dlogits


def upper_layers(inputs, size, turn, weights, layer, row, seeds, fanout):
    seed_total = seeds.shape[1]
    capacity = inputs[0].shape[0]
    hidden_width = weights.shape[2]
    total = capacity + 3 * seed_total
    split = round_up(total // 2, 16)
    smem = pl.BlockSpec(memory_space=pltpu.SMEM)
    vmem = pl.BlockSpec(memory_space=pltpu.VMEM)
    return pl.pallas_call(
        functools.partial(upper_kernel, fanout),
        in_specs=[smem] * 2 + [vmem] * (4 + len(inputs)),
        out_specs=[vmem] * 2,
        out_shape=[jax.ShapeDtypeStruct((length, hidden_width), jnp.bfloat16) for length in (split, total - split)],
        compiler_params=pltpu.CompilerParams(vmem_limit_bytes=32 * 2**20),
        name="upper_layers",
    )(size, turn, weights, layer, row, seeds, *inputs)


def grad_kernel(seed_total, classes, source_ref, *rest):
    count = (len(rest) - 3) // 3
    inputs_refs, upper_refs, lower_refs = rest[:count], rest[count : 2 * count], rest[2 * count : 3 * count]
    out_ref, dpreact_ref, units_ref = rest[3 * count :]
    capacity, double = inputs_refs[0].shape
    hidden_width = out_ref.shape[1]
    split = upper_refs[0].shape[0]
    rows = (((0,), (0,)), ((), ()))
    for place in range(count):
        source = source_ref[2 * count + place]
        upper_ref, lower_ref = upper_refs[place], lower_refs[place]
        dpreact_ref[source, :split] = upper_ref[...]
        dpreact_ref[source, split:] = lower_ref[: capacity - split]
        start = pl.multiple_of(source * seed_total, seed_total)
        for part in range(3):
            begin = capacity - split + part * seed_total
            units_ref[part, pl.ds(start, seed_total), :] = lower_ref[begin : begin + seed_total]
    first = jnp.zeros((double, hidden_width), jnp.float32)
    for place, inputs_ref in enumerate(inputs_refs):
        first = first + lax.dot_general(
            inputs_ref[...], dpreact_ref[source_ref[place]], rows, preferred_element_type=jnp.float32
        )
    out_ref[:double] = first
    for layer in range(2):
        second = lax.dot_general(units_ref[2], units_ref[layer], rows, preferred_element_type=jnp.float32)
        start = double + layer * round_up(classes, 8)
        out_ref[start : start + round_up(classes, 8)] = second[: round_up(classes, 8)]


def grad_layer(inputs, upper, lower, sources, seed_total, classes):
    capacity, double = inputs[0].shape
    hidden_width = upper[0].shape[1]
    vmem = pl.BlockSpec(memory_space=pltpu.VMEM)
    return pl.pallas_call(
        functools.partial(grad_kernel, seed_total, classes),
        in_specs=[pl.BlockSpec(memory_space=pltpu.SMEM)] + [vmem] * (3 * len(inputs)),
        out_specs=vmem,
        out_shape=jax.ShapeDtypeStruct((double + 2 * round_up(classes, 8), hidden_width), jnp.float32),
        scratch_shapes=[
            pltpu.VMEM((len(inputs), capacity, hidden_width), jnp.bfloat16),
            pltpu.VMEM((3, len(inputs) * seed_total, hidden_width), jnp.bfloat16),
        ],
        compiler_params=pltpu.CompilerParams(vmem_limit_bytes=40 * 2**20),
        name="grad_layer",
    )(sources, *inputs, *upper, *lower)


def final_kernel(mine_ref, other_ref, first_ref, second_ref):
    width = first_ref.shape[1]
    classes = second_ref.shape[0]
    total = mine_ref[...].astype(jnp.float32) + other_ref[...].astype(jnp.float32)
    for layer in range(2):
        first_ref[layer] = total[layer * width : (layer + 1) * width]
        start = 2 * width + layer * round_up(classes, 8)
        second_ref[:, layer, :] = total[start : start + classes]


def final_sum(mine, other, width, classes):
    hidden_width = mine.shape[1]
    first, second = pl.pallas_call(
        final_kernel,
        out_shape=[
            jax.ShapeDtypeStruct((2, width, hidden_width), jnp.float32),
            jax.ShapeDtypeStruct((classes, 2, hidden_width), jnp.float32),
        ],
        name="final_sum",
    )(mine, other)
    return first, jnp.transpose(second, (1, 2, 0))


def ring_of(count):
    if count % 2:
        return list(range(count))
    return list(range(0, count, 2)) + list(range(count - 1, 0, -2))


def send_along(array, ring, shift):
    count = len(ring)
    return lax.ppermute(array, "feat", [(ring[i], ring[(i + shift) % count]) for i in range(count)])


def partner(device, number, count):
    return device ^ number if count & (count - 1) == 0 else (device + number) % count


def sender(device, number, count):
    return next(i for i in range(count) if partner(i, number, count) == device)


def exchange(array, number, count):
    return lax.ppermute(array, "feat", [(i, partner(i, number, count)) for i in range(count)])


def ring_gather(upper, lower, ring):
    count = len(ring)
    halves = [[half] + [None] * (count - 1) for half in (upper, lower)]
    moving = [[half, half] for half in (upper, lower)]
    for hop in range(1, count // 2 + 1):
        for half in range(2):
            for way, sign in enumerate((1, -1)):
                if 2 * hop < count or half == way:
                    moving[half][way] = send_along(moving[half][way], ring, sign)
                    halves[half][-sign * hop % count] = moving[half][way]
    return halves


def group_sum(grads, width, classes):
    count = lax.axis_size("dp")
    mine = grads
    stride = 1
    while 2 * stride < count:
        mine = mine + lax.ppermute(mine, "dp", [(i, i ^ stride) for i in range(count)])
        stride *= 2
    mine = mine.astype(jnp.bfloat16)
    if count > 1:
        other = lax.ppermute(mine, "dp", [(i, i ^ stride) for i in range(count)])
    else:
        other = jnp.zeros_like(mine)
    return final_sum(mine, other, width, classes)


def shards(
    node_feats,
    first_layer,
    second_layer,
    seed_ids,
    hop1_ids,
    hop1_count,
    hop2_ids,
    hop2_count,
    batch_sizes,
    label_ids,
):
    groups, seed_total = seed_ids.shape
    row_total = hop2_count.shape[1]
    fanout = hop1_ids.shape[1] // seed_total
    slice_width = node_feats.shape[0]
    hidden_width = first_layer.shape[2]
    classes = second_layer.shape[2]
    capacity = round_up(seed_total + row_total // 2, 16)
    kept = round_up(capacity, LANES)
    column_rank = lax.axis_index("feat")
    group_start = lax.axis_index("dp") * groups
    sizes = lax.dynamic_slice_in_dim(batch_sizes, group_start, groups)
    order, enough = plan_rows(hop1_count, hop2_count, sizes, kept)
    count = lax.axis_size("feat")
    ring = ring_of(count)
    places = list(range(count))[::-1]
    if count & (count - 1) == 0:
        half = count // 2
        places = [t for t in places if t >= half][::-1] + [t for t in places if t < half]
    turns = [
        [partner(i, t, count) for t in places]
        + [sender(i, t, count) for t in places]
        + [ring[(ring.index(i) + t) % count] for t in range(count)]
        for i in range(count)
    ]
    turn = lax.dynamic_index_in_dim(jnp.array(turns, jnp.int32), column_rank, 0, keepdims=False)
    weights = lax.all_gather(first_layer.reshape(2 * slice_width, hidden_width), "feat", axis=0)
    lists = [
        enough[:, None, :],
        order[:, None, :],
        jnp.maximum(order % 16, 1).astype(jnp.float32)[:, None, :],
        jnp.concatenate([seed_ids, hop1_ids], axis=1)[:, None, :],
        hop2_ids[:, None, :],
    ]
    node_feats, turn, *lists = lax.optimization_barrier((node_feats, turn, *lists))
    table = build_table(node_feats)
    inputs, received, arrived = [], [], []
    for call in range(CALLS):
        begin, end = -(-call * count // CALLS), -(-(call + 1) * count // CALLS)
        *blocks, table = gather_layer(table, turn, begin, end, *lists, slice_width, capacity)
        if call < CALLS - 1:
            table, blocks, arrived = lax.optimization_barrier((table, blocks, arrived))
        else:
            blocks, arrived, order, hop1_count, label_ids, sizes, second_layer = lax.optimization_barrier(
                (blocks, arrived, order, hop1_count, label_ids, sizes, second_layer)
            )
        inputs += blocks
        received += arrived
        arrived = [exchange(block, t, count) if t else block for t, block in zip(places[begin:end], blocks)]
    received += arrived

    def own(array):
        return lax.dynamic_index_in_dim(array, column_rank, 0, keepdims=False)

    own_order = own(order)[None, :capacity]
    row = jnp.where(own_order % 16 > 0, own_order // 16, -1)
    seeds = jnp.stack([own(hop1_count), own(label_ids)])
    seeds = jnp.broadcast_to(seeds[:, :, None], (2, seed_total, LANES))
    size = lax.dynamic_slice_in_dim(sizes, column_rank, 1)
    layer = jnp.transpose(second_layer, (0, 2, 1))
    halves = upper_layers(received, size, turn, weights, layer, row, seeds, fanout)
    upper, lower = ring_gather(*halves, ring)
    grads = grad_layer(inputs, upper, lower, turn, seed_total, classes)
    return tuple(group_sum(grads, slice_width, classes))


def solution(mesh):
    return jax.shard_map(
        shards,
        mesh=mesh,
        in_specs=(
            P("feat", None),
            P(None, "feat", None),
            P(),
            P("dp", None),
            P("dp", None),
            P("dp", None),
            P("dp", None),
            P("dp", None),
            P(),
            P("dp", None),
        ),
        out_specs=(P(None, "feat", None), P()),
        check_vma=False,
    )
```

```python
import functools

import jax
import jax.numpy as jnp
from jax import lax
from jax.experimental import pallas as pl
from jax.experimental.pallas import tpu as pltpu
from jax.sharding import PartitionSpec as P

LANES = 128
TILE = 16
TILE_BITS = 4
CALLS = 3
BLOCK = 256


def round_up(value, step):
    return (value + step - 1) // step * step


def plan_rows(hop1_count, hop2_count, sizes, kept):
    groups, seed_total = hop1_count.shape
    row_total = hop2_count.shape[1]
    fanout = (row_total - seed_total) // seed_total
    live = jnp.arange(seed_total)[None, :] < sizes[:, None]
    near = jnp.arange(fanout)[None, None, :] < jnp.where(live, hop1_count, 0)[:, :, None]
    used = jnp.concatenate([live, near.reshape(groups, -1)], axis=1)
    count = jnp.where(used, hop2_count, 0)
    row = jnp.arange(row_total)[None, :]
    mixed = count * row_total + (row_total - 1 - row)
    place = jnp.sum((mixed[:, None, :] > mixed[:, :, None]).astype(jnp.int32), axis=2)
    packed = row * 16 + count
    order = jnp.sum(
        jnp.where(place[:, None, :] == jnp.arange(kept)[None, :, None], packed[:, None, :], 0), axis=2
    )
    enough = jnp.sum(
        (count[:, None, :] >= jnp.arange(16)[None, :, None]).astype(jnp.int32), axis=2
    )
    return order, enough


def table_kernel(*refs):
    *feats_refs, table_ref = refs
    step = pl.program_id(0)
    chunk = feats_refs[0].shape[1]
    width = sum(ref.shape[0] for ref in feats_refs)
    padded = table_ref.shape[1]
    down = lax.broadcasted_iota(jnp.int32, (BLOCK, BLOCK), 0)
    across = lax.broadcasted_iota(jnp.int32, (BLOCK, BLOCK), 1)
    identity = jnp.where(down == across, 1.0, 0.0).astype(jnp.bfloat16)
    filler = jnp.zeros((padded - width, BLOCK), jnp.bfloat16)
    for part in range(0, chunk // BLOCK, 2):
        pieces = []
        for at in (part * BLOCK, (part + 1) * BLOCK):
            pieces += [feats_ref[:, at : at + BLOCK] for feats_ref in feats_refs]
            if padded > width:
                pieces.append(filler)
        both = jnp.concatenate(pieces, axis=0)
        if part % 4:
            turned = jnp.transpose(both)
        else:
            turned = lax.dot_general(
                identity, both, (((1,), (1,)), ((), ())), preferred_element_type=jnp.float32
            ).astype(jnp.bfloat16)
        for side in range(2):
            start = pl.multiple_of(step * chunk + (part + side) * BLOCK, BLOCK)
            table_ref[pl.ds(start, BLOCK), :] = turned[:, side * padded : (side + 1) * padded]


def build_table(node_feats):
    width, nodes = node_feats.shape
    padded = max(width, LANES)
    chunk = min(nodes, 8192)
    streams = max(1, width // 32)
    return pl.pallas_call(
        table_kernel,
        grid=(nodes // chunk,),
        in_specs=[pl.BlockSpec((width // streams, chunk), lambda step, at=at: (at, step)) for at in range(streams)],
        out_specs=pl.BlockSpec(memory_space=pltpu.VMEM),
        out_shape=pltpu.VMEM((nodes, padded), jnp.bfloat16),
        compiler_params=pltpu.CompilerParams(vmem_limit_bytes=8 * 2**20),
        name="build_table",
    )(*[node_feats] * streams)


def gather_kernel(
    fanout, capacity, turn_ref, enough_ref, order_ref, own_ref, near_ref, count_ref, table_ref, *rest
):
    *inputs_refs, _, own_sum_ref, near_sum_ref = rest
    step = pl.program_id(0)
    width = inputs_refs[0].shape[1] // 2
    padded = table_ref.shape[1]

    tiles = table_ref.reshape(table_ref.shape[0] // TILE, TILE, padded)
    half = TILE // 2
    low = lax.broadcasted_iota(jnp.int32, (half, padded), 0)
    high = low + half

    def fetch(node, wanted=None):
        tile = tiles[node >> TILE_BITS].astype(jnp.float32)
        if wanted is None:
            line = jnp.full((half, padded), node, jnp.int32) & (TILE - 1)
        else:
            line = jnp.full((half, padded), jnp.where(wanted, node & (TILE - 1), TILE), jnp.int32)
        return jnp.where(line == low, tile[:half], jnp.where(line == high, tile[half:], 0.0))

    def add_lines(values):
        step = 1
        while step < half:
            chosen = (low & step) == 0
            values = [
                jnp.where(chosen, one, two) + pltpu.roll(jnp.where(chosen, two, one), half - step, 0)
                for one, two in zip(values[::2], values[1::2])
            ]
            step *= 2
        return values[0]

    def gather_rows(slots, exact, number, carry):
        first = pl.multiple_of(number * half, half)
        entries = [order_ref[0, 0, first + i] for i in range(half)]
        rows = [entry >> 4 for entry in entries]
        starts = [row * fanout for row in rows]

        def near(i, slot):
            node = near_ref[0, 0, starts[i] + slot]
            return fetch(node) if exact else fetch(node, slot < (entries[i] & 15))

        own_sum_ref[pl.ds(first, half), :] = add_lines([fetch(own_ref[0, 0, row]) for row in rows])
        nears = [near(i, 0) for i in range(half)]
        for slot in range(1, slots):
            nears = [nears[i] + near(i, slot) for i in range(half)]
        near_sum_ref[pl.ds(first, half), :] = add_lines(nears)
        return carry

    start = 0
    for slots in range(fanout, 0, -1):
        end = enough_ref[0, 0, slots]
        whole = jnp.maximum(lax.div(end, half), start)
        stop = lax.div(end + half - 1, half)
        lax.fori_loop(start, whole, functools.partial(gather_rows, slots, True), 0)
        lax.fori_loop(whole, stop, functools.partial(gather_rows, slots, False), 0)
        start = stop

    def clear(number, carry):
        first = pl.multiple_of(number * half, half)
        own_sum_ref[pl.ds(first, half), :] = jnp.zeros((half, padded), jnp.float32)
        near_sum_ref[pl.ds(first, half), :] = jnp.zeros((half, padded), jnp.float32)
        return carry

    lax.fori_loop(start, capacity // half, clear, 0)
    counts = jnp.transpose(jnp.broadcast_to(count_ref[0], (padded, count_ref.shape[2])))[:capacity]
    own = own_sum_ref[...].astype(jnp.bfloat16)[:, :width]
    near = (near_sum_ref[...] / counts).astype(jnp.bfloat16)[:, :width]
    both = jnp.concatenate([own, near], axis=1)
    for place, inputs_ref in enumerate(inputs_refs):

        @pl.when(step == place)
        def _():
            inputs_ref[...] = both


def gather_layer(table, turn, begin, end, enough, order, counts, own_ids, near_ids, width, capacity):
    nodes, padded = table.shape
    groups = end - begin
    kept = order.shape[2]
    row_total = own_ids.shape[2]
    fanout = near_ids.shape[2] // row_total

    def group_of(step, turn_ref):
        return (turn_ref[begin + step], 0, 0)

    def per_group(length):
        return pl.BlockSpec((1, 1, length), group_of, memory_space=pltpu.SMEM)

    return pl.pallas_call(
        functools.partial(gather_kernel, fanout, capacity),
        grid_spec=pltpu.PrefetchScalarGridSpec(
            num_scalar_prefetch=1,
            grid=(groups,),
            in_specs=[
                per_group(16),
                per_group(kept),
                per_group(row_total),
                per_group(row_total * fanout),
                pl.BlockSpec((1, 1, kept), group_of),
                pl.BlockSpec(memory_space=pltpu.VMEM),
            ],
            out_specs=[pl.BlockSpec((capacity, 2 * width), lambda step, turn_ref: (0, 0))] * groups
            + [pl.BlockSpec(memory_space=pltpu.VMEM)],
            scratch_shapes=[
                pltpu.VMEM((capacity, padded), jnp.float32),
                pltpu.VMEM((capacity, padded), jnp.float32),
            ],
        ),
        out_shape=[jax.ShapeDtypeStruct((capacity, 2 * width), jnp.bfloat16)] * groups
        + [pltpu.VMEM((nodes, padded), jnp.bfloat16)],
        input_output_aliases={6: groups},
        cost_estimate=pl.CostEstimate(
            flops=0, bytes_accessed=groups * capacity * fanout * TILE * padded * 2, transcendentals=0
        ),
        compiler_params=pltpu.CompilerParams(vmem_limit_bytes=14 * 2**20),
        name="gather_layer",
    )(
        turn, enough, order, own_ids, near_ids, counts,
        pltpu.with_memory_space_constraint(table, pltpu.VMEM),
    )


def upper_kernel(fanout, size_ref, turn_ref, weights_ref, layer_ref, row_ref, seed_ref, *rest):
    *inputs_refs, upper_ref, lower_ref = rest
    seed_total = seed_ref.shape[1]
    capacity = inputs_refs[0].shape[0]
    hidden_width = weights_ref.shape[2]
    classes = layer_ref.shape[1]
    size = size_ref[0]
    seed = lax.broadcasted_iota(jnp.int32, (seed_total, capacity), 0)
    row = jnp.broadcast_to(row_ref[...], (seed_total, capacity))
    first = seed_total + seed * fanout
    is_seed = jnp.where(row == seed, 1.0, 0.0).astype(jnp.bfloat16)
    is_near = jnp.where((row >= first) & (row < first + fanout), 1.0, 0.0).astype(jnp.bfloat16)
    preact = jnp.zeros((capacity, hidden_width), jnp.float32)
    for place, inputs_ref in enumerate(inputs_refs):
        source = turn_ref[len(inputs_refs) + place]
        preact = preact + jnp.dot(inputs_ref[...], weights_ref[source], preferred_element_type=jnp.float32)
    hidden = jnp.maximum(preact, 0.0).astype(jnp.bfloat16)
    counts = seed_ref[0][:, :1].astype(jnp.float32)
    last = (((1,), (1,)), ((), ()))
    seed_hidden = jnp.dot(is_seed, hidden, preferred_element_type=jnp.float32).astype(jnp.bfloat16)
    near_mean = (jnp.dot(is_near, hidden, preferred_element_type=jnp.float32) / counts).astype(jnp.bfloat16)
    logits = lax.dot_general(seed_hidden, layer_ref[0], last, preferred_element_type=jnp.float32)
    logits = logits + lax.dot_general(near_mean, layer_ref[1], last, preferred_element_type=jnp.float32)
    exponent = jnp.exp(logits - jnp.max(logits, axis=1, keepdims=True))
    probabilities = exponent / jnp.sum(exponent, axis=1, keepdims=True)
    label = jnp.broadcast_to(seed_ref[1][:, :1], (seed_total, classes))
    onehot = jnp.where(label == lax.broadcasted_iota(jnp.int32, (seed_total, classes), 1), 1.0, 0.0)
    valid = lax.broadcasted_iota(jnp.int32, (seed_total, classes), 0) < size
    dlogits = jnp.where(valid, (probabilities - onehot) / size.astype(jnp.float32), 0.0).astype(jnp.bfloat16)
    back_seed = jnp.dot(dlogits, layer_ref[0], preferred_element_type=jnp.float32)
    back_near = jnp.dot(dlogits, layer_ref[1], preferred_element_type=jnp.float32) / counts
    rows = (((0,), (0,)), ((), ()))
    spread = lax.dot_general(is_seed, back_seed.astype(jnp.bfloat16), rows, preferred_element_type=jnp.float32)
    spread = spread + lax.dot_general(
        is_near, back_near.astype(jnp.bfloat16), rows, preferred_element_type=jnp.float32
    )
    dpreact = jnp.where(preact > 0, spread, 0.0).astype(jnp.bfloat16)
    split = upper_ref.shape[0]
    upper_ref[...] = dpreact[:split]
    lower_ref[: capacity - split] = dpreact[split:]
    units = [seed_hidden, near_mean, jnp.zeros((seed_total, hidden_width), jnp.bfloat16)]
    for part, unit in enumerate(units):
        start = capacity - split + part * seed_total
        lower_ref[start : start + seed_total] = unit
    lower_ref[capacity - split + 2 * seed_total :, :classes] = dlogits


def upper_layers(inputs, size, turn, weights, layer, row, seeds, fanout):
    seed_total = seeds.shape[1]
    capacity = inputs[0].shape[0]
    hidden_width = weights.shape[2]
    total = capacity + 3 * seed_total
    split = round_up(total // 2, 16)
    smem = pl.BlockSpec(memory_space=pltpu.SMEM)
    vmem = pl.BlockSpec(memory_space=pltpu.VMEM)
    return pl.pallas_call(
        functools.partial(upper_kernel, fanout),
        in_specs=[smem] * 2 + [vmem] * (4 + len(inputs)),
        out_specs=[vmem] * 2,
        out_shape=[jax.ShapeDtypeStruct((length, hidden_width), jnp.bfloat16) for length in (split, total - split)],
        compiler_params=pltpu.CompilerParams(vmem_limit_bytes=32 * 2**20),
        name="upper_layers",
    )(size, turn, weights, layer, row, seeds, *inputs)


def grad_kernel(seed_total, classes, source_ref, *rest):
    count = (len(rest) - 3) // 3
    inputs_refs, upper_refs, lower_refs = rest[:count], rest[count : 2 * count], rest[2 * count : 3 * count]
    out_ref, dpreact_ref, units_ref = rest[3 * count :]
    capacity, double = inputs_refs[0].shape
    hidden_width = out_ref.shape[1]
    split = upper_refs[0].shape[0]
    rows = (((0,), (0,)), ((), ()))
    for place in range(count):
        source = source_ref[2 * count + place]
        upper_ref, lower_ref = upper_refs[place], lower_refs[place]
        dpreact_ref[source, :split] = upper_ref[...]
        dpreact_ref[source, split:] = lower_ref[: capacity - split]
        start = pl.multiple_of(source * seed_total, seed_total)
        for part in range(3):
            begin = capacity - split + part * seed_total
            units_ref[part, pl.ds(start, seed_total), :] = lower_ref[begin : begin + seed_total]
    first = jnp.zeros((double, hidden_width), jnp.float32)
    for place, inputs_ref in enumerate(inputs_refs):
        first = first + lax.dot_general(
            inputs_ref[...], dpreact_ref[source_ref[place]], rows, preferred_element_type=jnp.float32
        )
    out_ref[:double] = first
    for layer in range(2):
        second = lax.dot_general(units_ref[2], units_ref[layer], rows, preferred_element_type=jnp.float32)
        start = double + layer * round_up(classes, 8)
        out_ref[start : start + round_up(classes, 8)] = second[: round_up(classes, 8)]


def grad_layer(inputs, upper, lower, sources, seed_total, classes):
    capacity, double = inputs[0].shape
    hidden_width = upper[0].shape[1]
    vmem = pl.BlockSpec(memory_space=pltpu.VMEM)
    return pl.pallas_call(
        functools.partial(grad_kernel, seed_total, classes),
        in_specs=[pl.BlockSpec(memory_space=pltpu.SMEM)] + [vmem] * (3 * len(inputs)),
        out_specs=vmem,
        out_shape=jax.ShapeDtypeStruct((double + 2 * round_up(classes, 8), hidden_width), jnp.float32),
        scratch_shapes=[
            pltpu.VMEM((len(inputs), capacity, hidden_width), jnp.bfloat16),
            pltpu.VMEM((3, len(inputs) * seed_total, hidden_width), jnp.bfloat16),
        ],
        compiler_params=pltpu.CompilerParams(vmem_limit_bytes=40 * 2**20),
        name="grad_layer",
    )(sources, *inputs, *upper, *lower)


def final_kernel(mine_ref, other_ref, first_ref, second_ref):
    width = first_ref.shape[1]
    classes = second_ref.shape[0]
    total = mine_ref[...].astype(jnp.float32) + other_ref[...].astype(jnp.float32)
    for layer in range(2):
        first_ref[layer] = total[layer * width : (layer + 1) * width]
        start = 2 * width + layer * round_up(classes, 8)
        second_ref[:, layer, :] = total[start : start + classes]


def final_sum(mine, other, width, classes):
    hidden_width = mine.shape[1]
    first, second = pl.pallas_call(
        final_kernel,
        out_shape=[
            jax.ShapeDtypeStruct((2, width, hidden_width), jnp.float32),
            jax.ShapeDtypeStruct((classes, 2, hidden_width), jnp.float32),
        ],
        name="final_sum",
    )(mine, other)
    return first, jnp.transpose(second, (1, 2, 0))


def ring_of(count):
    if count % 2:
        return list(range(count))
    return list(range(0, count, 2)) + list(range(count - 1, 0, -2))


def send_along(array, ring, shift):
    count = len(ring)
    return lax.ppermute(array, "feat", [(ring[i], ring[(i + shift) % count]) for i in range(count)])


def partner(device, number, count):
    return device ^ number if count & (count - 1) == 0 else (device + number) % count


def sender(device, number, count):
    return next(i for i in range(count) if partner(i, number, count) == device)


def exchange(array, number, count):
    return lax.ppermute(array, "feat", [(i, partner(i, number, count)) for i in range(count)])


def ring_gather(upper, lower, ring):
    count = len(ring)
    halves = [[half] + [None] * (count - 1) for half in (upper, lower)]
    moving = [[half, half] for half in (upper, lower)]
    for hop in range(1, count // 2 + 1):
        for half in range(2):
            for way, sign in enumerate((1, -1)):
                if 2 * hop < count or half == way:
                    moving[half][way] = send_along(moving[half][way], ring, sign)
                    halves[half][-sign * hop % count] = moving[half][way]
    return halves


def group_sum(grads, width, classes):
    count = lax.axis_size("dp")
    mine = grads
    stride = 1
    while 2 * stride < count:
        mine = mine + lax.ppermute(mine, "dp", [(i, i ^ stride) for i in range(count)])
        stride *= 2
    mine = mine.astype(jnp.bfloat16)
    if count > 1:
        other = lax.ppermute(mine, "dp", [(i, i ^ stride) for i in range(count)])
    else:
        other = jnp.zeros_like(mine)
    return final_sum(mine, other, width, classes)


def shards(
    node_feats,
    first_layer,
    second_layer,
    seed_ids,
    hop1_ids,
    hop1_count,
    hop2_ids,
    hop2_count,
    batch_sizes,
    label_ids,
):
    groups, seed_total = seed_ids.shape
    row_total = hop2_count.shape[1]
    fanout = hop1_ids.shape[1] // seed_total
    slice_width = node_feats.shape[0]
    hidden_width = first_layer.shape[2]
    classes = second_layer.shape[2]
    capacity = round_up(seed_total + row_total // 2, 16)
    kept = round_up(capacity, LANES)
    column_rank = lax.axis_index("feat")
    group_start = lax.axis_index("dp") * groups
    sizes = lax.dynamic_slice_in_dim(batch_sizes, group_start, groups)
    order, enough = plan_rows(hop1_count, hop2_count, sizes, kept)
    count = lax.axis_size("feat")
    ring = ring_of(count)
    places = list(range(count))[::-1]
    if count > 2 and count & (count - 1) == 0:
        far, near = range(count // 2, count), range(count // 2 - 1, 1, -1)
        mixed = [((at + 0.5) / len(part), t) for part in (far, near) for at, t in enumerate(part)]
        places = [t for _, t in sorted(mixed)] + [1, 0]
    turns = [
        [partner(i, t, count) for t in places]
        + [sender(i, t, count) for t in places]
        + [ring[(ring.index(i) + t) % count] for t in range(count)]
        for i in range(count)
    ]
    turn = lax.dynamic_index_in_dim(jnp.array(turns, jnp.int32), column_rank, 0, keepdims=False)
    weights = lax.all_gather(first_layer.reshape(2 * slice_width, hidden_width), "feat", axis=0)
    lists = [
        enough[:, None, :],
        order[:, None, :],
        jnp.maximum(order % 16, 1).astype(jnp.float32)[:, None, :],
        jnp.concatenate([seed_ids, hop1_ids], axis=1)[:, None, :],
        hop2_ids[:, None, :],
    ]
    node_feats, turn, *lists = lax.optimization_barrier((node_feats, turn, *lists))
    table = build_table(node_feats)
    inputs, received, arrived = [], [], []
    for call in range(CALLS):
        begin, end = -(-call * count // CALLS), -(-(call + 1) * count // CALLS)
        *blocks, table = gather_layer(table, turn, begin, end, *lists, slice_width, capacity)
        if call < CALLS - 1:
            table, blocks, arrived = lax.optimization_barrier((table, blocks, arrived))
        else:
            blocks, arrived, order, hop1_count, label_ids, sizes, second_layer = lax.optimization_barrier(
                (blocks, arrived, order, hop1_count, label_ids, sizes, second_layer)
            )
        inputs += blocks
        received += arrived
        arrived = [exchange(block, t, count) if t else block for t, block in zip(places[begin:end], blocks)]
    received += arrived

    def own(array):
        return lax.dynamic_index_in_dim(array, column_rank, 0, keepdims=False)

    own_order = own(order)[None, :capacity]
    row = jnp.where(own_order % 16 > 0, own_order // 16, -1)
    seeds = jnp.stack([own(hop1_count), own(label_ids)])
    seeds = jnp.broadcast_to(seeds[:, :, None], (2, seed_total, LANES))
    size = lax.dynamic_slice_in_dim(sizes, column_rank, 1)
    layer = jnp.transpose(second_layer, (0, 2, 1))
    halves = upper_layers(received, size, turn, weights, layer, row, seeds, fanout)
    upper, lower = ring_gather(*halves, ring)
    grads = grad_layer(inputs, upper, lower, turn, seed_total, classes)
    return tuple(group_sum(grads, slice_width, classes))


def solution(mesh):
    return jax.shard_map(
        shards,
        mesh=mesh,
        in_specs=(
            P("feat", None),
            P(None, "feat", None),
            P(),
            P("dp", None),
            P("dp", None),
            P("dp", None),
            P("dp", None),
            P("dp", None),
            P(),
            P("dp", None),
        ),
        out_specs=(P(None, "feat", None), P()),
        check_vma=False,
    )
```

```python
import functools

import jax
import jax.numpy as jnp
from jax import lax
from jax.experimental import pallas as pl
from jax.experimental.pallas import tpu as pltpu
from jax.sharding import PartitionSpec as P

LANES = 128
TILE = 16
TILE_BITS = 4
CALLS = 3
BLOCK = 256


def round_up(value, step):
    return (value + step - 1) // step * step


def plan_rows(hop1_count, hop2_count, sizes, kept):
    groups, seed_total = hop1_count.shape
    row_total = hop2_count.shape[1]
    fanout = (row_total - seed_total) // seed_total
    live = jnp.arange(seed_total)[None, :] < sizes[:, None]
    near = jnp.arange(fanout)[None, None, :] < jnp.where(live, hop1_count, 0)[:, :, None]
    used = jnp.concatenate([live, near.reshape(groups, -1)], axis=1)
    count = jnp.where(used, hop2_count, 0)
    row = jnp.arange(row_total)[None, :]
    mixed = count * row_total + (row_total - 1 - row)
    place = jnp.sum((mixed[:, None, :] > mixed[:, :, None]).astype(jnp.int32), axis=2)
    packed = row * 16 + count
    order = jnp.sum(
        jnp.where(place[:, None, :] == jnp.arange(kept)[None, :, None], packed[:, None, :], 0), axis=2
    )
    enough = jnp.sum(
        (count[:, None, :] >= jnp.arange(16)[None, :, None]).astype(jnp.int32), axis=2
    )
    return order, enough


def table_kernel(*refs):
    *feats_refs, table_ref = refs
    step = pl.program_id(0)
    chunk = feats_refs[0].shape[1]
    width = sum(ref.shape[0] for ref in feats_refs)
    padded = table_ref.shape[1]
    down = lax.broadcasted_iota(jnp.int32, (BLOCK, BLOCK), 0)
    across = lax.broadcasted_iota(jnp.int32, (BLOCK, BLOCK), 1)
    identity = jnp.where(down == across, 1.0, 0.0).astype(jnp.bfloat16)
    filler = jnp.zeros((padded - width, BLOCK), jnp.bfloat16)
    for part in range(0, chunk // BLOCK, 2):
        pieces = []
        for at in (part * BLOCK, (part + 1) * BLOCK):
            pieces += [feats_ref[:, at : at + BLOCK] for feats_ref in feats_refs]
            if padded > width:
                pieces.append(filler)
        both = jnp.concatenate(pieces, axis=0)
        if part % 4:
            turned = jnp.transpose(both)
        else:
            turned = lax.dot_general(
                identity, both, (((1,), (1,)), ((), ())), preferred_element_type=jnp.float32
            ).astype(jnp.bfloat16)
        for side in range(2):
            start = pl.multiple_of(step * chunk + (part + side) * BLOCK, BLOCK)
            table_ref[pl.ds(start, BLOCK), :] = turned[:, side * padded : (side + 1) * padded]


def build_table(node_feats):
    width, nodes = node_feats.shape
    padded = max(width, LANES)
    chunk = min(nodes, 8192)
    streams = max(1, width // 32)
    return pl.pallas_call(
        table_kernel,
        grid=(nodes // chunk,),
        in_specs=[pl.BlockSpec((width // streams, chunk), lambda step, at=at: (at, step)) for at in range(streams)],
        out_specs=pl.BlockSpec(memory_space=pltpu.VMEM),
        out_shape=pltpu.VMEM((nodes, padded), jnp.bfloat16),
        compiler_params=pltpu.CompilerParams(vmem_limit_bytes=8 * 2**20),
        name="build_table",
    )(*[node_feats] * streams)


def gather_kernel(
    fanout, capacity, turn_ref, enough_ref, order_ref, own_ref, near_ref, count_ref, table_ref, *rest
):
    *inputs_refs, _, own_sum_ref, near_sum_ref = rest
    step = pl.program_id(0)
    width = inputs_refs[0].shape[1] // 2
    padded = table_ref.shape[1]

    tiles = table_ref.reshape(table_ref.shape[0] // TILE, TILE, padded)
    half = TILE // 2
    low = lax.broadcasted_iota(jnp.int32, (half, padded), 0)
    high = low + half

    def fetch(node, wanted=None):
        tile = tiles[node >> TILE_BITS].astype(jnp.float32)
        if wanted is None:
            line = jnp.full((half, padded), node, jnp.int32) & (TILE - 1)
        else:
            line = jnp.full((half, padded), jnp.where(wanted, node & (TILE - 1), TILE), jnp.int32)
        return jnp.where(line == low, tile[:half], jnp.where(line == high, tile[half:], 0.0))

    def add_lines(values):
        step = 1
        while step < half:
            chosen = (low & step) == 0
            values = [
                jnp.where(chosen, one, two) + pltpu.roll(jnp.where(chosen, two, one), half - step, 0)
                for one, two in zip(values[::2], values[1::2])
            ]
            step *= 2
        return values[0]

    def gather_rows(slots, exact, number, carry):
        first = pl.multiple_of(number * half, half)
        entries = [order_ref[0, 0, first + i] for i in range(half)]
        rows = [entry >> 4 for entry in entries]
        starts = [row * fanout for row in rows]

        def near(i, slot):
            node = near_ref[0, 0, starts[i] + slot]
            return fetch(node) if exact else fetch(node, slot < (entries[i] & 15))

        own_sum_ref[pl.ds(first, half), :] = add_lines([fetch(own_ref[0, 0, row]) for row in rows])
        nears = [near(i, 0) for i in range(half)]
        for slot in range(1, slots):
            nears = [nears[i] + near(i, slot) for i in range(half)]
        near_sum_ref[pl.ds(first, half), :] = add_lines(nears)
        return carry

    start = 0
    for slots in range(fanout, 0, -1):
        end = enough_ref[0, 0, slots]
        whole = jnp.maximum(lax.div(end, half), start)
        stop = lax.div(end + half - 1, half)
        lax.fori_loop(start, whole, functools.partial(gather_rows, slots, True), 0)
        lax.fori_loop(whole, stop, functools.partial(gather_rows, slots, False), 0)
        start = stop

    def clear(number, carry):
        first = pl.multiple_of(number * half, half)
        own_sum_ref[pl.ds(first, half), :] = jnp.zeros((half, padded), jnp.float32)
        near_sum_ref[pl.ds(first, half), :] = jnp.zeros((half, padded), jnp.float32)
        return carry

    lax.fori_loop(start, capacity // half, clear, 0)
    counts = jnp.transpose(jnp.broadcast_to(count_ref[0], (padded, count_ref.shape[2])))[:capacity]
    own = own_sum_ref[...].astype(jnp.bfloat16)[:, :width]
    near = (near_sum_ref[...] / counts).astype(jnp.bfloat16)[:, :width]
    both = jnp.concatenate([own, near], axis=1)
    for place, inputs_ref in enumerate(inputs_refs):

        @pl.when(step == place)
        def _():
            inputs_ref[...] = both


def gather_layer(table, turn, begin, end, enough, order, counts, own_ids, near_ids, width, capacity):
    nodes, padded = table.shape
    groups = end - begin
    kept = order.shape[2]
    row_total = own_ids.shape[2]
    fanout = near_ids.shape[2] // row_total

    def group_of(step, turn_ref):
        return (turn_ref[begin + step], 0, 0)

    def per_group(length):
        return pl.BlockSpec((1, 1, length), group_of, memory_space=pltpu.SMEM)

    return pl.pallas_call(
        functools.partial(gather_kernel, fanout, capacity),
        grid_spec=pltpu.PrefetchScalarGridSpec(
            num_scalar_prefetch=1,
            grid=(groups,),
            in_specs=[
                per_group(16),
                per_group(kept),
                per_group(row_total),
                per_group(row_total * fanout),
                pl.BlockSpec((1, 1, kept), group_of),
                pl.BlockSpec(memory_space=pltpu.VMEM),
            ],
            out_specs=[pl.BlockSpec((capacity, 2 * width), lambda step, turn_ref: (0, 0))] * groups
            + [pl.BlockSpec(memory_space=pltpu.VMEM)],
            scratch_shapes=[
                pltpu.VMEM((capacity, padded), jnp.float32),
                pltpu.VMEM((capacity, padded), jnp.float32),
            ],
        ),
        out_shape=[jax.ShapeDtypeStruct((capacity, 2 * width), jnp.bfloat16)] * groups
        + [pltpu.VMEM((nodes, padded), jnp.bfloat16)],
        input_output_aliases={6: groups},
        cost_estimate=pl.CostEstimate(
            flops=0, bytes_accessed=groups * capacity * fanout * TILE * padded * 2, transcendentals=0
        ),
        compiler_params=pltpu.CompilerParams(vmem_limit_bytes=14 * 2**20),
        name="gather_layer",
    )(
        turn, enough, order, own_ids, near_ids, counts,
        pltpu.with_memory_space_constraint(table, pltpu.VMEM),
    )


def upper_kernel(fanout, size_ref, turn_ref, weights_ref, layer_ref, row_ref, seed_ref, *rest):
    *inputs_refs, upper_ref, lower_ref = rest
    seed_total = seed_ref.shape[1]
    capacity = inputs_refs[0].shape[0]
    hidden_width = weights_ref.shape[2]
    classes = layer_ref.shape[1]
    size = size_ref[0]
    seed = lax.broadcasted_iota(jnp.int32, (seed_total, capacity), 0)
    row = jnp.broadcast_to(row_ref[...], (seed_total, capacity))
    first = seed_total + seed * fanout
    is_seed = jnp.where(row == seed, 1.0, 0.0).astype(jnp.bfloat16)
    is_near = jnp.where((row >= first) & (row < first + fanout), 1.0, 0.0).astype(jnp.bfloat16)
    preact = jnp.zeros((capacity, hidden_width), jnp.float32)
    for place, inputs_ref in enumerate(inputs_refs):
        source = turn_ref[len(inputs_refs) + place]
        preact = preact + jnp.dot(inputs_ref[...], weights_ref[source], preferred_element_type=jnp.float32)
    hidden = jnp.maximum(preact, 0.0).astype(jnp.bfloat16)
    counts = seed_ref[0][:, :1].astype(jnp.float32)
    last = (((1,), (1,)), ((), ()))
    seed_hidden = jnp.dot(is_seed, hidden, preferred_element_type=jnp.float32).astype(jnp.bfloat16)
    near_mean = (jnp.dot(is_near, hidden, preferred_element_type=jnp.float32) / counts).astype(jnp.bfloat16)
    logits = lax.dot_general(seed_hidden, layer_ref[0], last, preferred_element_type=jnp.float32)
    logits = logits + lax.dot_general(near_mean, layer_ref[1], last, preferred_element_type=jnp.float32)
    exponent = jnp.exp(logits - jnp.max(logits, axis=1, keepdims=True))
    probabilities = exponent / jnp.sum(exponent, axis=1, keepdims=True)
    label = jnp.broadcast_to(seed_ref[1][:, :1], (seed_total, classes))
    onehot = jnp.where(label == lax.broadcasted_iota(jnp.int32, (seed_total, classes), 1), 1.0, 0.0)
    valid = lax.broadcasted_iota(jnp.int32, (seed_total, classes), 0) < size
    dlogits = jnp.where(valid, (probabilities - onehot) / size.astype(jnp.float32), 0.0).astype(jnp.bfloat16)
    back_seed = jnp.dot(dlogits, layer_ref[0], preferred_element_type=jnp.float32)
    back_near = jnp.dot(dlogits, layer_ref[1], preferred_element_type=jnp.float32) / counts
    rows = (((0,), (0,)), ((), ()))
    spread = lax.dot_general(is_seed, back_seed.astype(jnp.bfloat16), rows, preferred_element_type=jnp.float32)
    spread = spread + lax.dot_general(
        is_near, back_near.astype(jnp.bfloat16), rows, preferred_element_type=jnp.float32
    )
    dpreact = jnp.where(preact > 0, spread, 0.0).astype(jnp.bfloat16)
    split = upper_ref.shape[0]
    upper_ref[...] = dpreact[:split]
    lower_ref[: capacity - split] = dpreact[split:]
    units = [seed_hidden, near_mean, jnp.zeros((seed_total, hidden_width), jnp.bfloat16)]
    for part, unit in enumerate(units):
        start = capacity - split + part * seed_total
        lower_ref[start : start + seed_total] = unit
    lower_ref[capacity - split + 2 * seed_total :, :classes] = dlogits


def upper_layers(inputs, size, turn, weights, layer, row, seeds, fanout):
    seed_total = seeds.shape[1]
    capacity = inputs[0].shape[0]
    hidden_width = weights.shape[2]
    total = capacity + 3 * seed_total
    split = round_up(total // 2, 16)
    smem = pl.BlockSpec(memory_space=pltpu.SMEM)
    vmem = pl.BlockSpec(memory_space=pltpu.VMEM)
    return pl.pallas_call(
        functools.partial(upper_kernel, fanout),
        in_specs=[smem] * 2 + [vmem] * (4 + len(inputs)),
        out_specs=[vmem] * 2,
        out_shape=[jax.ShapeDtypeStruct((length, hidden_width), jnp.bfloat16) for length in (split, total - split)],
        compiler_params=pltpu.CompilerParams(vmem_limit_bytes=32 * 2**20),
        name="upper_layers",
    )(size, turn, weights, layer, row, seeds, *inputs)


def grad_kernel(seed_total, classes, source_ref, *rest):
    count = (len(rest) - 3) // 3
    inputs_refs, upper_refs, lower_refs = rest[:count], rest[count : 2 * count], rest[2 * count : 3 * count]
    out_ref, dpreact_ref, units_ref = rest[3 * count :]
    capacity, double = inputs_refs[0].shape
    hidden_width = out_ref.shape[1]
    split = upper_refs[0].shape[0]
    rows = (((0,), (0,)), ((), ()))
    for place in range(count):
        source = source_ref[2 * count + place]
        upper_ref, lower_ref = upper_refs[place], lower_refs[place]
        dpreact_ref[source, :split] = upper_ref[...]
        dpreact_ref[source, split:] = lower_ref[: capacity - split]
        start = pl.multiple_of(source * seed_total, seed_total)
        for part in range(3):
            begin = capacity - split + part * seed_total
            units_ref[part, pl.ds(start, seed_total), :] = lower_ref[begin : begin + seed_total]
    first = jnp.zeros((double, hidden_width), jnp.float32)
    for place, inputs_ref in enumerate(inputs_refs):
        first = first + lax.dot_general(
            inputs_ref[...], dpreact_ref[source_ref[place]], rows, preferred_element_type=jnp.float32
        )
    out_ref[:double] = first
    for layer in range(2):
        second = lax.dot_general(units_ref[2], units_ref[layer], rows, preferred_element_type=jnp.float32)
        start = double + layer * round_up(classes, 8)
        out_ref[start : start + round_up(classes, 8)] = second[: round_up(classes, 8)]


def grad_layer(inputs, upper, lower, sources, seed_total, classes):
    capacity, double = inputs[0].shape
    hidden_width = upper[0].shape[1]
    vmem = pl.BlockSpec(memory_space=pltpu.VMEM)
    return pl.pallas_call(
        functools.partial(grad_kernel, seed_total, classes),
        in_specs=[pl.BlockSpec(memory_space=pltpu.SMEM)] + [vmem] * (3 * len(inputs)),
        out_specs=vmem,
        out_shape=jax.ShapeDtypeStruct((double + 2 * round_up(classes, 8), hidden_width), jnp.float32),
        scratch_shapes=[
            pltpu.VMEM((len(inputs), capacity, hidden_width), jnp.bfloat16),
            pltpu.VMEM((3, len(inputs) * seed_total, hidden_width), jnp.bfloat16),
        ],
        compiler_params=pltpu.CompilerParams(vmem_limit_bytes=40 * 2**20),
        name="grad_layer",
    )(sources, *inputs, *upper, *lower)


def final_kernel(mine_ref, other_ref, first_ref, second_ref):
    width = first_ref.shape[1]
    classes = second_ref.shape[0]
    total = mine_ref[...].astype(jnp.float32) + other_ref[...].astype(jnp.float32)
    for layer in range(2):
        first_ref[layer] = total[layer * width : (layer + 1) * width]
        start = 2 * width + layer * round_up(classes, 8)
        second_ref[:, layer, :] = total[start : start + classes]


def final_sum(mine, other, width, classes):
    hidden_width = mine.shape[1]
    first, second = pl.pallas_call(
        final_kernel,
        out_shape=[
            jax.ShapeDtypeStruct((2, width, hidden_width), jnp.float32),
            jax.ShapeDtypeStruct((classes, 2, hidden_width), jnp.float32),
        ],
        name="final_sum",
    )(mine, other)
    return first, jnp.transpose(second, (1, 2, 0))


def ring_of(count):
    if count % 2:
        return list(range(count))
    return list(range(0, count, 2)) + list(range(count - 1, 0, -2))


def send_along(array, ring, shift):
    count = len(ring)
    return lax.ppermute(array, "feat", [(ring[i], ring[(i + shift) % count]) for i in range(count)])


def partner(device, number, count):
    return device ^ number if count & (count - 1) == 0 else (device + number) % count


def sender(device, number, count):
    return next(i for i in range(count) if partner(i, number, count) == device)


def exchange(array, number, count):
    return lax.ppermute(array, "feat", [(i, partner(i, number, count)) for i in range(count)])


def ring_gather(upper, lower, ring):
    count = len(ring)
    halves = [[half] + [None] * (count - 1) for half in (upper, lower)]
    moving = [[half, half] for half in (upper, lower)]
    for hop in range(1, count // 2 + 1):
        for half in range(2):
            for way, sign in enumerate((1, -1)):
                if 2 * hop < count or half == way:
                    moving[half][way] = send_along(moving[half][way], ring, sign)
                    halves[half][-sign * hop % count] = moving[half][way]
    return halves


def group_sum(grads, width, classes):
    count = lax.axis_size("dp")
    mine = grads
    stride = 1
    while 2 * stride < count:
        mine = mine + lax.ppermute(mine, "dp", [(i, i ^ stride) for i in range(count)])
        stride *= 2
    mine = mine.astype(jnp.bfloat16)
    if count > 1:
        other = lax.ppermute(mine, "dp", [(i, i ^ stride) for i in range(count)])
    else:
        other = jnp.zeros_like(mine)
    return final_sum(mine, other, width, classes)


def shards(
    node_feats,
    first_layer,
    second_layer,
    seed_ids,
    hop1_ids,
    hop1_count,
    hop2_ids,
    hop2_count,
    batch_sizes,
    label_ids,
):
    groups, seed_total = seed_ids.shape
    row_total = hop2_count.shape[1]
    fanout = hop1_ids.shape[1] // seed_total
    slice_width = node_feats.shape[0]
    hidden_width = first_layer.shape[2]
    classes = second_layer.shape[2]
    capacity = round_up(seed_total + row_total // 2, 16)
    kept = round_up(capacity, LANES)
    column_rank = lax.axis_index("feat")
    group_start = lax.axis_index("dp") * groups
    sizes = lax.dynamic_slice_in_dim(batch_sizes, group_start, groups)
    order, enough = plan_rows(hop1_count, hop2_count, sizes, kept)
    count = lax.axis_size("feat")
    ring = ring_of(count)
    places = list(range(count))[::-1]
    if count > 2 and count & (count - 1) == 0:
        far, near = range(count // 2, count), range(count // 2 - 1, 1, -1)
        mixed = [((at + 0.5) / len(part), t) for part in (far, near) for at, t in enumerate(part)]
        places = [t for _, t in sorted(mixed)] + [1, 0]
    turns = [
        [partner(i, t, count) for t in places]
        + [sender(i, t, count) for t in places]
        + [ring[(ring.index(i) + t) % count] for t in range(count)]
        for i in range(count)
    ]
    turn = lax.dynamic_index_in_dim(jnp.array(turns, jnp.int32), column_rank, 0, keepdims=False)
    weights = lax.all_gather(first_layer.reshape(2 * slice_width, hidden_width), "feat", axis=0)
    lists = [
        enough[:, None, :],
        order[:, None, :],
        jnp.maximum(order % 16, 1).astype(jnp.float32)[:, None, :],
        jnp.concatenate([seed_ids, hop1_ids], axis=1)[:, None, :],
        hop2_ids[:, None, :],
    ]
    node_feats, turn, *lists = lax.optimization_barrier((node_feats, turn, *lists))
    table = build_table(node_feats)
    inputs, received, arrived = [], [], []
    for call in range(CALLS):
        begin, end = -(-call * count // CALLS), -(-(call + 1) * count // CALLS)
        *blocks, table = gather_layer(table, turn, begin, end, *lists, slice_width, capacity)
        if call < CALLS - 1:
            table, blocks, arrived = lax.optimization_barrier((table, blocks, arrived))
        else:
            blocks, arrived, order, hop1_count, label_ids, sizes, second_layer, weights = (
                lax.optimization_barrier(
                    (blocks, arrived, order, hop1_count, label_ids, sizes, second_layer, weights)
                )
            )
            weights = jnp.where(turn[0] >= 0, weights, jnp.zeros_like(weights))
        inputs += blocks
        received += arrived
        arrived = [exchange(block, t, count) if t else block for t, block in zip(places[begin:end], blocks)]
    received += arrived

    def own(array):
        return lax.dynamic_index_in_dim(array, column_rank, 0, keepdims=False)

    own_order = own(order)[None, :capacity]
    row = jnp.where(own_order % 16 > 0, own_order // 16, -1)
    seeds = jnp.stack([own(hop1_count), own(label_ids)])
    seeds = jnp.broadcast_to(seeds[:, :, None], (2, seed_total, LANES))
    size = lax.dynamic_slice_in_dim(sizes, column_rank, 1)
    layer = jnp.transpose(second_layer, (0, 2, 1))
    halves = upper_layers(received, size, turn, weights, layer, row, seeds, fanout)
    upper, lower = ring_gather(*halves, ring)
    grads = grad_layer(inputs, upper, lower, turn, seed_total, classes)
    return tuple(group_sum(grads, slice_width, classes))


def solution(mesh):
    return jax.shard_map(
        shards,
        mesh=mesh,
        in_specs=(
            P("feat", None),
            P(None, "feat", None),
            P(),
            P("dp", None),
            P("dp", None),
            P("dp", None),
            P("dp", None),
            P("dp", None),
            P(),
            P("dp", None),
        ),
        out_specs=(P(None, "feat", None), P()),
        check_vma=False,
    )
```
